128 devices in a mesh: gx: 8 (over y, core), gy: 16 (over x, z).
Axes of the slice: x: 4, y: 4, z: 4, core: 2. Of those that a mesh axis runs over, the one named last changes fastest.
Arguments:
- eps_field: bfloat16 [48, 512, 2048], P(None, 'gx', 'gy'), may hold values from 1 to 10
- charge: float32 [48, 512, 2048], P(None, 'gx', 'gy'), may hold values from -6 to 6
- potential_start: float32 [48, 512, 2048], P(None, 'gx', 'gy'), may hold values from -3 to 3
- colloid_vel: float32 [3, 4096], P(None, ('gx', 'gy')), may hold values from -0.3 to 0.3
- colloid_spin: float32 [3, 4096], P(None, ('gx', 'gy')), may hold values from -0.06 to 0.06
- link_dir: int32 [8, 16, 32768], P('gx', 'gy'), may hold values from 0 to 17
- link_colloid: int32 [8, 16, 32768], P('gx', 'gy'), may hold values from -1 to 4095, as said below
- link_site: int32 [8, 16, 32768], P('gx', 'gy'), may hold values from 0 to 8191
- link_depth: int32 [8, 16, 32768], P('gx', 'gy'), may hold values from 0 to 47
- link_pop: float32 [8, 16, 32768], P('gx', 'gy'), may hold values from -0.1 to 0.1
- link_rb: float32 [3, 8, 16, 32768], P(None, 'gx', 'gy'), may hold values from -9 to 9
Outputs:
- potential: float32 [48, 512, 2048], P(None, 'gx', 'gy')
- force_torque: float32 [6, 4096], P(None, ('gx', 'gy'))
- link_out: float32 [8, 16, 32768], P('gx', 'gy')
The draws below stay inside these ranges and needn't reach their ends.
Inputs may be any that keep to these rules, and one draw needn't show every extreme that they name: `link_colloid`: an empty slot holds -1 and the live slots of a tile come first; at least 16384 slots of every tile are live and every slot of at least one tile. The tile with index i along gx and j along gy owns the colloids (i n + j) * 32 up to (i n + j + 1) * 32 - 1, where n is the number of tiles along gy; a live slot names a colloid owned by its own tile or by one of the eight tiles beside it, wrapping around.
All inputs are finite; a program needn't handle non-finite values.
Results may differ from the reference program's by a relative error of at most 0.0003.
Values may be sent and summed in bfloat16 or wider, within the bound.
A program may use at most 128 MiB of HBM per device.

```python
import math
import jax
import jax.numpy as jnp
import numpy as np
from jax import lax

NZ = 48
TX = 64
TY = 128
NC_DEV = 32
LINKS = 32768
SWEEPS = 6
RADIUS = 8
TILES_X = 8
TILES_Y = 16
NX = 512
NY = 2048
NC = 4096


def draw_link_colloid(key, part):
    base = jax.random.fold_in(key, 4711)
    key_live, key_full, key_stepx, key_stepy, key_slot = jax.random.split(base, 5)
    tile_count = TILES_X * TILES_Y
    live_count = jax.random.randint(key_live, (tile_count,), LINKS // 2, LINKS + 1)
    full_tile = jax.random.randint(key_full, (), 0, tile_count)
    tile_index = jnp.arange(tile_count, dtype=jnp.int32)
    live_count = jnp.where(tile_index == full_tile, LINKS, live_count)
    step_x = jax.random.randint(key_stepx, (tile_count, LINKS), -1, 2)
    step_y = jax.random.randint(key_stepy, (tile_count, LINKS), -1, 2)
    slot_index = jax.random.randint(key_slot, (tile_count, LINKS), 0, NC_DEV)
    home_x = (tile_index // TILES_Y)[:, None]
    home_y = (tile_index % TILES_Y)[:, None]
    owner = (home_x + step_x) % TILES_X * TILES_Y + (home_y + step_y) % TILES_Y
    colloid_ids = owner * NC_DEV + slot_index
    position = jnp.arange(LINKS, dtype=jnp.int32)[None, :]
    colloid_ids = jnp.where(position < live_count[:, None], colloid_ids, -1)
    return colloid_ids.reshape(TILES_X, TILES_Y, LINKS).astype(jnp.int32)


def with_ends(drawn, own_key, smallest, top_value):
    spot = [jax.random.randint(jax.random.fold_in(own_key, axis), (), 0, length) for axis, length in enumerate(drawn.shape)]
    widest = drawn.shape.index(max(drawn.shape))
    neighbour = spot[:widest] + [(spot[widest] + 1) % drawn.shape[widest]] + spot[widest + 1:]
    return drawn.at[tuple(spot)].set(smallest).at[tuple(neighbour)].set(top_value)


def level_of(rng, shape, pieces, low, top_value):
    def one(dim, blocks):
        heights = jax.random.uniform(jax.random.fold_in(jax.random.fold_in(rng, 6), dim), (blocks,), jnp.float32, low / len(pieces), top_value / len(pieces))
        return jnp.repeat(jnp.exp(heights), shape[dim] // blocks).reshape((-1,) + (1,) * (len(shape) - dim - 1))

    level = one(*pieces[0])
    for cut in pieces[1:]:
        level = level * one(*cut)
    return level


def normal_values(key, extent, width, reach, pieces=(), kind=jnp.bfloat16):
    level = level_of(key, extent, pieces, -0.22, 0.18) if pieces else 1.0
    result = jax.random.normal(key, extent, jnp.float32) * width * level
    return jnp.minimum(jnp.maximum(result, -reach), reach).astype(kind)


def setup_inputs(seed: int = 0) -> dict:
    arg_keys = jax.random.split(jax.random.key(seed), 12)
    return {
        "eps_field": jnp.clip(jnp.exp(math.log(10.0) - 2.3025851 * jax.random.uniform(arg_keys[0], (NZ, NX, NY), jnp.float32) ** level_of(arg_keys[0], (NZ, NX, NY), ((1, 8), (2, 16)), -0.2, 0.2)), 1.0, 10.0).astype(jnp.bfloat16),
        "charge": normal_values(arg_keys[1], (NZ, NX, NY), 1.0, 6.0, ((1, 8), (2, 16)), jnp.float32),
        "potential_start": normal_values(arg_keys[2], (NZ, NX, NY), 0.5, 3.0, ((1, 8), (2, 16)), jnp.float32),
        "colloid_vel": normal_values(arg_keys[3], (3, NC), 0.05, 0.3, ((1, 128),), jnp.float32),
        "colloid_spin": normal_values(arg_keys[4], (3, NC), 0.01, 0.06, ((1, 128),), jnp.float32),
        "link_dir": with_ends(jax.random.randint(arg_keys[5], (TILES_X, TILES_Y, LINKS), 0, 18), jax.random.fold_in(arg_keys[5], 1), 0, 17).astype(jnp.int32),
        "link_colloid": draw_link_colloid(jax.random.fold_in(arg_keys[11], 71), 0),
        "link_site": with_ends(jax.random.randint(arg_keys[7], (TILES_X, TILES_Y, LINKS), 0, TX * TY), jax.random.fold_in(arg_keys[7], 1), 0, (TX * TY) - 1).astype(jnp.int32),
        "link_depth": with_ends(jax.random.randint(arg_keys[8], (TILES_X, TILES_Y, LINKS), 0, NZ), jax.random.fold_in(arg_keys[8], 1), 0, NZ - 1).astype(jnp.int32),
        "link_pop": normal_values(arg_keys[9], (TILES_X, TILES_Y, LINKS), 0.015625, 0.1, ((0, 8), (1, 16)), jnp.float32),
        "link_rb": jnp.clip(jax.random.uniform(arg_keys[10], (3, TILES_X, TILES_Y, LINKS), jnp.float32, -9.0, 9.0) * level_of(arg_keys[10], (3, TILES_X, TILES_Y, LINKS), ((1, 8), (2, 16)), -0.4, 0.0), -9.0, 9.0),
    }


velocity_table = np.array([[1, 0, 0], [-1, 0, 0], [0, 1, 0], [0, -1, 0], [0, 0, 1], [0, 0, -1], [1, 1, 0], [1, -1, 0], [-1, 1, 0], [-1, -1, 0], [1, 0, 1], [1, 0, -1], [-1, 0, 1], [-1, 0, -1], [0, 1, 1], [0, 1, -1], [0, -1, 1], [0, -1, -1]], dtype=np.float32).T
weight_table = np.array([1.0 / 18.0] * 6 + [1.0 / 36.0] * 12, dtype=np.float32)
OVER_RELAX = 1.6


def lattice_lookup(directions):
    onehot = (directions[None, :] == jnp.arange(18, dtype=jnp.int32)[:, None]).astype(jnp.float32)
    velocity = jnp.dot(jnp.asarray(velocity_table).astype(jnp.float32), onehot, precision=lax.Precision.HIGHEST)
    weight = jnp.dot(jnp.asarray(weight_table).astype(jnp.float32)[None, :], onehot, precision=lax.Precision.HIGHEST)[0]
    return velocity, weight


def cross_product(first, second):
    return jnp.stack([first[1] * second[2] - first[2] * second[1], first[2] * second[0] - first[0] * second[2], first[0] * second[1] - first[1] * second[0]])


def link_terms(pops, velocity, weight, valid, offsets, at_links, pressure):
    boundary = at_links[0:3] + cross_product(at_links[3:6], offsets)
    along = jnp.sum(velocity * boundary, axis=0)
    transfer = (2.0 * pops - 6.0 * weight * along + weight * pressure) * valid
    force = velocity * transfer[None, :]
    torque = cross_product(offsets, force)
    return jnp.concatenate([force, torque], axis=0)


def reflected(pops, velocity, weight, valid, offsets, at_links):
    boundary = at_links[0:3] + cross_product(at_links[3:6], offsets)
    along = jnp.sum(velocity * boundary, axis=0)
    return pops - 6.0 * weight * along * valid


def owner_update(motion, sums):
    mass = 4.0 / 3.0 * math.pi * RADIUS ** 3
    inertia = 0.4 * mass * RADIUS ** 2
    new_motion = jnp.concatenate([motion[0:3] + sums[0:3] / mass, motion[3:6] + sums[3:6] / inertia], axis=0)
    report = jnp.concatenate([sums[0:3], sums[3:6] / RADIUS], axis=0)
    return new_motion, report


def relax_colour(phi_pad, eps_pad, charge, colour_mask):
    eps_slab = jnp.pad(eps_pad, ((1, 1), (0, 0), (0, 0)), mode="edge")
    padded = jnp.pad(phi_pad, ((1, 1), (0, 0), (0, 0)))
    eps_centre = eps_slab[1:-1, 1:-1, 1:-1]
    centre = padded[1:-1, 1:-1, 1:-1]
    eps_sides = [eps_slab[:-2, 1:-1, 1:-1], eps_slab[2:, 1:-1, 1:-1], eps_slab[1:-1, :-2, 1:-1], eps_slab[1:-1, 2:, 1:-1], eps_slab[1:-1, 1:-1, :-2], eps_slab[1:-1, 1:-1, 2:]]
    phi_sides = [padded[:-2, 1:-1, 1:-1], padded[2:, 1:-1, 1:-1], padded[1:-1, :-2, 1:-1], padded[1:-1, 2:, 1:-1], padded[1:-1, 1:-1, :-2], padded[1:-1, 1:-1, 2:]]
    numerator = charge
    denominator = jnp.zeros_like(charge)
    for eps_side, phi_side in zip(eps_sides, phi_sides):
        face = 0.5 * (eps_centre + eps_side)
        numerator = numerator + face * phi_side
        denominator = denominator + face
    target = numerator / denominator
    return jnp.where(colour_mask, centre + OVER_RELAX * (target - centre), centre)


def reference(eps_field, charge, potential_start, colloid_vel, colloid_spin, link_dir, link_colloid, link_site, link_depth, link_pop, link_rb):
    eps_whole = eps_field.astype(jnp.float32)
    eps_pad = jnp.pad(eps_whole, ((0, 0), (1, 1), (1, 1)), mode="wrap")
    shape = charge.shape
    parity = (lax.broadcasted_iota(jnp.int32, shape, 0) + lax.broadcasted_iota(jnp.int32, shape, 1) + lax.broadcasted_iota(jnp.int32, shape, 2)) % 2
    potential = potential_start
    for sweep_index in range(SWEEPS):
        for colour in (0, 1):
            phi_pad = jnp.pad(potential, ((0, 0), (1, 1), (1, 1)), mode="wrap")
            potential = relax_colour(phi_pad, eps_pad, charge, parity == colour)

    phi_flat = potential.reshape(-1)
    eps_flat = eps_whole.reshape(-1)
    motion = jnp.concatenate([colloid_vel, colloid_spin], axis=0)
    motion_rows = motion.T
    tile_count = TILES_X * TILES_Y
    dirs_all = link_dir.reshape(tile_count, LINKS)
    ids_all = link_colloid.reshape(tile_count, LINKS)
    sites_all = link_site.reshape(tile_count, LINKS)
    depths_all = link_depth.reshape(tile_count, LINKS)
    pops_all = link_pop.reshape(tile_count, LINKS)
    offsets_all = link_rb.reshape(3, tile_count, LINKS).transpose(1, 0, 2)
    tile_ids = jnp.arange(tile_count, dtype=jnp.int32)

    def tile_sum(total, inputs):
        tile, directions, colloid_ids, sites, depth, pops, offsets = inputs
        velocity, weight = lattice_lookup(directions)
        valid_mask = colloid_ids >= 0
        valid = valid_mask.astype(jnp.float32)
        row = sites // TY + (tile // TILES_Y) * TX
        column = sites % TY + (tile % TILES_Y) * TY
        place = ((depth * NX + row) * NY + column).astype(jnp.int32)
        phi_here = jnp.take(phi_flat, place)
        pressure = 0.5 * jnp.take(eps_flat, place) * phi_here * phi_here
        at_links = jnp.take(motion_rows, jnp.where(valid_mask, colloid_ids, 0), axis=0).T
        terms = link_terms(pops, velocity, weight, valid, offsets, at_links, pressure)
        target = jnp.where(valid_mask, colloid_ids, NC).astype(jnp.int32)
        partial_value = jax.ops.segment_sum(terms.T, target, num_segments=NC + 1)[:NC]
        return total + partial_value, jnp.zeros((), jnp.float32)

    sums_rows = lax.scan(tile_sum, jnp.zeros((NC, 6), jnp.float32), (tile_ids, dirs_all, ids_all, sites_all, depths_all, pops_all, offsets_all))[0]
    new_motion, report = owner_update(motion, sums_rows.T)
    moved_rows = new_motion.T

    def tile_out(inputs):
        directions, colloid_ids, pops, offsets = inputs
        velocity, weight = lattice_lookup(directions)
        valid_mask = colloid_ids >= 0
        valid = valid_mask.astype(jnp.float32)
        at_links = jnp.take(moved_rows, jnp.where(valid_mask, colloid_ids, 0), axis=0).T
        return reflected(pops, velocity, weight, valid, offsets, at_links)

    link_out = lax.map(tile_out, (dirs_all, ids_all, pops_all, offsets_all)).reshape(TILES_X, TILES_Y, LINKS)
    return potential, report, link_out
```

```python
import math

import jax
import jax.numpy as jnp
import numpy as np
from jax import lax
from jax.experimental import pallas as pl
from jax.experimental.pallas import tpu as pltpu
from jax.sharding import PartitionSpec as P

TILES_X, TILES_Y = 8, 16
NC_DEV = 32
LINKS = 32768
RADIUS = 8
SWEEPS=6
OVER_RELAX=1.6
NZ, TX, TY = 48, 64, 128
HALF = NZ//2
ROWS = 112
TOP = 24
LANES = 256
DEPTH = 2*SWEEPS

def parity_mask(colour, shape):
    s = lax.broadcasted_iota(jnp.int32, shape, 0) + lax.broadcasted_iota(jnp.int32, shape, 1)
    return (s + colour) % 2 == 0

def relax_kernel(eps_ref, charge_ref, phi_ref, pot_ref, q_ref, p_refs, e_refs, c_refs, coef_refs):
    even = parity_mask(0, (8, LANES))
    lane = lax.broadcasted_iota(jnp.int32, (8, LANES), 1)
    inside = (lane < TY + 16) | (lane >= LANES - 16)
    zero = jnp.zeros((8, LANES), jnp.float32)
    for ref in (*p_refs, *e_refs):
        for g in (0, ROWS - 8):
            def clear(m, _):
                ref[m, g:g + 8, :] = zero
                return 0
            lax.fori_loop(0, HALF + 2, clear, 0)
    for ref in p_refs:
        for g in range(0, ROWS, 8):
            ref[0, g:g + 8, :] = zero
            ref[HALF + 1, g:g + 8, :] = zero

    def compact(m, _):
        for r in range(0, ROWS - 16, 16):
            a = eps_ref[2 * m, r:r + 16, :].astype(jnp.float32)
            b = eps_ref[2 * m + 1, r:r + 16, :].astype(jnp.float32)
            for h in (0, 8):
                a1, b1 = a[h:h + 8], b[h:h + 8]
                e_refs[0][m + 1, r + 8 + h:r + 16 + h, :] = jnp.where(even, a1, b1)
                e_refs[1][m + 1, r + 8 + h:r + 16 + h, :] = jnp.where(even, b1, a1)
        for r in range(0, ROWS - 16, 8):
            a = phi_ref[2 * m, r:r + 8, :]
            b = phi_ref[2 * m + 1, r:r + 8, :]
            p_refs[0][m + 1, r + 8:r + 16, :] = jnp.where(even, a, b)
            p_refs[1][m + 1, r + 8:r + 16, :] = jnp.where(even, b, a)
        return 0
    lax.fori_loop(0, HALF, compact, 0)
    for g in range(8, ROWS - 8, 8):
        for c in (0, 1):
            e_refs[1 - c][0, g:g + 8, :] = e_refs[c][1, g:g + 8, :]
            e_refs[1 - c][HALF + 1, g:g + 8, :] = e_refs[c][HALF, g:g + 8, :]

    def sides(ref, m, g, low):
        here = ref[m + 1, g:g + 8, :]
        return (
            here,
            jnp.where(low, ref[m, g:g + 8, :], ref[m + 2, g:g + 8, :]),
            ref[m + 1, g - 1:g + 7, :],
            ref[m + 1, g + 1:g + 9, :],
            pltpu.roll(here, 1, 1),
            pltpu.roll(here, LANES - 1, 1),
        )

    for c in (0, 1):
        low = even if c == 0 else ~even
        def coefs(m, _):
            for g in range(8, ROWS - 8, 8):
                centre = e_refs[c][m + 1, g:g + 8, :]
                faces = [0.5 * (centre + side) for side in sides(e_refs[1 - c], m, g, low)]
                total = faces[0]
                for face in faces[1:]:
                    total = total + face
                scale = jnp.where(inside & (total > 0.0), OVER_RELAX / total, 0.0)
                ch = jnp.where(low, charge_ref[2 * m, g - 8:g, :], charge_ref[2 * m + 1, g - 8:g, :])
                c_refs[c][m, g - 8:g, :] = scale * ch
                for i in range(6):
                    coef_refs[c][i, m, g - 8:g, :] = scale * faces[i]
            return 0
        lax.fori_loop(0, HALF, coefs, 0)

    for step in range(DEPTH):
        c = step % 2
        low = even if c == 0 else ~even
        reach = -(-(DEPTH - 1 - step) // 8) * 8
        def half(m, _):
            for g in range(TOP - reach, TOP + TX + reach, 8):
                value = c_refs[c][m, g - 8:g, :] - (OVER_RELAX - 1.0) * p_refs[c][m + 1, g:g + 8, :]
                for i, side in enumerate(sides(p_refs[1 - c], m, g, low)):
                    value = value + coef_refs[c][i, m, g - 8:g, :] * side
                p_refs[c][m + 1, g:g + 8, :] = value
            return 0
        lax.fori_loop(0, HALF, half, 0)

    evn = parity_mask(0, (8, TY))
    def out(m, _):
        for g in range(0, TX, 8):
            a = p_refs[0][m + 1, TOP + g:TOP + g + 8, 0:TY]
            b = p_refs[1][m + 1, TOP + g:TOP + g + 8, 0:TY]
            ea = e_refs[0][m + 1, TOP + g:TOP + g + 8, 0:TY]
            eb = e_refs[1][m + 1, TOP + g:TOP + g + 8, 0:TY]
            lo, hi = jnp.where(evn, a, b), jnp.where(evn, b, a)
            elo, ehi = jnp.where(evn, ea, eb), jnp.where(evn, eb, ea)
            pot_ref[2 * m, g:g + 8, :] = lo
            pot_ref[2 * m + 1, g:g + 8, :] = hi
            q_ref[2 * m, g:g + 8, :] = 0.5 * elo * lo * lo
            q_ref[2 * m + 1, g:g + 8, :] = 0.5 * ehi * hi * hi
        return 0
    lax.fori_loop(0, HALF, out, 0)

def relax(eps_p, charge_p, phi_p):
    vm = lambda *s: pltpu.VMEM(s, jnp.float32)
    return pl.pallas_call(
        relax_kernel,
        out_shape=(jax.ShapeDtypeStruct((NZ, TX, TY), jnp.float32),) * 2,
        in_specs=[pl.BlockSpec(memory_space=pltpu.VMEM)] * 3,
        out_specs=(pl.BlockSpec(memory_space=pltpu.VMEM),) * 2,
        scratch_shapes=[
            [vm(HALF + 2, ROWS, LANES)] * 2,
            [vm(HALF + 2, ROWS, LANES)] * 2,
            [vm(HALF, ROWS - 16, LANES)] * 2,
            [vm(6, HALF, ROWS - 16, LANES)] * 2,
        ],
        name="relax",
        compiler_params=pltpu.CompilerParams(vmem_limit_bytes=62 * 2**20),
    )(eps_p, charge_p, phi_p)


CHUNK = 4096
SLOTS = 9 * NC_DEV
SLOTS_PAD = 384
VELOCITY = np.array(
    [[1, 0, 0], [-1, 0, 0], [0, 1, 0], [0, -1, 0], [0, 0, 1], [0, 0, -1], [1, 1, 0], [1, -1, 0], [-1, 1, 0],
     [-1, -1, 0], [1, 0, 1], [1, 0, -1], [-1, 0, 1], [-1, 0, -1], [0, 1, 1], [0, 1, -1], [0, -1, 1], [0, -1, -1]],
    dtype=np.float32,
).T
WEIGHT = np.array([1.0 / 18.0] * 6 + [1.0 / 36.0] * 12, dtype=np.float32)


def lattice_table():
    rows = np.zeros((4, 8, 128), np.float32)
    rows[0:3, :, 0:18] = VELOCITY[:, None, :]
    rows[3, :, 0:18] = WEIGHT[None, :]
    return jnp.asarray(rows.reshape(32, 128))


def split(values):
    high = values.astype(jnp.bfloat16).astype(jnp.float32)
    return jnp.concatenate([high, values - high], axis=0).astype(jnp.bfloat16)


def cross(first, second):
    return (
        first[1] * second[2] - first[2] * second[1],
        first[2] * second[0] - first[0] * second[2],
        first[0] * second[1] - first[1] * second[0],
    )


def decode(lat_ref, direction):
    return [jnp.take_along_axis(lat_ref[8 * i:8 * i + 8, :], direction, axis=1) for i in range(4)]


def motions_at(table, slot_ref, base, onehot_ref, at_ref):
    ids = lax.broadcasted_iota(jnp.int32, (SLOTS, 128), 0)
    for pair in range(4):
        halves = [ids == slot_ref[pl.ds(base + 2 * pair + h, 1), :] for h in (0, 1)]
        onehot = jnp.concatenate([half.astype(jnp.float32) for half in halves], axis=1).astype(jnp.bfloat16)
        if onehot_ref is not None:
            onehot_ref[:, 256 * pair:256 * pair + 256] = onehot
        found = jnp.dot(table, onehot, preferred_element_type=jnp.float32)
        found = found[0:8] + found[8:16]
        at_ref[16 * pair:16 * pair + 8, :] = found[:, 0:128]
        at_ref[16 * pair + 8:16 * pair + 16, :] = found[:, 128:256]
    return [at_ref[pl.ds(i, 8, stride=8), :] for i in range(6)]


def along_link(motion, velocity, offsets):
    spin = cross(motion[3:6], offsets)
    return sum(velocity[i] * (motion[i] + spin[i]) for i in range(3))


def links_kernel(row_ref, site_ref, dir_ref, ids_ref, pop_ref, rb_ref, q_ref, table_ref, lat_ref, slot_ref, sums_ref, onehot_ref, at_ref, term_ref):
    home_x = lax.axis_index("gx")
    home_y = lax.axis_index("gy")
    lane = lax.broadcasted_iota(jnp.int32, (8, 128), 1)
    sub = lax.broadcasted_iota(jnp.int32, (8, 128), 0)

    @pl.when(pl.program_id(0) == 0)
    def _():
        sums_ref[...] = jnp.zeros_like(sums_ref)
        term_ref[...] = jnp.zeros_like(term_ref)

    table = split(table_ref[...])[:, 0:SLOTS]

    def group(b, _):
        base = pl.multiple_of(b * 8, 8)
        rows = pl.ds(base, 8)
        ids = ids_ref[rows, :]
        owner = ids >> 5
        near_x = ((owner >> 4) - home_x + 1) & (TILES_X - 1)
        near_y = ((owner & (TILES_Y - 1)) - home_y + 1) & (TILES_Y - 1)
        slot_ref[rows, :] = jnp.where(ids >= 0, (near_x * 3 + near_y) * NC_DEV + (ids & (NC_DEV - 1)), -1)
        column = site_ref[rows, :] & 127
        pressure = jnp.zeros((8, 128), jnp.float32)
        for j in range(128):
            at = lambda s: jnp.broadcast_to(q_ref[pl.ds(row_ref[b * 1024 + s * 128 + j], 1), :], (8, 128))
            picked = at(0)
            for s in range(1, 8):
                picked = jnp.where(sub == s, at(s), picked)
            pressure = jnp.where(lane == j, jnp.take_along_axis(picked, column, axis=1), pressure)
        *velocity, weight = decode(lat_ref, dir_ref[rows, :])
        offsets = [rb_ref[i, rows, :] for i in range(3)]
        motion = motions_at(table, slot_ref, base, onehot_ref, at_ref)
        along = along_link(motion, velocity, offsets)
        transfer = 2.0 * pop_ref[rows, :] - 6.0 * weight * along + weight * pressure
        transfer = jnp.where(ids >= 0, transfer, 0.0)
        force = [v * transfer for v in velocity]
        for i, term in enumerate((*force, *cross(offsets, force))):
            term_ref[pl.ds(i, 8, stride=8), :] = term
        total = jnp.zeros((16, SLOTS), jnp.float32)
        for pair in range(4):
            terms = jnp.concatenate([term_ref[16 * pair:16 * pair + 8, :], term_ref[16 * pair + 8:16 * pair + 16, :]], axis=1)
            total = total + lax.dot_general(
                split(terms), onehot_ref[:, 256 * pair:256 * pair + 256], (((1,), (1,)), ((), ())),
                preferred_element_type=jnp.float32,
            )
        sums_ref[:, 0:SLOTS] += total[0:8] + total[8:16]
        return 0

    lax.fori_loop(0, CHUNK // 1024, group, 0)


def link_spec(lead=None):
    if lead is None:
        return pl.BlockSpec((CHUNK // 128, 128), lambda i: (i, 0))
    return pl.BlockSpec((lead, CHUNK // 128, 128), lambda i: (0, i, 0))


def whole(*shape):
    return pl.BlockSpec(shape, lambda i: (0,) * len(shape))


def link_sums(row, site, direction, ids, pop, rb, q, table):
    return pl.pallas_call(
        links_kernel,
        grid=(LINKS // CHUNK,),
        in_specs=[
            pl.BlockSpec((CHUNK,), lambda i: (i,), memory_space=pltpu.SMEM),
            link_spec(), link_spec(), link_spec(), link_spec(), link_spec(3),
            whole(NZ * TX, TY), whole(8, SLOTS_PAD), whole(32, 128),
        ],
        out_specs=(link_spec(), whole(8, SLOTS_PAD)),
        out_shape=(jax.ShapeDtypeStruct((LINKS // 128, 128), jnp.int32), jax.ShapeDtypeStruct((8, SLOTS_PAD), jnp.float32)),
        scratch_shapes=[pltpu.VMEM((SLOTS, 1024), jnp.bfloat16), pltpu.VMEM((64, 128), jnp.float32), pltpu.VMEM((64, 128), jnp.float32)],
        name="link_sums",
        compiler_params=pltpu.CompilerParams(vmem_limit_bytes=40 * 2**20),
    )(row, site, direction, ids, pop, rb, q, table, lattice_table())


def reflect_kernel(dir_ref, slot_ref, pop_ref, rb_ref, table_ref, lat_ref, out_ref, at_ref):
    table = split(table_ref[...])[:, 0:SLOTS]

    def group(b, _):
        base = pl.multiple_of(b * 8, 8)
        rows = pl.ds(base, 8)
        *velocity, weight = decode(lat_ref, dir_ref[rows, :])
        offsets = [rb_ref[i, rows, :] for i in range(3)]
        motion = motions_at(table, slot_ref, base, None, at_ref)
        along = jnp.where(slot_ref[rows, :] >= 0, along_link(motion, velocity, offsets), 0.0)
        out_ref[rows, :] = pop_ref[rows, :] - 6.0 * weight * along
        return 0

    lax.fori_loop(0, CHUNK // 1024, group, 0)


def reflect(direction, slot, pop, rb, table):
    return pl.pallas_call(
        reflect_kernel,
        grid=(LINKS // CHUNK,),
        in_specs=[link_spec(), link_spec(), link_spec(), link_spec(3), whole(8, SLOTS_PAD), whole(32, 128)],
        out_specs=link_spec(),
        out_shape=jax.ShapeDtypeStruct((LINKS // 128, 128), jnp.float32),
        scratch_shapes=[pltpu.VMEM((64, 128), jnp.float32)],
        name="reflect",
        compiler_params=pltpu.CompilerParams(vmem_limit_bytes=40 * 2**20),
    )(direction, slot, pop, rb, table, lattice_table())


def beside():
    x, y = lax.axis_index("gx"), lax.axis_index("gy")
    for t in range(9):
        if t != 4:
            yield t, (lax.rem(x + t // 3 - 1 + TILES_X, TILES_X), lax.rem(y + t % 3 - 1 + TILES_Y, TILES_Y))


def greet():
    barrier = pltpu.get_barrier_semaphore()
    for _, device in beside():
        pl.semaphore_signal(barrier, inc=1, device_id=device, device_id_type=pl.DeviceIdType.MESH)
    pl.semaphore_wait(barrier, 8)


def post(source, got_ref, send_sem, recv_sem):
    copies = []
    for t, device in beside():
        copy = pltpu.make_async_remote_copy(
            src_ref=source(t), dst_ref=got_ref.at[8 - t], send_sem=send_sem.at[t], recv_sem=recv_sem.at[8 - t],
            device_id=device, device_id_type=pl.DeviceIdType.MESH,
        )
        copy.start()
        copies.append(copy)
    return copies


def write_table(table_ref, block):
    for tile in range(3):
        total = jnp.zeros((8, 128), jnp.float32)
        for i in range(4):
            if 4 * tile + i < 9:
                value = block(4 * tile + i)
                total = total + (pltpu.roll(value, NC_DEV * i, 1) if i else value)
        table_ref[:, 128 * tile:128 * tile + 128] = total


def share_kernel(motion_ref, table_ref, got_ref, send_sem, recv_sem):
    greet()
    copies = post(lambda t: motion_ref, got_ref, send_sem, recv_sem)
    for copy in copies:
        copy.wait()
    write_table(table_ref, lambda t: motion_ref[...] if t == 4 else got_ref[t])


def update_kernel(sums_ref, motion_ref, report_ref, table_ref, part_ref, got_ref, new_ref, back_ref, send_sem, recv_sem, send2_sem, recv2_sem):
    greet()
    lane = lax.broadcasted_iota(jnp.int32, (8, 128), 1)
    row = lax.broadcasted_iota(jnp.int32, (8, 128), 0)
    for t in range(9):
        value = sums_ref[:, 128 * (t // 4):128 * (t // 4) + 128]
        if t % 4:
            value = pltpu.roll(value, 128 - NC_DEV * (t % 4), 1)
        part_ref[t] = jnp.where(lane < NC_DEV, value, 0.0)
    copies = post(lambda t: part_ref.at[t], got_ref, send_sem, recv_sem)
    total = part_ref[4]
    for copy in copies:
        copy.wait()
    for t in range(9):
        if t != 4:
            total = total + got_ref[t]
    mass = 4.0 / 3.0 * math.pi * RADIUS**3
    inertia = 0.4 * mass * RADIUS**2
    report_ref[...] = jnp.where(row < 3, total, total / RADIUS)
    new_ref[...] = motion_ref[...] + jnp.where(row < 3, total / mass, total / inertia)
    copies = post(lambda t: new_ref, back_ref, send2_sem, recv2_sem)
    for copy in copies:
        copy.wait()
    write_table(table_ref, lambda t: new_ref[...] if t == 4 else back_ref[t])


VM = pl.BlockSpec(memory_space=pltpu.VMEM)


def share_motion(motion):
    return pl.pallas_call(
        share_kernel,
        out_shape=jax.ShapeDtypeStruct((8, SLOTS_PAD), jnp.float32),
        in_specs=[VM],
        out_specs=VM,
        scratch_shapes=[pltpu.VMEM((9, 8, 128), jnp.float32), pltpu.SemaphoreType.DMA((9,)), pltpu.SemaphoreType.DMA((9,))],
        name="share_motion",
        compiler_params=pltpu.CompilerParams(collective_id=0, has_side_effects=True),
    )(motion)


def update(sums, motion):
    return pl.pallas_call(
        update_kernel,
        out_shape=(jax.ShapeDtypeStruct((8, 128), jnp.float32), jax.ShapeDtypeStruct((8, SLOTS_PAD), jnp.float32)),
        in_specs=[VM, VM],
        out_specs=(VM, VM),
        scratch_shapes=[
            pltpu.VMEM((9, 8, 128), jnp.float32), pltpu.VMEM((9, 8, 128), jnp.float32),
            pltpu.VMEM((8, 128), jnp.float32), pltpu.VMEM((9, 8, 128), jnp.float32),
            pltpu.SemaphoreType.DMA((9,)), pltpu.SemaphoreType.DMA((9,)), pltpu.SemaphoreType.DMA((9,)), pltpu.SemaphoreType.DMA((9,)),
        ],
        name="update",
        compiler_params=pltpu.CompilerParams(collective_id=1, has_side_effects=True),
    )(sums, motion)


def neighbours(axis, value_low, value_high):
    count = lax.axis_size(axis)
    forward = [(i, (i + 1) % count) for i in range(count)]
    backward = [(target, source) for source, target in forward]
    return lax.ppermute(value_low, axis, forward), lax.ppermute(value_high, axis, backward)


def framed(block):
    low, high = neighbours("gx", block[:, TX - 16:], block[:, :16])
    block = jnp.concatenate([low, block, high], axis=1)
    low, high = neighbours("gy", block[:, :, TY - 16:], block[:, :, :16])
    gap = jnp.zeros((NZ, TX + 32, LANES - TY - 32), block.dtype)
    return jnp.concatenate([block, high, gap, low], axis=2)


def shards(
    eps_field, charge, potential_start, colloid_vel, colloid_spin, link_dir, link_colloid, link_site, link_depth,
    link_pop, link_rb,
):
    flat = lambda a: a.reshape(LINKS // 128, 128)
    motion = jnp.pad(jnp.concatenate([colloid_vel, colloid_spin], axis=0), ((0, 2), (0, 128 - NC_DEV)))
    table = share_motion(motion)
    potential, q = relax(framed(eps_field), framed(charge), framed(potential_start))
    row = link_depth.reshape(-1) * TX + (link_site.reshape(-1) >> 7)
    rb = link_rb.reshape(3, LINKS // 128, 128)
    slot, sums = link_sums(
        row, flat(link_site), flat(link_dir), flat(link_colloid), flat(link_pop), rb, q.reshape(NZ * TX, TY), table
    )
    report, table = update(sums, motion)
    link_out = reflect(flat(link_dir), slot, flat(link_pop), rb, table).reshape(link_pop.shape)
    return potential, report[0:6, 0:NC_DEV], link_out


def solution(mesh):
    tile = P(None, "gx", "gy")
    owned = P(None, ("gx", "gy"))
    link = P("gx", "gy", None)
    return jax.shard_map(
        shards,
        mesh=mesh,
        in_specs=(tile, tile, tile, owned, owned, link, link, link, link, link, P(None, "gx", "gy", None)),
        out_specs=(tile, owned, link),
        check_vma=False,
    )
```

```python
import math

import jax
import jax.numpy as jnp
import numpy as np
from jax import lax
from jax.experimental import pallas as pl
from jax.experimental.pallas import tpu as pltpu
from jax.sharding import PartitionSpec as P

TILES_X, TILES_Y = 8, 16
NC_DEV = 32
LINKS = 32768
RADIUS = 8
SWEEPS = 6
OVER_RELAX = 1.6
NZ, TX, TY = 48, 64, 128
HALF = NZ // 2
GROUPS = HALF // 8
ROWS = 96
TOP = 16


def beside():
    x, y = lax.axis_index("gx"), lax.axis_index("gy")
    for t in range(9):
        if t != 4:
            yield t, (lax.rem(x + t // 3 - 1 + TILES_X, TILES_X), lax.rem(y + t % 3 - 1 + TILES_Y, TILES_Y))


def greet():
    barrier = pltpu.get_barrier_semaphore()
    for _, device in beside():
        pl.semaphore_signal(barrier, inc=1, device_id=device, device_id_type=pl.DeviceIdType.MESH)
    return lambda: pl.semaphore_wait(barrier, 8)


class Mail:
    def __init__(self, send_sem, recv_sem):
        self.sems, self.count, self.copies, self.device = (send_sem, recv_sem), 0, [], dict(beside())

    def send(self, t, source, target):
        copy = pltpu.make_async_remote_copy(
            src_ref=source, dst_ref=target, send_sem=self.sems[0].at[self.count], recv_sem=self.sems[1].at[self.count],
            device_id=self.device[t], device_id_type=pl.DeviceIdType.MESH,
        )
        copy.start()
        self.count += 1
        self.copies.append(copy)

    def wait(self):
        for copy in self.copies:
            copy.wait()
        self.copies = []


def write_table(table_ref, block):
    for tile in range(3):
        total = jnp.zeros((8, 128), jnp.float32)
        for i in range(4):
            if 4 * tile + i < 9:
                value = block(4 * tile + i)
                total = total + (pltpu.roll(value, NC_DEV * i, 1) if i else value)
        table_ref[:, 128 * tile:128 * tile + 128] = total


def relax_kernel(
    eps_ref, charge_ref, phi_ref, motion_ref, pot_ref, q_ref, table_ref,
    p_refs, e_refs, ps_refs, es_refs, gs_refs, c_refs, coef_refs, cs_refs, coefs_refs,
    to_low, to_high, from_low, from_high, x_eps, x_charge, x_phi, to2_low, to2_high, from2_low, from2_high, x2_refs,
    got_ref, send_sem, recv_sem,
):
    sub = lax.broadcasted_iota(jnp.int32, (8, 128), 0)
    lane = lax.broadcasted_iota(jnp.int32, (8, 128), 1)
    even = (sub + lane) % 2 == 0
    odd = ~even
    first = lane % 16 < 8
    slot = lane // 16
    zero = jnp.zeros((8, 128), jnp.float32)
    blocks = range(8, ROWS - 8, 8)
    greeted = greet()
    mail = Mail(send_sem, recv_sem)

    def pack(plane, low_ref, high_ref, at):
        def group(g, _):
            for r in range(0, TX, 16):
                low, high = [zero, zero], [zero, zero]
                for k in range(16):
                    rows = plane(g, k, r)
                    for h in (0, 1):
                        value = rows[h]
                        here = lane // 8 == k
                        low[h] = jnp.where(here, pltpu.roll(value, 8 * k, 1) if k else value, low[h])
                        high[h] = jnp.where(here, pltpu.roll(value, 8 * (k + 1), 1) if k < 15 else value, high[h])
                for h in (0, 1):
                    low_ref[at + g, r + 8 * h:r + 8 * h + 8, :] = low[h]
                    high_ref[at + g, r + 8 * h:r + 8 * h + 8, :] = high[h]
            return 0
        lax.fori_loop(0, GROUPS, group, 0)

    def send_sides(low_ref, high_ref, dst_low, dst_high, at):
        span = pl.ds(at, GROUPS)
        for t, rows, target in ((3, (0, TX), 8), (0, (0, 8), 72), (6, (TX - 8, 8), 0)):
            mail.send(t, low_ref.at[span, pl.ds(*rows), :], dst_high.at[span, pl.ds(target, rows[1]), :])
            mail.send(t + 2, high_ref.at[span, pl.ds(*rows), :], dst_low.at[span, pl.ds(target, rows[1]), :])

    def natural(ref):
        def plane(g, k, r):
            value = ref[16 * g + k, r:r + 16, :].astype(jnp.float32)
            return value[0:8], value[8:16]
        return plane

    pack(natural(phi_ref), to_low, to_high, 0)
    greeted()
    send_sides(to_low, to_high, from_low, from_high, 0)
    for ref, target, rows in ((phi_ref, x_phi, 8), (eps_ref, x_eps, 16), (charge_ref, x_charge, 8)):
        mail.send(1, ref.at[:, pl.ds(0, rows), :], target.at[1])
        mail.send(7, ref.at[:, pl.ds(TX - rows, rows), :], target.at[0])
    pack(natural(eps_ref), to_low, to_high, GROUPS)
    send_sides(to_low, to_high, from_low, from_high, GROUPS)
    pack(natural(charge_ref), to_low, to_high, 2 * GROUPS)
    send_sides(to_low, to_high, from_low, from_high, 2 * GROUPS)
    for t, _ in beside():
        mail.send(t, motion_ref, got_ref.at[8 - t])

    def clear(m, _):
        for ref in (*p_refs, *e_refs):
            for g in (0, ROWS - 8):
                ref[m, g:g + 8, :] = zero
        return 0
    lax.fori_loop(0, HALF + 2, clear, 0)
    for ref in p_refs:
        for g in blocks:
            ref[0, g:g + 8, :] = zero
            ref[HALF + 1, g:g + 8, :] = zero
    for ref in (*ps_refs, *es_refs):
        for g in (0, ROWS - 8):
            for m in range(GROUPS + 2):
                ref[m, g:g + 8, :] = zero
    for ref in ps_refs:
        for g in blocks:
            ref[0, g:g + 8, :] = zero
            ref[GROUPS + 1, g:g + 8, :] = zero

    def two(refs, m, rows, a, b):
        refs[0][m, rows, :] = jnp.where(even, a, b)
        refs[1][m, rows, :] = jnp.where(even, b, a)

    def compact(m, _):
        for r in range(0, TX, 16):
            a = eps_ref[2 * m, r:r + 16, :].astype(jnp.float32)
            b = eps_ref[2 * m + 1, r:r + 16, :].astype(jnp.float32)
            for h in (0, 8):
                two(e_refs, m + 1, slice(TOP + r + h, TOP + r + h + 8), a[h:h + 8], b[h:h + 8])
        for r in range(0, TX, 8):
            two(p_refs, m + 1, slice(TOP + r, TOP + r + 8), phi_ref[2 * m, r:r + 8, :], phi_ref[2 * m + 1, r:r + 8, :])
        return 0
    lax.fori_loop(0, HALF, compact, 0)

    mail.wait()
    write_table(table_ref, lambda t: motion_ref[...] if t == 4 else got_ref[t])

    def edges(m, _):
        for side, g in ((0, 8), (1, TOP + TX)):
            rows = slice(8, 16) if side == 0 else slice(0, 8)
            a = x_eps[side, 2 * m].astype(jnp.float32)[rows]
            b = x_eps[side, 2 * m + 1].astype(jnp.float32)[rows]
            two(e_refs, m + 1, slice(g, g + 8), a, b)
            two(p_refs, m + 1, slice(g, g + 8), x_phi[side, 2 * m], x_phi[side, 2 * m + 1])
        return 0
    lax.fori_loop(0, HALF, edges, 0)

    def unpacked(low_ref, high_ref, at, r):
        low, high = low_ref[at, r:r + 8, :], high_ref[at, r:r + 8, :]
        return jnp.where(first, low, pltpu.roll(high, 8, 1)), jnp.where(first, pltpu.roll(low, 120, 1), high)

    def strips(g, _):
        for r in range(0, TX + 16, 8):
            rows = slice(8 + r, 16 + r)
            two(ps_refs, g + 1, rows, *unpacked(from_low, from_high, g, r))
            two(es_refs, g + 1, rows, *unpacked(from_low, from_high, GROUPS + g, r))
            two(gs_refs, g, slice(r, r + 8), *unpacked(from_low, from_high, 2 * GROUPS + g, r))
        return 0
    lax.fori_loop(0, GROUPS, strips, 0)
    for g in blocks:
        rows = slice(g, g + 8)
        for c in (0, 1):
            e_refs[1 - c][0, rows, :] = e_refs[c][1, rows, :]
            e_refs[1 - c][HALF + 1, rows, :] = e_refs[c][HALF, rows, :]
            es_refs[1 - c][0, rows, :] = pltpu.roll(es_refs[c][1, rows, :], 112, 1)
            es_refs[1 - c][GROUPS + 1, rows, :] = pltpu.roll(es_refs[c][GROUPS, rows, :], 16, 1)

    def main_sides(ref, strip_ref, m, g, low):
        rows = slice(g, g + 8)
        here = ref[m + 1, rows, :]
        seam = pltpu.roll(strip_ref[m // 8 + 1, rows, :], 120 - 16 * (m % 8), 1)
        return (
            here,
            jnp.where(low, ref[m, rows, :], ref[m + 2, rows, :]),
            ref[m + 1, g - 1:g + 7, :],
            ref[m + 1, g + 1:g + 9, :],
            pltpu.roll(jnp.where(lane == 127, seam, here), 1, 1),
            pltpu.roll(jnp.where(lane == 0, seam, here), 127, 1),
        )

    def strip_sides(ref, strip_ref, n, g, low):
        rows = slice(g, g + 8)
        here = strip_ref[n + 1, rows, :]
        seam = zero
        for k in range(8):
            seam = jnp.where(slot == k, pltpu.roll(ref[8 * n + k + 1, rows, :], 16 * k + 8, 1), seam)
        below = pltpu.roll(jnp.where(slot == 7, strip_ref[n, rows, :], here), 16, 1)
        above = pltpu.roll(jnp.where(slot == 0, strip_ref[n + 2, rows, :], here), 112, 1)
        return (
            here,
            jnp.where(low, below, above),
            strip_ref[n + 1, g - 1:g + 7, :],
            strip_ref[n + 1, g + 1:g + 9, :],
            pltpu.roll(jnp.where(lane % 16 == 7, seam, here), 1, 1),
            pltpu.roll(jnp.where(lane % 16 == 8, seam, here), 127, 1),
        )

    def weights(centre, sides, charge, c_ref, coef_ref, m, g):
        faces = [0.5 * (centre + side) for side in sides]
        total = faces[0]
        for face in faces[1:]:
            total = total + face
        scale = OVER_RELAX / total
        c_ref[m, g - 8:g, :] = scale * charge
        for i in range(6):
            coef_ref[i, m, g - 8:g, :] = scale * faces[i]

    for c in (0, 1):
        low = odd if c else even

        def main_weights(m, _):
            for g in blocks:
                if g == 8:
                    a, b = x_charge[0, 2 * m], x_charge[0, 2 * m + 1]
                elif g == TOP + TX:
                    a, b = x_charge[1, 2 * m], x_charge[1, 2 * m + 1]
                else:
                    a, b = charge_ref[2 * m, g - TOP:g - TOP + 8, :], charge_ref[2 * m + 1, g - TOP:g - TOP + 8, :]
                sides = main_sides(e_refs[1 - c], es_refs[1 - c], m, g, low)
                weights(e_refs[c][m + 1, g:g + 8, :], sides, jnp.where(low, a, b), c_refs[c], coef_refs[c], m, g)
            return 0
        lax.fori_loop(0, HALF, main_weights, 0)

        def strip_weights(n, _):
            for g in blocks:
                sides = strip_sides(e_refs[1 - c], es_refs[1 - c], n, g, low)
                weights(es_refs[c][n + 1, g:g + 8, :], sides, gs_refs[c][n, g - 8:g, :], cs_refs[c], coefs_refs[c], n, g)
            return 0
        lax.fori_loop(0, GROUPS, strip_weights, 0)

    def updated(own, sides, c_ref, coef_ref, m, g):
        value = c_ref[m, g - 8:g, :] - (OVER_RELAX - 1.0) * own
        for i, side in enumerate(sides):
            value = value + coef_ref[i, m, g - 8:g, :] * side
        return value

    def step(c, inner):
        low = odd if c else even

        def main_step(m, _):
            for g in blocks[1:-1] if inner else blocks:
                sides = main_sides(p_refs[1 - c], ps_refs[1 - c], m, g, low)
                p_refs[c][m + 1, g:g + 8, :] = updated(p_refs[c][m + 1, g:g + 8, :], sides, c_refs[c], coef_refs[c], m, g)
            return 0
        lax.fori_loop(0, HALF, main_step, 0)
        if inner:
            return

        def strip_step(n, _):
            for g in blocks:
                sides = strip_sides(p_refs[1 - c], ps_refs[1 - c], n, g, low)
                ps_refs[c][n + 1, g:g + 8, :] = updated(ps_refs[c][n + 1, g:g + 8, :], sides, cs_refs[c], coefs_refs[c], n, g)
            return 0
        lax.fori_loop(0, GROUPS, strip_step, 0)

    def three(i, _):
        step(0, False)
        step(1, False)
        return 0
    lax.fori_loop(0, 3, three, 0)
    step(0, False)
    step(1, True)

    def coloured(g, k, r):
        value = p_refs[k % 2][8 * g + k // 2 + 1, TOP + r:TOP + r + 16, :]
        return value[0:8], value[8:16]

    for c in (0, 1):
        mail.send(1, p_refs[c].at[pl.ds(1, HALF), pl.ds(TOP, 8), :], x2_refs[c].at[1])
        mail.send(7, p_refs[c].at[pl.ds(1, HALF), pl.ds(TOP + TX - 8, 8), :], x2_refs[c].at[0])
    pack(coloured, to2_low, to2_high, 0)
    send_sides(to2_low, to2_high, from2_low, from2_high, 0)
    mail.wait()

    def edges2(m, _):
        for c in (0, 1):
            p_refs[c][m + 1, 8:16, :] = x2_refs[c][0, m]
            p_refs[c][m + 1, TOP + TX:TOP + TX + 8, :] = x2_refs[c][1, m]
        return 0
    lax.fori_loop(0, HALF, edges2, 0)

    def strips2(g, _):
        for r in range(0, TX + 16, 8):
            a, b = unpacked(from2_low, from2_high, g, r)
            ps_refs[0][g + 1, 8 + r:16 + r, :] = a
            ps_refs[1][g + 1, 8 + r:16 + r, :] = b
        return 0
    lax.fori_loop(0, GROUPS, strips2, 0)
    step(0, False)
    step(1, False)
    step(0, False)
    step(1, True)

    def out(m, _):
        for g in range(0, TX, 8):
            a, b = [ref[m + 1, TOP + g:TOP + g + 8, :] for ref in p_refs]
            ea, eb = [ref[m + 1, TOP + g:TOP + g + 8, :] for ref in e_refs]
            lo, hi = jnp.where(even, a, b), jnp.where(even, b, a)
            elo, ehi = jnp.where(even, ea, eb), jnp.where(even, eb, ea)
            pot_ref[2 * m, g:g + 8, :] = lo
            pot_ref[2 * m + 1, g:g + 8, :] = hi
            q_ref[2 * m, g:g + 8, :] = 0.5 * elo * lo * lo
            q_ref[2 * m + 1, g:g + 8, :] = 0.5 * ehi * hi * hi
        return 0
    lax.fori_loop(0, HALF, out, 0)


def relax(eps, charge, phi, motion):
    vm = lambda *s: pltpu.VMEM(s, jnp.float32)
    spec = pl.BlockSpec(memory_space=pltpu.VMEM)
    return pl.pallas_call(
        relax_kernel,
        out_shape=(
            jax.ShapeDtypeStruct((NZ, TX, TY), jnp.float32),
            jax.ShapeDtypeStruct((NZ, TX, TY), jnp.float32),
            jax.ShapeDtypeStruct((8, SLOTS_PAD), jnp.float32),
        ),
        in_specs=[spec] * 4,
        out_specs=(spec,) * 3,
        scratch_shapes=[
            [vm(HALF + 2, ROWS, 128)] * 2,
            [vm(HALF + 2, ROWS, 128)] * 2,
            [vm(GROUPS + 2, ROWS, 128)] * 2,
            [vm(GROUPS + 2, ROWS, 128)] * 2,
            [vm(GROUPS, ROWS - 16, 128)] * 2,
            [vm(HALF, ROWS - 16, 128)] * 2,
            [vm(6, HALF, ROWS - 16, 128)] * 2,
            [vm(GROUPS, ROWS - 16, 128)] * 2,
            [vm(6, GROUPS, ROWS - 16, 128)] * 2,
            vm(3 * GROUPS, TX, 128), vm(3 * GROUPS, TX, 128),
            vm(3 * GROUPS, TX + 16, 128), vm(3 * GROUPS, TX + 16, 128),
            pltpu.VMEM((2, NZ, 16, 128), jnp.bfloat16), vm(2, NZ, 8, 128), vm(2, NZ, 8, 128),
            vm(GROUPS, TX, 128), vm(GROUPS, TX, 128),
            vm(GROUPS, TX + 16, 128), vm(GROUPS, TX + 16, 128),
            [vm(2, HALF, 8, 128)] * 2,
            vm(9, 8, 128),
            pltpu.SemaphoreType.DMA((42,)), pltpu.SemaphoreType.DMA((42,)),
        ],
        name="relax",
        compiler_params=pltpu.CompilerParams(vmem_limit_bytes=58 * 2**20, collective_id=0, has_side_effects=True),
    )(eps, charge, phi, motion)


CHUNK = 4096
SLOTS = 9 * NC_DEV
SLOTS_PAD = 384
VELOCITY = np.array(
    [[1, 0, 0], [-1, 0, 0], [0, 1, 0], [0, -1, 0], [0, 0, 1], [0, 0, -1], [1, 1, 0], [1, -1, 0], [-1, 1, 0],
     [-1, -1, 0], [1, 0, 1], [1, 0, -1], [-1, 0, 1], [-1, 0, -1], [0, 1, 1], [0, 1, -1], [0, -1, 1], [0, -1, -1]],
    dtype=np.float32,
).T
WEIGHT = np.array([1.0 / 18.0] * 6 + [1.0 / 36.0] * 12, dtype=np.float32)


def lattice_table():
    rows = np.zeros((4, 8, 128), np.float32)
    rows[0:3, :, 0:18] = VELOCITY[:, None, :]
    rows[3, :, 0:18] = WEIGHT[None, :]
    return jnp.asarray(rows.reshape(32, 128))


def split(values):
    high = values.astype(jnp.bfloat16).astype(jnp.float32)
    return jnp.concatenate([high, values - high], axis=0).astype(jnp.bfloat16)


def cross(first, second):
    return (
        first[1] * second[2] - first[2] * second[1],
        first[2] * second[0] - first[0] * second[2],
        first[0] * second[1] - first[1] * second[0],
    )


def decode(lat_ref, direction):
    return [jnp.take_along_axis(lat_ref[8 * i:8 * i + 8, :], direction, axis=1) for i in range(4)]


def motions_at(table, slot_ref, base, onehot_ref, at_ref):
    ids = lax.broadcasted_iota(jnp.int32, (SLOTS, 128), 0)
    for pair in range(4):
        halves = [ids == slot_ref[pl.ds(base + 2 * pair + h, 1), :] for h in (0, 1)]
        onehot = jnp.concatenate([half.astype(jnp.float32) for half in halves], axis=1).astype(jnp.bfloat16)
        if onehot_ref is not None:
            onehot_ref[:, 256 * pair:256 * pair + 256] = onehot
        found = jnp.dot(table, onehot, preferred_element_type=jnp.float32)
        found = found[0:8] + found[8:16]
        at_ref[16 * pair:16 * pair + 8, :] = found[:, 0:128]
        at_ref[16 * pair + 8:16 * pair + 16, :] = found[:, 128:256]
    return [at_ref[pl.ds(i, 8, stride=8), :] for i in range(6)]


def along_link(motion, velocity, offsets):
    spin = cross(motion[3:6], offsets)
    return sum(velocity[i] * (motion[i] + spin[i]) for i in range(3))


def links_kernel(row_ref, site_ref, dir_ref, ids_ref, pop_ref, rb_ref, q_ref, table_ref, lat_ref, slot_ref, sums_ref, onehot_ref, at_ref, term_ref):
    home_x = lax.axis_index("gx")
    home_y = lax.axis_index("gy")
    lane = lax.broadcasted_iota(jnp.int32, (8, 128), 1)
    sub = lax.broadcasted_iota(jnp.int32, (8, 128), 0)

    @pl.when(pl.program_id(0) == 0)
    def _():
        sums_ref[...] = jnp.zeros_like(sums_ref)
        term_ref[...] = jnp.zeros_like(term_ref)

    table = split(table_ref[...])[:, 0:SLOTS]

    def group(b, _):
        base = pl.multiple_of(b * 8, 8)
        rows = pl.ds(base, 8)
        ids = ids_ref[rows, :]
        owner = ids >> 5
        near_x = ((owner >> 4) - home_x + 1) & (TILES_X - 1)
        near_y = ((owner & (TILES_Y - 1)) - home_y + 1) & (TILES_Y - 1)
        slot_ref[rows, :] = jnp.where(ids >= 0, (near_x * 3 + near_y) * NC_DEV + (ids & (NC_DEV - 1)), -1)
        column = site_ref[rows, :] & 127
        pressure = jnp.zeros((8, 128), jnp.float32)
        for j in range(128):
            at = lambda s: jnp.broadcast_to(q_ref[pl.ds(row_ref[b * 1024 + s * 128 + j], 1), :], (8, 128))
            picked = at(0)
            for s in range(1, 8):
                picked = jnp.where(sub == s, at(s), picked)
            pressure = jnp.where(lane == j, jnp.take_along_axis(picked, column, axis=1), pressure)
        *velocity, weight = decode(lat_ref, dir_ref[rows, :])
        offsets = [rb_ref[i, rows, :] for i in range(3)]
        motion = motions_at(table, slot_ref, base, onehot_ref, at_ref)
        along = along_link(motion, velocity, offsets)
        transfer = 2.0 * pop_ref[rows, :] - 6.0 * weight * along + weight * pressure
        transfer = jnp.where(ids >= 0, transfer, 0.0)
        force = [v * transfer for v in velocity]
        for i, term in enumerate((*force, *cross(offsets, force))):
            term_ref[pl.ds(i, 8, stride=8), :] = term
        total = jnp.zeros((16, SLOTS), jnp.float32)
        for pair in range(4):
            terms = jnp.concatenate([term_ref[16 * pair:16 * pair + 8, :], term_ref[16 * pair + 8:16 * pair + 16, :]], axis=1)
            total = total + lax.dot_general(
                split(terms), onehot_ref[:, 256 * pair:256 * pair + 256], (((1,), (1,)), ((), ())),
                preferred_element_type=jnp.float32,
            )
        sums_ref[:, 0:SLOTS] += total[0:8] + total[8:16]
        return 0

    lax.fori_loop(0, CHUNK // 1024, group, 0)


def link_spec(lead=None):
    if lead is None:
        return pl.BlockSpec((CHUNK // 128, 128), lambda i: (i, 0))
    return pl.BlockSpec((lead, CHUNK // 128, 128), lambda i: (0, i, 0))


def whole(*shape):
    return pl.BlockSpec(shape, lambda i: (0,) * len(shape))


def link_sums(row, site, direction, ids, pop, rb, q, table):
    return pl.pallas_call(
        links_kernel,
        grid=(LINKS // CHUNK,),
        in_specs=[
            pl.BlockSpec((CHUNK,), lambda i: (i,), memory_space=pltpu.SMEM),
            link_spec(), link_spec(), link_spec(), link_spec(), link_spec(3),
            whole(NZ * TX, TY), whole(8, SLOTS_PAD), whole(32, 128),
        ],
        out_specs=(link_spec(), whole(8, SLOTS_PAD)),
        out_shape=(jax.ShapeDtypeStruct((LINKS // 128, 128), jnp.int32), jax.ShapeDtypeStruct((8, SLOTS_PAD), jnp.float32)),
        scratch_shapes=[pltpu.VMEM((SLOTS, 1024), jnp.bfloat16), pltpu.VMEM((64, 128), jnp.float32), pltpu.VMEM((64, 128), jnp.float32)],
        name="link_sums",
        compiler_params=pltpu.CompilerParams(vmem_limit_bytes=40 * 2**20),
    )(row, site, direction, ids, pop, rb, q, table, lattice_table())


def reflect_kernel(dir_ref, slot_ref, pop_ref, rb_ref, table_ref, lat_ref, out_ref, at_ref):
    table = split(table_ref[...])[:, 0:SLOTS]

    def group(b, _):
        base = pl.multiple_of(b * 8, 8)
        rows = pl.ds(base, 8)
        *velocity, weight = decode(lat_ref, dir_ref[rows, :])
        offsets = [rb_ref[i, rows, :] for i in range(3)]
        motion = motions_at(table, slot_ref, base, None, at_ref)
        along = jnp.where(slot_ref[rows, :] >= 0, along_link(motion, velocity, offsets), 0.0)
        out_ref[rows, :] = pop_ref[rows, :] - 6.0 * weight * along
        return 0

    lax.fori_loop(0, CHUNK // 1024, group, 0)


def reflect(direction, slot, pop, rb, table):
    return pl.pallas_call(
        reflect_kernel,
        grid=(LINKS // CHUNK,),
        in_specs=[link_spec(), link_spec(), link_spec(), link_spec(3), whole(8, SLOTS_PAD), whole(32, 128)],
        out_specs=link_spec(),
        out_shape=jax.ShapeDtypeStruct((LINKS // 128, 128), jnp.float32),
        scratch_shapes=[pltpu.VMEM((64, 128), jnp.float32)],
        name="reflect",
        compiler_params=pltpu.CompilerParams(vmem_limit_bytes=40 * 2**20),
    )(direction, slot, pop, rb, table, lattice_table())


def update_kernel(sums_ref, motion_ref, report_ref, table_ref, part_ref, got_ref, new_ref, back_ref, send_sem, recv_sem):
    greeted = greet()
    mail = Mail(send_sem, recv_sem)
    lane = lax.broadcasted_iota(jnp.int32, (8, 128), 1)
    row = lax.broadcasted_iota(jnp.int32, (8, 128), 0)
    for t in range(9):
        value = sums_ref[:, 128 * (t // 4):128 * (t // 4) + 128]
        if t % 4:
            value = pltpu.roll(value, 128 - NC_DEV * (t % 4), 1)
        part_ref[t] = jnp.where(lane < NC_DEV, value, 0.0)
    greeted()
    for t, _ in beside():
        mail.send(t, part_ref.at[t], got_ref.at[8 - t])
    total = part_ref[4]
    mail.wait()
    for t in range(9):
        if t != 4:
            total = total + got_ref[t]
    mass = 4.0 / 3.0 * math.pi * RADIUS**3
    inertia = 0.4 * mass * RADIUS**2
    report_ref[...] = jnp.where(row < 3, total, total / RADIUS)
    new_ref[...] = motion_ref[...] + jnp.where(row < 3, total / mass, total / inertia)
    for t, _ in beside():
        mail.send(t, new_ref, back_ref.at[8 - t])
    mail.wait()
    write_table(table_ref, lambda t: new_ref[...] if t == 4 else back_ref[t])


VM = pl.BlockSpec(memory_space=pltpu.VMEM)


def update(sums, motion):
    return pl.pallas_call(
        update_kernel,
        out_shape=(jax.ShapeDtypeStruct((8, 128), jnp.float32), jax.ShapeDtypeStruct((8, SLOTS_PAD), jnp.float32)),
        in_specs=[VM, VM],
        out_specs=(VM, VM),
        scratch_shapes=[
            pltpu.VMEM((9, 8, 128), jnp.float32), pltpu.VMEM((9, 8, 128), jnp.float32),
            pltpu.VMEM((8, 128), jnp.float32), pltpu.VMEM((9, 8, 128), jnp.float32),
            pltpu.SemaphoreType.DMA((16,)), pltpu.SemaphoreType.DMA((16,)),
        ],
        name="update",
        compiler_params=pltpu.CompilerParams(collective_id=1, has_side_effects=True),
    )(sums, motion)


def shards(
    eps_field, charge, potential_start, colloid_vel, colloid_spin, link_dir, link_colloid, link_site, link_depth,
    link_pop, link_rb,
):
    flat = lambda a: a.reshape(LINKS // 128, 128)
    motion = jnp.pad(jnp.concatenate([colloid_vel, colloid_spin], axis=0), ((0, 2), (0, 128 - NC_DEV)))
    potential, q, table = relax(eps_field, charge, potential_start, motion)
    row = link_depth.reshape(-1) * TX + (link_site.reshape(-1) >> 7)
    rb = link_rb.reshape(3, LINKS // 128, 128)
    slot, sums = link_sums(
        row, flat(link_site), flat(link_dir), flat(link_colloid), flat(link_pop), rb, q.reshape(NZ * TX, TY), table
    )
    report, table = update(sums, motion)
    link_out = reflect(flat(link_dir), slot, flat(link_pop), rb, table).reshape(link_pop.shape)
    return potential, report[0:6, 0:NC_DEV], link_out


def solution(mesh):
    tile = P(None, "gx", "gy")
    owned = P(None, ("gx", "gy"))
    link = P("gx", "gy", None)
    return jax.shard_map(
        shards,
        mesh=mesh,
        in_specs=(tile, tile, tile, owned, owned, link, link, link, link, link, P(None, "gx", "gy", None)),
        out_specs=(tile, owned, link),
        check_vma=False,
    )
```

```python
import math

import jax
import jax.numpy as jnp
import numpy as np
from jax import lax
from jax.experimental import pallas as pl
from jax.experimental.pallas import tpu as pltpu
from jax.sharding import PartitionSpec as P

TILES_X, TILES_Y = 8, 16
NC_DEV = 32
LINKS = 32768
RADIUS = 8
SWEEPS = 6
OVER_RELAX = 1.6
NZ, TX, TY = 48, 64, 128
HALF = NZ // 2
GROUPS = HALF // 8
ROWS = 96
TOP = 16
UNROLL = 8
WU = 4


def beside():
    x, y = lax.axis_index("gx"), lax.axis_index("gy")
    for t in range(9):
        if t != 4:
            yield t, (lax.rem(x + t // 3 - 1 + TILES_X, TILES_X), lax.rem(y + t % 3 - 1 + TILES_Y, TILES_Y))


def greet():
    barrier = pltpu.get_barrier_semaphore()
    for _, device in beside():
        pl.semaphore_signal(barrier, inc=1, device_id=device, device_id_type=pl.DeviceIdType.MESH)
    return lambda: pl.semaphore_wait(barrier, 8)


class Mail:
    def __init__(self, send_sem, recv_sem):
        self.sems, self.count, self.copies, self.device = (send_sem, recv_sem), 0, [], dict(beside())

    def send(self, t, source, target):
        copy = pltpu.make_async_remote_copy(
            src_ref=source, dst_ref=target, send_sem=self.sems[0].at[self.count], recv_sem=self.sems[1].at[self.count],
            device_id=self.device[t], device_id_type=pl.DeviceIdType.MESH,
        )
        copy.start()
        self.count += 1
        self.copies.append(copy)

    def wait(self):
        for copy in self.copies:
            copy.wait()
        self.copies = []


def write_table(table_ref, block):
    for tile in range(3):
        total = jnp.zeros((8, 128), jnp.float32)
        for i in range(4):
            if 4 * tile + i < 9:
                value = block(4 * tile + i)
                total = total + (pltpu.roll(value, NC_DEV * i, 1) if i else value)
        table_ref[:, 128 * tile:128 * tile + 128] = total


def relax_kernel(
    eps_ref, charge_ref, phi_ref, motion_ref, pot_ref, q_ref, table_ref,
    p_refs, e_refs, ps_refs, es_refs, gs_refs, seam_refs, c_refs, coef_refs, cs_refs, coefs_refs,
    to_low, to_high, from_low, from_high, x_eps, x_charge, x_phi, to2_low, to2_high, from2_low, from2_high, x2_refs,
    got_ref, send_sem, recv_sem,
):
    sub = lax.broadcasted_iota(jnp.int32, (8, 128), 0)
    lane = lax.broadcasted_iota(jnp.int32, (8, 128), 1)
    even = (sub + lane) % 2 == 0
    odd = ~even
    first = lane % 16 < 8
    slot = lane // 16
    zero = jnp.zeros((8, 128), jnp.float32)
    blocks = range(8, ROWS - 8, 8)
    greeted = greet()
    mail = Mail(send_sem, recv_sem)

    def pack(plane, low_ref, high_ref, at):
        def group(g, _):
            for r in range(0, TX, 16):
                low, high = [zero, zero], [zero, zero]
                for k in range(16):
                    rows = plane(g, k, r)
                    for h in (0, 1):
                        value = rows[h]
                        here = lane // 8 == k
                        low[h] = jnp.where(here, pltpu.roll(value, 8 * k, 1) if k else value, low[h])
                        high[h] = jnp.where(here, pltpu.roll(value, 8 * (k + 1), 1) if k < 15 else value, high[h])
                for h in (0, 1):
                    low_ref[at + g, r + 8 * h:r + 8 * h + 8, :] = low[h]
                    high_ref[at + g, r + 8 * h:r + 8 * h + 8, :] = high[h]
            return 0
        lax.fori_loop(0, GROUPS, group, 0)

    def send_sides(low_ref, high_ref, dst_low, dst_high, at):
        span = pl.ds(at, GROUPS)
        for t, rows, target in ((3, (0, TX), 8), (0, (0, 8), 72), (6, (TX - 8, 8), 0)):
            mail.send(t, low_ref.at[span, pl.ds(*rows), :], dst_high.at[span, pl.ds(target, rows[1]), :])
            mail.send(t + 2, high_ref.at[span, pl.ds(*rows), :], dst_low.at[span, pl.ds(target, rows[1]), :])

    def natural(ref):
        def plane(g, k, r):
            value = ref[16 * g + k, r:r + 16, :].astype(jnp.float32)
            return value[0:8], value[8:16]
        return plane

    def send_rows(ref, target, rows):
        mail.send(1, ref.at[:, pl.ds(0, rows), :], target.at[1])
        mail.send(7, ref.at[:, pl.ds(TX - rows, rows), :], target.at[0])

    pack(natural(eps_ref), to_low, to_high, GROUPS)
    greeted()
    send_sides(to_low, to_high, from_low, from_high, GROUPS)
    send_rows(eps_ref, x_eps, 16)
    send_rows(charge_ref, x_charge, 8)
    pack(natural(charge_ref), to_low, to_high, 2 * GROUPS)
    send_sides(to_low, to_high, from_low, from_high, 2 * GROUPS)
    early, mail.copies = mail.copies, []
    send_rows(phi_ref, x_phi, 8)
    pack(natural(phi_ref), to_low, to_high, 0)
    send_sides(to_low, to_high, from_low, from_high, 0)
    for t, _ in beside():
        mail.send(t, motion_ref, got_ref.at[8 - t])

    def clear(m, _):
        for ref in (*p_refs, *e_refs):
            for g in (0, ROWS - 8):
                ref[m, g:g + 8, :] = zero
        return 0
    lax.fori_loop(0, HALF + 2, clear, 0)
    for ref in p_refs:
        for g in blocks:
            ref[0, g:g + 8, :] = zero
            ref[HALF + 1, g:g + 8, :] = zero
    for ref in (*ps_refs, *es_refs):
        for g in (0, ROWS - 8):
            for m in range(GROUPS + 2):
                ref[m, g:g + 8, :] = zero
    for ref in ps_refs:
        for g in blocks:
            ref[0, g:g + 8, :] = zero
            ref[GROUPS + 1, g:g + 8, :] = zero

    def two(refs, m, rows, a, b):
        refs[0][m, rows, :] = jnp.where(even, a, b)
        refs[1][m, rows, :] = jnp.where(even, b, a)

    def compact(m, _):
        for r in range(0, TX, 16):
            a = eps_ref[2 * m, r:r + 16, :].astype(jnp.float32)
            b = eps_ref[2 * m + 1, r:r + 16, :].astype(jnp.float32)
            for h in (0, 8):
                two(e_refs, m + 1, slice(TOP + r + h, TOP + r + h + 8), a[h:h + 8], b[h:h + 8])
        for r in range(0, TX, 8):
            two(p_refs, m + 1, slice(TOP + r, TOP + r + 8), phi_ref[2 * m, r:r + 8, :], phi_ref[2 * m + 1, r:r + 8, :])
        return 0
    lax.fori_loop(0, HALF, compact, 0)

    for copy in early:
        copy.wait()

    def edges(m, _):
        for side, g in ((0, 8), (1, TOP + TX)):
            rows = slice(8, 16) if side == 0 else slice(0, 8)
            a = x_eps[side, 2 * m].astype(jnp.float32)[rows]
            b = x_eps[side, 2 * m + 1].astype(jnp.float32)[rows]
            two(e_refs, m + 1, slice(g, g + 8), a, b)
        return 0
    lax.fori_loop(0, HALF, edges, 0)

    def unpacked(low_ref, high_ref, at, r):
        low, high = low_ref[at, r:r + 8, :], high_ref[at, r:r + 8, :]
        return jnp.where(first, low, pltpu.roll(high, 8, 1)), jnp.where(first, pltpu.roll(low, 120, 1), high)

    def strips(g, _):
        for r in range(0, TX + 16, 8):
            rows = slice(8 + r, 16 + r)
            two(es_refs, g + 1, rows, *unpacked(from_low, from_high, GROUPS + g, r))
            two(gs_refs, g, slice(r, r + 8), *unpacked(from_low, from_high, 2 * GROUPS + g, r))
        return 0
    lax.fori_loop(0, GROUPS, strips, 0)
    for g in blocks:
        rows = slice(g, g + 8)
        for c in (0, 1):
            e_refs[1 - c][0, rows, :] = e_refs[c][1, rows, :]
            e_refs[1 - c][HALF + 1, rows, :] = e_refs[c][HALF, rows, :]
            es_refs[1 - c][0, rows, :] = pltpu.roll(es_refs[c][1, rows, :], 112, 1)
            es_refs[1 - c][GROUPS + 1, rows, :] = pltpu.roll(es_refs[c][GROUPS, rows, :], 16, 1)

    def turn(seam_ref, n, g, value):
        for k in range(8):
            seam_ref[8 * n + k, g - 8:g, :] = pltpu.roll(value, 120 - 16 * k, 1)

    def turn_all(strip_refs):
        def one(n, _):
            for g in blocks:
                for c in (0, 1):
                    turn(seam_refs[c], n, g, strip_refs[c][n + 1, g:g + 8, :])
            return 0
        lax.fori_loop(0, GROUPS, one, 0)

    def main_sides(ref, seam_ref, m, g, low):
        rows = slice(g, g + 8)
        here = ref[m + 1, rows, :]
        seam = seam_ref[m, g - 8:g, :]
        return (
            here,
            jnp.where(low, ref[m, rows, :], ref[m + 2, rows, :]),
            ref[m + 1, g - 1:g + 7, :],
            ref[m + 1, g + 1:g + 9, :],
            pltpu.roll(jnp.where(lane == 127, seam, here), 1, 1),
            pltpu.roll(jnp.where(lane == 0, seam, here), 127, 1),
        )

    def strip_sides(ref, strip_ref, n, g, low):
        rows = slice(g, g + 8)
        here = strip_ref[n + 1, rows, :]
        seam = zero
        for k in range(8):
            seam = jnp.where(slot == k, pltpu.roll(ref[8 * n + k + 1, rows, :], 16 * k + 8, 1), seam)
        below = pltpu.roll(jnp.where(slot == 7, strip_ref[n, rows, :], here), 16, 1)
        above = pltpu.roll(jnp.where(slot == 0, strip_ref[n + 2, rows, :], here), 112, 1)
        return (
            here,
            jnp.where(low, below, above),
            strip_ref[n + 1, g - 1:g + 7, :],
            strip_ref[n + 1, g + 1:g + 9, :],
            pltpu.roll(jnp.where(lane % 16 == 7, seam, here), 1, 1),
            pltpu.roll(jnp.where(lane % 16 == 8, seam, here), 127, 1),
        )

    turn_all(es_refs)

    def weights(centre, sides, charge, c_ref, coef_ref, m, g):
        faces = [0.5 * (centre + side) for side in sides]
        total = faces[0]
        for face in faces[1:]:
            total = total + face
        scale = OVER_RELAX / total
        c_ref[m, g - 8:g, :] = scale * charge
        for i in range(6):
            coef_ref[i, m, g - 8:g, :] = scale * faces[i]

    for c in (0, 1):
        low = odd if c else even

        def main_weights(n, _):
            for k in range(WU):
                m = WU * n + k
                for g in blocks:
                    if g == 8:
                        a, b = x_charge[0, 2 * m], x_charge[0, 2 * m + 1]
                    elif g == TOP + TX:
                        a, b = x_charge[1, 2 * m], x_charge[1, 2 * m + 1]
                    else:
                        a, b = charge_ref[2 * m, g - TOP:g - TOP + 8, :], charge_ref[2 * m + 1, g - TOP:g - TOP + 8, :]
                    sides = main_sides(e_refs[1 - c], seam_refs[1 - c], m, g, low)
                    weights(e_refs[c][m + 1, g:g + 8, :], sides, jnp.where(low, a, b), c_refs[c], coef_refs[c], m, g)
            return 0
        lax.fori_loop(0, HALF // WU, main_weights, 0)

        def strip_weights(n, _):
            for g in blocks:
                sides = strip_sides(e_refs[1 - c], es_refs[1 - c], n, g, low)
                weights(es_refs[c][n + 1, g:g + 8, :], sides, gs_refs[c][n, g - 8:g, :], cs_refs[c], coefs_refs[c], n, g)
            return 0
        lax.fori_loop(0, GROUPS, strip_weights, 0)

    def updated(own, sides, c_ref, coef_ref, m, g):
        parts = [coef_ref[i, m, g - 8:g, :] * side for i, side in enumerate(sides)]
        first_part = c_ref[m, g - 8:g, :] - (OVER_RELAX - 1.0) * own
        return ((first_part + parts[0]) + (parts[1] + parts[2])) + (parts[3] + (parts[4] + parts[5]))

    def step(c, inner):
        low = odd if c else even

        def main_step(n, _):
            for k in range(UNROLL):
                m = UNROLL * n + k
                chosen = blocks[1:-1] if inner else blocks
                values = []
                for g in chosen:
                    sides = main_sides(p_refs[1 - c], seam_refs[1 - c], m, g, low)
                    values.append(updated(p_refs[c][m + 1, g:g + 8, :], sides, c_refs[c], coef_refs[c], m, g))
                for g, value in zip(chosen, values):
                    p_refs[c][m + 1, g:g + 8, :] = value
            return 0
        lax.fori_loop(0, HALF // UNROLL, main_step, 0)
        if inner:
            return

        def strip_step(n, _):
            for g in blocks:
                sides = strip_sides(p_refs[1 - c], ps_refs[1 - c], n, g, low)
                value = updated(ps_refs[c][n + 1, g:g + 8, :], sides, cs_refs[c], coefs_refs[c], n, g)
                ps_refs[c][n + 1, g:g + 8, :] = value
                turn(seam_refs[c], n, g, value)
            return 0
        lax.fori_loop(0, GROUPS, strip_step, 0)

    mail.wait()
    write_table(table_ref, lambda t: motion_ref[...] if t == 4 else got_ref[t])

    def edges1(m, _):
        for side, g in ((0, 8), (1, TOP + TX)):
            two(p_refs, m + 1, slice(g, g + 8), x_phi[side, 2 * m], x_phi[side, 2 * m + 1])
        return 0
    lax.fori_loop(0, HALF, edges1, 0)

    def strips1(g, _):
        for r in range(0, TX + 16, 8):
            two(ps_refs, g + 1, slice(8 + r, 16 + r), *unpacked(from_low, from_high, g, r))
        return 0
    lax.fori_loop(0, GROUPS, strips1, 0)
    turn_all(ps_refs)

    def three(i, _):
        step(0, False)
        step(1, False)
        return 0
    lax.fori_loop(0, 3, three, 0)
    step(0, False)
    step(1, True)

    def coloured(g, k, r):
        value = p_refs[k % 2][8 * g + k // 2 + 1, TOP + r:TOP + r + 16, :]
        return value[0:8], value[8:16]

    for c in (0, 1):
        mail.send(1, p_refs[c].at[pl.ds(1, HALF), pl.ds(TOP, 8), :], x2_refs[c].at[1])
        mail.send(7, p_refs[c].at[pl.ds(1, HALF), pl.ds(TOP + TX - 8, 8), :], x2_refs[c].at[0])
    pack(coloured, to2_low, to2_high, 0)
    send_sides(to2_low, to2_high, from2_low, from2_high, 0)
    mail.wait()

    def edges2(m, _):
        for c in (0, 1):
            p_refs[c][m + 1, 8:16, :] = x2_refs[c][0, m]
            p_refs[c][m + 1, TOP + TX:TOP + TX + 8, :] = x2_refs[c][1, m]
        return 0
    lax.fori_loop(0, HALF, edges2, 0)

    def strips2(g, _):
        for r in range(0, TX + 16, 8):
            a, b = unpacked(from2_low, from2_high, g, r)
            ps_refs[0][g + 1, 8 + r:16 + r, :] = a
            ps_refs[1][g + 1, 8 + r:16 + r, :] = b
        return 0
    lax.fori_loop(0, GROUPS, strips2, 0)
    turn_all(ps_refs)
    step(0, False)
    step(1, False)
    step(0, False)
    step(1, True)

    def out(m, _):
        for g in range(0, TX, 8):
            a, b = [ref[m + 1, TOP + g:TOP + g + 8, :] for ref in p_refs]
            ea, eb = [ref[m + 1, TOP + g:TOP + g + 8, :] for ref in e_refs]
            lo, hi = jnp.where(even, a, b), jnp.where(even, b, a)
            elo, ehi = jnp.where(even, ea, eb), jnp.where(even, eb, ea)
            pot_ref[2 * m, g:g + 8, :] = lo
            pot_ref[2 * m + 1, g:g + 8, :] = hi
            q_ref[2 * m, g:g + 8, :] = 0.5 * elo * lo * lo
            q_ref[2 * m + 1, g:g + 8, :] = 0.5 * ehi * hi * hi
        return 0
    lax.fori_loop(0, HALF, out, 0)


def relax(eps, charge, phi, motion):
    vm = lambda *s: pltpu.VMEM(s, jnp.float32)
    spec = pl.BlockSpec(memory_space=pltpu.VMEM)
    return pl.pallas_call(
        relax_kernel,
        out_shape=(
            jax.ShapeDtypeStruct((NZ, TX, TY), jnp.float32),
            jax.ShapeDtypeStruct((NZ, TX, TY), jnp.float32),
            jax.ShapeDtypeStruct((8, SLOTS_PAD), jnp.float32),
        ),
        in_specs=[spec] * 4,
        out_specs=(spec,) * 3,
        scratch_shapes=[
            [vm(HALF + 2, ROWS, 128)] * 2,
            [vm(HALF + 2, ROWS, 128)] * 2,
            [vm(GROUPS + 2, ROWS, 128)] * 2,
            [vm(GROUPS + 2, ROWS, 128)] * 2,
            [vm(GROUPS, ROWS - 16, 128)] * 2,
            [vm(HALF, ROWS - 16, 128)] * 2,
            [vm(HALF, ROWS - 16, 128)] * 2,
            [vm(6, HALF, ROWS - 16, 128)] * 2,
            [vm(GROUPS, ROWS - 16, 128)] * 2,
            [vm(6, GROUPS, ROWS - 16, 128)] * 2,
            vm(3 * GROUPS, TX, 128), vm(3 * GROUPS, TX, 128),
            vm(3 * GROUPS, TX + 16, 128), vm(3 * GROUPS, TX + 16, 128),
            pltpu.VMEM((2, NZ, 16, 128), jnp.bfloat16), vm(2, NZ, 8, 128), vm(2, NZ, 8, 128),
            vm(GROUPS, TX, 128), vm(GROUPS, TX, 128),
            vm(GROUPS, TX + 16, 128), vm(GROUPS, TX + 16, 128),
            [vm(2, HALF, 8, 128)] * 2,
            vm(9, 8, 128),
            pltpu.SemaphoreType.DMA((42,)), pltpu.SemaphoreType.DMA((42,)),
        ],
        name="relax",
        compiler_params=pltpu.CompilerParams(vmem_limit_bytes=58 * 2**20, collective_id=0, has_side_effects=True),
    )(eps, charge, phi, motion)


CHUNK = 4096
SLOTS = 9 * NC_DEV
SLOTS_PAD = 384
VELOCITY = np.array(
    [[1, 0, 0], [-1, 0, 0], [0, 1, 0], [0, -1, 0], [0, 0, 1], [0, 0, -1], [1, 1, 0], [1, -1, 0], [-1, 1, 0],
     [-1, -1, 0], [1, 0, 1], [1, 0, -1], [-1, 0, 1], [-1, 0, -1], [0, 1, 1], [0, 1, -1], [0, -1, 1], [0, -1, -1]],
    dtype=np.float32,
).T
WEIGHT = np.array([1.0 / 18.0] * 6 + [1.0 / 36.0] * 12, dtype=np.float32)


def lattice_table():
    rows = np.zeros((4, 8, 128), np.float32)
    rows[0:3, :, 0:18] = VELOCITY[:, None, :]
    rows[3, :, 0:18] = WEIGHT[None, :]
    return jnp.asarray(rows.reshape(32, 128))


def split(values):
    high = values.astype(jnp.bfloat16).astype(jnp.float32)
    return jnp.concatenate([high, values - high], axis=0).astype(jnp.bfloat16)


def cross(first, second):
    return (
        first[1] * second[2] - first[2] * second[1],
        first[2] * second[0] - first[0] * second[2],
        first[0] * second[1] - first[1] * second[0],
    )


def decode(lat_ref, direction):
    return [jnp.take_along_axis(lat_ref[8 * i:8 * i + 8, :], direction, axis=1) for i in range(4)]


def motions_at(table, slot_ref, base, onehot_ref, at_ref):
    ids = lax.broadcasted_iota(jnp.int32, (SLOTS, 128), 0)
    for pair in range(4):
        halves = [ids == slot_ref[pl.ds(base + 2 * pair + h, 1), :] for h in (0, 1)]
        onehot = jnp.concatenate([half.astype(jnp.float32) for half in halves], axis=1).astype(jnp.bfloat16)
        if onehot_ref is not None:
            onehot_ref[:, 256 * pair:256 * pair + 256] = onehot
        found = jnp.dot(table, onehot, preferred_element_type=jnp.float32)
        found = found[0:8] + found[8:16]
        at_ref[16 * pair:16 * pair + 8, :] = found[:, 0:128]
        at_ref[16 * pair + 8:16 * pair + 16, :] = found[:, 128:256]
    return [at_ref[pl.ds(i, 8, stride=8), :] for i in range(6)]


def along_link(motion, velocity, offsets):
    spin = cross(motion[3:6], offsets)
    return sum(velocity[i] * (motion[i] + spin[i]) for i in range(3))


def links_kernel(row_ref, site_ref, dir_ref, ids_ref, pop_ref, rb_ref, q_ref, table_ref, lat_ref, slot_ref, sums_ref, onehot_ref, at_ref, term_ref):
    home_x = lax.axis_index("gx")
    home_y = lax.axis_index("gy")
    lane = lax.broadcasted_iota(jnp.int32, (8, 128), 1)
    sub = lax.broadcasted_iota(jnp.int32, (8, 128), 0)

    @pl.when(pl.program_id(0) == 0)
    def _():
        sums_ref[...] = jnp.zeros_like(sums_ref)
        term_ref[...] = jnp.zeros_like(term_ref)

    table = split(table_ref[...])[:, 0:SLOTS]

    def group(b, _):
        base = pl.multiple_of(b * 8, 8)
        rows = pl.ds(base, 8)
        ids = ids_ref[rows, :]
        owner = ids >> 5
        near_x = ((owner >> 4) - home_x + 1) & (TILES_X - 1)
        near_y = ((owner & (TILES_Y - 1)) - home_y + 1) & (TILES_Y - 1)
        slot_ref[rows, :] = jnp.where(ids >= 0, (near_x * 3 + near_y) * NC_DEV + (ids & (NC_DEV - 1)), -1)
        column = site_ref[rows, :] & 127
        pressure = jnp.zeros((8, 128), jnp.float32)
        for j in range(128):
            at = lambda s: jnp.broadcast_to(q_ref[pl.ds(row_ref[b * 1024 + s * 128 + j], 1), :], (8, 128))
            picked = at(0)
            for s in range(1, 8):
                picked = jnp.where(sub == s, at(s), picked)
            pressure = jnp.where(lane == j, jnp.take_along_axis(picked, column, axis=1), pressure)
        *velocity, weight = decode(lat_ref, dir_ref[rows, :])
        offsets = [rb_ref[i, rows, :] for i in range(3)]
        motion = motions_at(table, slot_ref, base, onehot_ref, at_ref)
        along = along_link(motion, velocity, offsets)
        transfer = 2.0 * pop_ref[rows, :] - 6.0 * weight * along + weight * pressure
        transfer = jnp.where(ids >= 0, transfer, 0.0)
        force = [v * transfer for v in velocity]
        for i, term in enumerate((*force, *cross(offsets, force))):
            term_ref[pl.ds(i, 8, stride=8), :] = term
        total = jnp.zeros((16, SLOTS), jnp.float32)
        for pair in range(4):
            terms = jnp.concatenate([term_ref[16 * pair:16 * pair + 8, :], term_ref[16 * pair + 8:16 * pair + 16, :]], axis=1)
            total = total + lax.dot_general(
                split(terms), onehot_ref[:, 256 * pair:256 * pair + 256], (((1,), (1,)), ((), ())),
                preferred_element_type=jnp.float32,
            )
        sums_ref[:, 0:SLOTS] += total[0:8] + total[8:16]
        return 0

    lax.fori_loop(0, CHUNK // 1024, group, 0)


def link_spec(lead=None):
    if lead is None:
        return pl.BlockSpec((CHUNK // 128, 128), lambda i: (i, 0))
    return pl.BlockSpec((lead, CHUNK // 128, 128), lambda i: (0, i, 0))


def whole(*shape):
    return pl.BlockSpec(shape, lambda i: (0,) * len(shape))


def link_sums(row, site, direction, ids, pop, rb, q, table):
    return pl.pallas_call(
        links_kernel,
        grid=(LINKS // CHUNK,),
        in_specs=[
            pl.BlockSpec((CHUNK,), lambda i: (i,), memory_space=pltpu.SMEM),
            link_spec(), link_spec(), link_spec(), link_spec(), link_spec(3),
            whole(NZ * TX, TY), whole(8, SLOTS_PAD), whole(32, 128),
        ],
        out_specs=(link_spec(), whole(8, SLOTS_PAD)),
        out_shape=(jax.ShapeDtypeStruct((LINKS // 128, 128), jnp.int32), jax.ShapeDtypeStruct((8, SLOTS_PAD), jnp.float32)),
        scratch_shapes=[pltpu.VMEM((SLOTS, 1024), jnp.bfloat16), pltpu.VMEM((64, 128), jnp.float32), pltpu.VMEM((64, 128), jnp.float32)],
        name="link_sums",
        compiler_params=pltpu.CompilerParams(vmem_limit_bytes=40 * 2**20),
    )(row, site, direction, ids, pop, rb, q, table, lattice_table())


def reflect_kernel(dir_ref, slot_ref, pop_ref, rb_ref, table_ref, lat_ref, out_ref, at_ref):
    table = split(table_ref[...])[:, 0:SLOTS]

    def group(b, _):
        base = pl.multiple_of(b * 8, 8)
        rows = pl.ds(base, 8)
        *velocity, weight = decode(lat_ref, dir_ref[rows, :])
        offsets = [rb_ref[i, rows, :] for i in range(3)]
        motion = motions_at(table, slot_ref, base, None, at_ref)
        along = jnp.where(slot_ref[rows, :] >= 0, along_link(motion, velocity, offsets), 0.0)
        out_ref[rows, :] = pop_ref[rows, :] - 6.0 * weight * along
        return 0

    lax.fori_loop(0, CHUNK // 1024, group, 0)


def reflect(direction, slot, pop, rb, table):
    return pl.pallas_call(
        reflect_kernel,
        grid=(LINKS // CHUNK,),
        in_specs=[link_spec(), link_spec(), link_spec(), link_spec(3), whole(8, SLOTS_PAD), whole(32, 128)],
        out_specs=link_spec(),
        out_shape=jax.ShapeDtypeStruct((LINKS // 128, 128), jnp.float32),
        scratch_shapes=[pltpu.VMEM((64, 128), jnp.float32)],
        name="reflect",
        compiler_params=pltpu.CompilerParams(vmem_limit_bytes=40 * 2**20),
    )(direction, slot, pop, rb, table, lattice_table())


def update_kernel(sums_ref, motion_ref, report_ref, table_ref, part_ref, got_ref, new_ref, back_ref, send_sem, recv_sem):
    greeted = greet()
    mail = Mail(send_sem, recv_sem)
    lane = lax.broadcasted_iota(jnp.int32, (8, 128), 1)
    row = lax.broadcasted_iota(jnp.int32, (8, 128), 0)
    for t in range(9):
        value = sums_ref[:, 128 * (t // 4):128 * (t // 4) + 128]
        if t % 4:
            value = pltpu.roll(value, 128 - NC_DEV * (t % 4), 1)
        part_ref[t] = jnp.where(lane < NC_DEV, value, 0.0)
    greeted()
    for t, _ in beside():
        mail.send(t, part_ref.at[t], got_ref.at[8 - t])
    total = part_ref[4]
    mail.wait()
    for t in range(9):
        if t != 4:
            total = total + got_ref[t]
    mass = 4.0 / 3.0 * math.pi * RADIUS**3
    inertia = 0.4 * mass * RADIUS**2
    report_ref[...] = jnp.where(row < 3, total, total / RADIUS)
    new_ref[...] = motion_ref[...] + jnp.where(row < 3, total / mass, total / inertia)
    for t, _ in beside():
        mail.send(t, new_ref, back_ref.at[8 - t])
    mail.wait()
    write_table(table_ref, lambda t: new_ref[...] if t == 4 else back_ref[t])


VM = pl.BlockSpec(memory_space=pltpu.VMEM)


def update(sums, motion):
    return pl.pallas_call(
        update_kernel,
        out_shape=(jax.ShapeDtypeStruct((8, 128), jnp.float32), jax.ShapeDtypeStruct((8, SLOTS_PAD), jnp.float32)),
        in_specs=[VM, VM],
        out_specs=(VM, VM),
        scratch_shapes=[
            pltpu.VMEM((9, 8, 128), jnp.float32), pltpu.VMEM((9, 8, 128), jnp.float32),
            pltpu.VMEM((8, 128), jnp.float32), pltpu.VMEM((9, 8, 128), jnp.float32),
            pltpu.SemaphoreType.DMA((16,)), pltpu.SemaphoreType.DMA((16,)),
        ],
        name="update",
        compiler_params=pltpu.CompilerParams(collective_id=1, has_side_effects=True),
    )(sums, motion)


def shards(
    eps_field, charge, potential_start, colloid_vel, colloid_spin, link_dir, link_colloid, link_site, link_depth,
    link_pop, link_rb,
):
    flat = lambda a: a.reshape(LINKS // 128, 128)
    motion = jnp.pad(jnp.concatenate([colloid_vel, colloid_spin], axis=0), ((0, 2), (0, 128 - NC_DEV)))
    potential, q, table = relax(eps_field, charge, potential_start, motion)
    row = link_depth.reshape(-1) * TX + (link_site.reshape(-1) >> 7)
    rb = link_rb.reshape(3, LINKS // 128, 128)
    slot, sums = link_sums(
        row, flat(link_site), flat(link_dir), flat(link_colloid), flat(link_pop), rb, q.reshape(NZ * TX, TY), table
    )
    report, table = update(sums, motion)
    link_out = reflect(flat(link_dir), slot, flat(link_pop), rb, table).reshape(link_pop.shape)
    return potential, report[0:6, 0:NC_DEV], link_out


def solution(mesh):
    tile = P(None, "gx", "gy")
    owned = P(None, ("gx", "gy"))
    link = P("gx", "gy", None)
    return jax.shard_map(
        shards,
        mesh=mesh,
        in_specs=(tile, tile, tile, owned, owned, link, link, link, link, link, P(None, "gx", "gy", None)),
        out_specs=(tile, owned, link),
        check_vma=False,
    )
```

```python
import math

import jax
import jax.numpy as jnp
import numpy as np
from jax import lax
from jax.experimental import pallas as pl
from jax.experimental.pallas import tpu as pltpu
from jax.sharding import PartitionSpec as P

TILES_X, TILES_Y = 8, 16
NC_DEV = 32
LINKS = 32768
RADIUS = 8
SWEEPS = 6
OVER_RELAX = 1.6
NZ, TX, TY = 48, 64, 128
HALF = NZ // 2
GROUPS = HALF // 8
ROWS = 96
TOP = 16
UNROLL = 8
WU = 4


def beside():
    x, y = lax.axis_index("gx"), lax.axis_index("gy")
    for t in range(9):
        if t != 4:
            yield t, (lax.rem(x + t // 3 - 1 + TILES_X, TILES_X), lax.rem(y + t % 3 - 1 + TILES_Y, TILES_Y))


def greet():
    barrier = pltpu.get_barrier_semaphore()
    for _, device in beside():
        pl.semaphore_signal(barrier, inc=1, device_id=device, device_id_type=pl.DeviceIdType.MESH)
    return lambda: pl.semaphore_wait(barrier, 8)


class Mail:
    def __init__(self, send_sem, recv_sem):
        self.sems, self.count, self.copies, self.device = (send_sem, recv_sem), 0, [], dict(beside())

    def send(self, t, source, target):
        copy = pltpu.make_async_remote_copy(
            src_ref=source, dst_ref=target, send_sem=self.sems[0].at[self.count], recv_sem=self.sems[1].at[self.count],
            device_id=self.device[t], device_id_type=pl.DeviceIdType.MESH,
        )
        copy.start()
        self.count += 1
        self.copies.append(copy)

    def wait(self):
        for copy in self.copies:
            copy.wait()
        self.copies = []


def write_table(table_ref, block):
    for tile in range(3):
        total = jnp.zeros((8, 128), jnp.float32)
        for i in range(4):
            if 4 * tile + i < 9:
                value = block(4 * tile + i)
                total = total + (pltpu.roll(value, NC_DEV * i, 1) if i else value)
        table_ref[:, 128 * tile:128 * tile + 128] = total


def relax_kernel(
    eps_ref, charge_ref, phi_ref, motion_ref, pot_ref, q_ref, table_ref,
    p_refs, e_refs, ps_refs, es_refs, gs_refs, seam_refs, c_refs, coef_refs, cs_refs, coefs_refs,
    to_low, to_high, from_low, from_high, x_eps, x_charge, x_phi, to2_low, to2_high, from2_low, from2_high, x2_refs,
    got_ref, send_sem, recv_sem,
):
    sub = lax.broadcasted_iota(jnp.int32, (8, 128), 0)
    lane = lax.broadcasted_iota(jnp.int32, (8, 128), 1)
    even = (sub + lane) % 2 == 0
    odd = ~even
    first = lane % 16 < 8
    slot = lane // 16
    zero = jnp.zeros((8, 128), jnp.float32)
    blocks = range(8, ROWS - 8, 8)
    greeted = greet()
    mail = Mail(send_sem, recv_sem)

    def pack(plane, low_ref, high_ref, at):
        def group(g, _):
            for r in range(0, TX, 16):
                low, high = [zero, zero], [zero, zero]
                for k in range(16):
                    rows = plane(g, k, r)
                    for h in (0, 1):
                        value = rows[h]
                        here = lane // 8 == k
                        low[h] = jnp.where(here, pltpu.roll(value, 8 * k, 1) if k else value, low[h])
                        high[h] = jnp.where(here, pltpu.roll(value, 8 * (k + 1), 1) if k < 15 else value, high[h])
                for h in (0, 1):
                    low_ref[at + g, r + 8 * h:r + 8 * h + 8, :] = low[h]
                    high_ref[at + g, r + 8 * h:r + 8 * h + 8, :] = high[h]
            return 0
        lax.fori_loop(0, GROUPS, group, 0)

    def send_sides(low_ref, high_ref, dst_low, dst_high, at):
        span = pl.ds(at, GROUPS)
        for t, rows, target in ((3, (0, TX), 8), (0, (0, 8), 72), (6, (TX - 8, 8), 0)):
            mail.send(t, low_ref.at[span, pl.ds(*rows), :], dst_high.at[span, pl.ds(target, rows[1]), :])
            mail.send(t + 2, high_ref.at[span, pl.ds(*rows), :], dst_low.at[span, pl.ds(target, rows[1]), :])

    def natural(ref):
        def plane(g, k, r):
            value = ref[16 * g + k, r:r + 16, :].astype(jnp.float32)
            return value[0:8], value[8:16]
        return plane

    def send_rows(ref, target, rows):
        mail.send(1, ref.at[:, pl.ds(0, rows), :], target.at[1])
        mail.send(7, ref.at[:, pl.ds(TX - rows, rows), :], target.at[0])

    pack(natural(eps_ref), to_low, to_high, GROUPS)
    greeted()
    send_sides(to_low, to_high, from_low, from_high, GROUPS)
    send_rows(eps_ref, x_eps, 16)
    send_rows(charge_ref, x_charge, 8)
    pack(natural(charge_ref), to_low, to_high, 2 * GROUPS)
    send_sides(to_low, to_high, from_low, from_high, 2 * GROUPS)
    early, mail.copies = mail.copies, []
    send_rows(phi_ref, x_phi, 8)
    pack(natural(phi_ref), to_low, to_high, 0)
    send_sides(to_low, to_high, from_low, from_high, 0)
    for t, _ in beside():
        mail.send(t, motion_ref, got_ref.at[8 - t])

    def clear(m, _):
        for ref in (*p_refs, *e_refs):
            for g in (0, ROWS - 8):
                ref[m, g:g + 8, :] = zero
        return 0
    lax.fori_loop(0, HALF + 2, clear, 0)
    for ref in p_refs:
        for g in blocks:
            ref[0, g:g + 8, :] = zero
            ref[HALF + 1, g:g + 8, :] = zero
    for ref in (*ps_refs, *es_refs):
        for g in (0, ROWS - 8):
            for m in range(GROUPS + 2):
                ref[m, g:g + 8, :] = zero
    for ref in ps_refs:
        for g in blocks:
            ref[0, g:g + 8, :] = zero
            ref[GROUPS + 1, g:g + 8, :] = zero

    def two(refs, m, rows, a, b):
        refs[0][m, rows, :] = jnp.where(even, a, b)
        refs[1][m, rows, :] = jnp.where(even, b, a)

    def compact(m, _):
        for r in range(0, TX, 16):
            a = eps_ref[2 * m, r:r + 16, :].astype(jnp.float32)
            b = eps_ref[2 * m + 1, r:r + 16, :].astype(jnp.float32)
            for h in (0, 8):
                two(e_refs, m + 1, slice(TOP + r + h, TOP + r + h + 8), a[h:h + 8], b[h:h + 8])
        for r in range(0, TX, 8):
            two(p_refs, m + 1, slice(TOP + r, TOP + r + 8), phi_ref[2 * m, r:r + 8, :], phi_ref[2 * m + 1, r:r + 8, :])
        return 0
    lax.fori_loop(0, HALF, compact, 0)

    for copy in early:
        copy.wait()

    def edges(m, _):
        for side, g in ((0, 8), (1, TOP + TX)):
            rows = slice(8, 16) if side == 0 else slice(0, 8)
            a = x_eps[side, 2 * m].astype(jnp.float32)[rows]
            b = x_eps[side, 2 * m + 1].astype(jnp.float32)[rows]
            two(e_refs, m + 1, slice(g, g + 8), a, b)
        return 0
    lax.fori_loop(0, HALF, edges, 0)

    def unpacked(low_ref, high_ref, at, r):
        low, high = low_ref[at, r:r + 8, :], high_ref[at, r:r + 8, :]
        return jnp.where(first, low, pltpu.roll(high, 8, 1)), jnp.where(first, pltpu.roll(low, 120, 1), high)

    def strips(g, _):
        for r in range(0, TX + 16, 8):
            rows = slice(8 + r, 16 + r)
            two(es_refs, g + 1, rows, *unpacked(from_low, from_high, GROUPS + g, r))
            two(gs_refs, g, slice(r, r + 8), *unpacked(from_low, from_high, 2 * GROUPS + g, r))
        return 0
    lax.fori_loop(0, GROUPS, strips, 0)
    for g in blocks:
        rows = slice(g, g + 8)
        for c in (0, 1):
            e_refs[1 - c][0, rows, :] = e_refs[c][1, rows, :]
            e_refs[1 - c][HALF + 1, rows, :] = e_refs[c][HALF, rows, :]
            es_refs[1 - c][0, rows, :] = pltpu.roll(es_refs[c][1, rows, :], 112, 1)
            es_refs[1 - c][GROUPS + 1, rows, :] = pltpu.roll(es_refs[c][GROUPS, rows, :], 16, 1)

    def turn(seam_ref, n, g, value):
        for k in range(8):
            seam_ref[8 * n + k, g - 8:g, :] = pltpu.roll(value, 120 - 16 * k, 1)

    def turn_all(strip_refs):
        def one(n, _):
            for g in blocks:
                for c in (0, 1):
                    turn(seam_refs[c], n, g, strip_refs[c][n + 1, g:g + 8, :])
            return 0
        lax.fori_loop(0, GROUPS, one, 0)

    def main_sides(ref, seam_ref, m, g, low):
        rows = slice(g, g + 8)
        here = ref[m + 1, rows, :]
        seam = seam_ref[m, g - 8:g, :]
        return (
            here,
            jnp.where(low, ref[m, rows, :], ref[m + 2, rows, :]),
            ref[m + 1, g - 1:g + 7, :],
            ref[m + 1, g + 1:g + 9, :],
            pltpu.roll(jnp.where(lane == 127, seam, here), 1, 1),
            pltpu.roll(jnp.where(lane == 0, seam, here), 127, 1),
        )

    def strip_sides(ref, strip_ref, n, g, low):
        rows = slice(g, g + 8)
        here = strip_ref[n + 1, rows, :]
        seam = zero
        for k in range(8):
            seam = jnp.where(slot == k, pltpu.roll(ref[8 * n + k + 1, rows, :], 16 * k + 8, 1), seam)
        below = pltpu.roll(jnp.where(slot == 7, strip_ref[n, rows, :], here), 16, 1)
        above = pltpu.roll(jnp.where(slot == 0, strip_ref[n + 2, rows, :], here), 112, 1)
        return (
            here,
            jnp.where(low, below, above),
            strip_ref[n + 1, g - 1:g + 7, :],
            strip_ref[n + 1, g + 1:g + 9, :],
            pltpu.roll(jnp.where(lane % 16 == 7, seam, here), 1, 1),
            pltpu.roll(jnp.where(lane % 16 == 8, seam, here), 127, 1),
        )

    turn_all(es_refs)

    def weights(centre, sides, charge, c_ref, coef_ref, m, g):
        faces = [0.5 * (centre + side) for side in sides]
        total = faces[0]
        for face in faces[1:]:
            total = total + face
        scale = OVER_RELAX / total
        c_ref[m, g - 8:g, :] = scale * charge
        for i in range(6):
            coef_ref[i, m, g - 8:g, :] = scale * faces[i]

    for c in (0, 1):
        low = odd if c else even

        def main_weights(n, _):
            for k in range(WU):
                m = WU * n + k
                for g in blocks:
                    if g == 8:
                        a, b = x_charge[0, 2 * m], x_charge[0, 2 * m + 1]
                    elif g == TOP + TX:
                        a, b = x_charge[1, 2 * m], x_charge[1, 2 * m + 1]
                    else:
                        a, b = charge_ref[2 * m, g - TOP:g - TOP + 8, :], charge_ref[2 * m + 1, g - TOP:g - TOP + 8, :]
                    sides = main_sides(e_refs[1 - c], seam_refs[1 - c], m, g, low)
                    weights(e_refs[c][m + 1, g:g + 8, :], sides, jnp.where(low, a, b), c_refs[c], coef_refs[c], m, g)
            return 0
        lax.fori_loop(0, HALF // WU, main_weights, 0)

        def strip_weights(n, _):
            for g in blocks:
                sides = strip_sides(e_refs[1 - c], es_refs[1 - c], n, g, low)
                weights(es_refs[c][n + 1, g:g + 8, :], sides, gs_refs[c][n, g - 8:g, :], cs_refs[c], coefs_refs[c], n, g)
            return 0
        lax.fori_loop(0, GROUPS, strip_weights, 0)

    def updated(own, sides, c_ref, coef_ref, m, g):
        parts = [coef_ref[i, m, g - 8:g, :] * side for i, side in enumerate(sides)]
        first_part = c_ref[m, g - 8:g, :] - (OVER_RELAX - 1.0) * own
        return ((first_part + parts[0]) + (parts[1] + parts[2])) + (parts[3] + (parts[4] + parts[5]))

    def step(c, inner):
        low = odd if c else even

        def main_step(n, _):
            for k in range(UNROLL):
                m = UNROLL * n + k
                chosen = blocks[1:-1] if inner else blocks
                values = []
                for g in chosen:
                    sides = main_sides(p_refs[1 - c], seam_refs[1 - c], m, g, low)
                    values.append(updated(p_refs[c][m + 1, g:g + 8, :], sides, c_refs[c], coef_refs[c], m, g))
                for g, value in zip(chosen, values):
                    p_refs[c][m + 1, g:g + 8, :] = value
            return 0
        lax.fori_loop(0, HALF // UNROLL, main_step, 0)
        if inner:
            return

        def strip_step(n, _):
            for g in blocks:
                sides = strip_sides(p_refs[1 - c], ps_refs[1 - c], n, g, low)
                value = updated(ps_refs[c][n + 1, g:g + 8, :], sides, cs_refs[c], coefs_refs[c], n, g)
                ps_refs[c][n + 1, g:g + 8, :] = value
                turn(seam_refs[c], n, g, value)
            return 0
        lax.fori_loop(0, GROUPS, strip_step, 0)

    mail.wait()
    write_table(table_ref, lambda t: motion_ref[...] if t == 4 else got_ref[t])

    def edges1(m, _):
        for side, g in ((0, 8), (1, TOP + TX)):
            two(p_refs, m + 1, slice(g, g + 8), x_phi[side, 2 * m], x_phi[side, 2 * m + 1])
        return 0
    lax.fori_loop(0, HALF, edges1, 0)

    def strips1(g, _):
        for r in range(0, TX + 16, 8):
            two(ps_refs, g + 1, slice(8 + r, 16 + r), *unpacked(from_low, from_high, g, r))
        return 0
    lax.fori_loop(0, GROUPS, strips1, 0)
    turn_all(ps_refs)

    def three(i, _):
        step(0, False)
        step(1, False)
        return 0
    lax.fori_loop(0, 3, three, 0)
    step(0, False)
    step(1, True)

    def coloured(g, k, r):
        value = p_refs[k % 2][8 * g + k // 2 + 1, TOP + r:TOP + r + 16, :]
        return value[0:8], value[8:16]

    for c in (0, 1):
        mail.send(1, p_refs[c].at[pl.ds(1, HALF), pl.ds(TOP, 8), :], x2_refs[c].at[1])
        mail.send(7, p_refs[c].at[pl.ds(1, HALF), pl.ds(TOP + TX - 8, 8), :], x2_refs[c].at[0])
    pack(coloured, to2_low, to2_high, 0)
    send_sides(to2_low, to2_high, from2_low, from2_high, 0)
    mail.wait()

    def edges2(m, _):
        for c in (0, 1):
            p_refs[c][m + 1, 8:16, :] = x2_refs[c][0, m]
            p_refs[c][m + 1, TOP + TX:TOP + TX + 8, :] = x2_refs[c][1, m]
        return 0
    lax.fori_loop(0, HALF, edges2, 0)

    def strips2(g, _):
        for r in range(0, TX + 16, 8):
            a, b = unpacked(from2_low, from2_high, g, r)
            ps_refs[0][g + 1, 8 + r:16 + r, :] = a
            ps_refs[1][g + 1, 8 + r:16 + r, :] = b
        return 0
    lax.fori_loop(0, GROUPS, strips2, 0)
    turn_all(ps_refs)
    step(0, False)
    step(1, False)
    step(0, False)
    step(1, True)

    def out(m, _):
        for g in range(0, TX, 8):
            a, b = [ref[m + 1, TOP + g:TOP + g + 8, :] for ref in p_refs]
            ea, eb = [ref[m + 1, TOP + g:TOP + g + 8, :] for ref in e_refs]
            lo, hi = jnp.where(even, a, b), jnp.where(even, b, a)
            elo, ehi = jnp.where(even, ea, eb), jnp.where(even, eb, ea)
            pot_ref[2 * m, g:g + 8, :] = lo
            pot_ref[2 * m + 1, g:g + 8, :] = hi
            q_ref[2 * m, g:g + 8, :] = 0.5 * elo * lo * lo
            q_ref[2 * m + 1, g:g + 8, :] = 0.5 * ehi * hi * hi
        return 0
    lax.fori_loop(0, HALF, out, 0)


def relax(eps, charge, phi, motion):
    vm = lambda *s: pltpu.VMEM(s, jnp.float32)
    spec = pl.BlockSpec(memory_space=pltpu.VMEM)
    return pl.pallas_call(
        relax_kernel,
        out_shape=(
            jax.ShapeDtypeStruct((NZ, TX, TY), jnp.float32),
            jax.ShapeDtypeStruct((NZ, TX, TY), jnp.float32),
            jax.ShapeDtypeStruct((8, SLOTS_PAD), jnp.float32),
        ),
        in_specs=[spec] * 4,
        out_specs=(spec,) * 3,
        scratch_shapes=[
            [vm(HALF + 2, ROWS, 128)] * 2,
            [vm(HALF + 2, ROWS, 128)] * 2,
            [vm(GROUPS + 2, ROWS, 128)] * 2,
            [vm(GROUPS + 2, ROWS, 128)] * 2,
            [vm(GROUPS, ROWS - 16, 128)] * 2,
            [vm(HALF, ROWS - 16, 128)] * 2,
            [vm(HALF, ROWS - 16, 128)] * 2,
            [vm(6, HALF, ROWS - 16, 128)] * 2,
            [vm(GROUPS, ROWS - 16, 128)] * 2,
            [vm(6, GROUPS, ROWS - 16, 128)] * 2,
            vm(3 * GROUPS, TX, 128), vm(3 * GROUPS, TX, 128),
            vm(3 * GROUPS, TX + 16, 128), vm(3 * GROUPS, TX + 16, 128),
            pltpu.VMEM((2, NZ, 16, 128), jnp.bfloat16), vm(2, NZ, 8, 128), vm(2, NZ, 8, 128),
            vm(GROUPS, TX, 128), vm(GROUPS, TX, 128),
            vm(GROUPS, TX + 16, 128), vm(GROUPS, TX + 16, 128),
            [vm(2, HALF, 8, 128)] * 2,
            vm(9, 8, 128),
            pltpu.SemaphoreType.DMA((42,)), pltpu.SemaphoreType.DMA((42,)),
        ],
        name="relax",
        compiler_params=pltpu.CompilerParams(vmem_limit_bytes=58 * 2**20, collective_id=0, has_side_effects=True),
    )(eps, charge, phi, motion)


CHUNK = 1024
CHUNKS = LINKS // CHUNK
RING = 2
SLOTS = 9 * NC_DEV
SLOTS_PAD = 384
VELOCITY = np.array(
    [[1, 0, 0], [-1, 0, 0], [0, 1, 0], [0, -1, 0], [0, 0, 1], [0, 0, -1], [1, 1, 0], [1, -1, 0], [-1, 1, 0],
     [-1, -1, 0], [1, 0, 1], [1, 0, -1], [-1, 0, 1], [-1, 0, -1], [0, 1, 1], [0, 1, -1], [0, -1, 1], [0, -1, -1]],
    dtype=np.float32,
).T
WEIGHT = np.array([1.0 / 18.0] * 6 + [1.0 / 36.0] * 12, dtype=np.float32)


def lattice_table():
    rows = np.zeros((4, 8, 128), np.float32)
    rows[0:3, :, 0:18] = VELOCITY[:, None, :]
    rows[3, :, 0:18] = WEIGHT[None, :]
    return jnp.asarray(rows.reshape(32, 128))


def split(values):
    high = values.astype(jnp.bfloat16).astype(jnp.float32)
    return jnp.concatenate([high, values - high], axis=0).astype(jnp.bfloat16)


def cross(first, second):
    return (
        first[1] * second[2] - first[2] * second[1],
        first[2] * second[0] - first[0] * second[2],
        first[0] * second[1] - first[1] * second[0],
    )


def decode(lat_ref, direction):
    return [jnp.take_along_axis(lat_ref[8 * i:8 * i + 8, :], direction, axis=1) for i in range(4)]


def onehot_of(slot_ref, base, pair):
    ids = lax.broadcasted_iota(jnp.int32, (SLOTS, 128), 0)
    halves = [ids == slot_ref[pl.ds(base + 2 * pair + h, 1), :] for h in (0, 1)]
    return jnp.concatenate([half.astype(jnp.float32) for half in halves], axis=1).astype(jnp.bfloat16)


def found_at(table, onehot, pair, at_ref):
    found = jnp.dot(table, onehot, preferred_element_type=jnp.float32)
    found = found[0:8] + found[8:16]
    at_ref[16 * pair:16 * pair + 8, :] = found[:, 0:128]
    at_ref[16 * pair + 8:16 * pair + 16, :] = found[:, 128:256]


def links_kernel(
    row_ref, site_ref, dir_ref, ids_ref, pop_ref, rb_ref, q_ref, table_ref, lat_ref, slot_ref, gain_ref, sums_ref,
    onehot_ref, at_ref, term_ref, index_refs, index_sem,
):
    home_x = lax.axis_index("gx")
    home_y = lax.axis_index("gy")
    lane = lax.broadcasted_iota(jnp.int32, (8, 128), 1)
    sub = lax.broadcasted_iota(jnp.int32, (8, 128), 0)

    def fetch(b, k):
        rows = row_ref.at[pl.ds(pl.multiple_of(b * CHUNK, CHUNK), CHUNK)]
        return pltpu.make_async_copy(rows, index_refs[k], index_sem.at[k])

    for k in range(RING):
        fetch(k, k).start()
    sums_ref[...] = jnp.zeros_like(sums_ref)
    term_ref[...] = jnp.zeros_like(term_ref)
    table = split(table_ref[...])[:, 0:SLOTS]

    def group(b, k):
        base = pl.multiple_of(b * 8, 8)
        rows = pl.ds(base, 8)
        ids = ids_ref[rows, :]
        owner = ids >> 5
        near_x = ((owner >> 4) - home_x + 1) & (TILES_X - 1)
        near_y = ((owner & (TILES_Y - 1)) - home_y + 1) & (TILES_Y - 1)
        slot_ref[rows, :] = jnp.where(ids >= 0, (near_x * 3 + near_y) * NC_DEV + (ids & (NC_DEV - 1)), -1)
        column = site_ref[rows, :] & 127
        pressure = jnp.zeros((8, 128), jnp.float32)
        fetch(b, k).wait()
        for j in range(128):
            at = lambda s: jnp.broadcast_to(q_ref[pl.ds(index_refs[k][s * 128 + j], 1), :], (8, 128))
            picked = at(0)
            for s in range(1, 8):
                picked = jnp.where(sub == s, at(s), picked)
            pressure = jnp.where(lane == j, jnp.take_along_axis(picked, column, axis=1), pressure)

        @pl.when(b + RING < CHUNKS)
        def _():
            fetch(b + RING, k).start()

        *velocity, weight = decode(lat_ref, dir_ref[rows, :])
        offsets = [rb_ref[i, rows, :] for i in range(3)]
        arms = (*velocity, *cross(offsets, velocity))
        for pair in range(4):
            onehot = onehot_of(slot_ref, base, pair)
            onehot_ref[:, 256 * pair:256 * pair + 256] = onehot
            found_at(table, onehot, pair, at_ref)
        live = ids >= 0
        scale = jnp.where(live, 6.0 * weight, 0.0)
        source = jnp.where(live, 2.0 * pop_ref[rows, :] + weight * pressure, 0.0)
        for i, arm in enumerate(arms):
            gain = scale * arm
            gain_ref[i, rows, :] = gain
            source = source - gain * at_ref[pl.ds(i, 8, stride=8), :]
        for i, arm in enumerate(arms):
            term_ref[pl.ds(i, 8, stride=8), :] = arm * source
        total = jnp.zeros((16, SLOTS), jnp.float32)
        for pair in range(4):
            terms = jnp.concatenate([term_ref[16 * pair:16 * pair + 8, :], term_ref[16 * pair + 8:16 * pair + 16, :]], axis=1)
            total = total + lax.dot_general(
                split(terms), onehot_ref[:, 256 * pair:256 * pair + 256], (((1,), (1,)), ((), ())),
                preferred_element_type=jnp.float32,
            )
        sums_ref[:, 0:SLOTS] += total[0:8] + total[8:16]

    def ring(i, _):
        for k in range(RING):
            group(i * RING + k, k)
        return 0

    lax.fori_loop(0, CHUNKS // RING, ring, 0)


VM = pl.BlockSpec(memory_space=pltpu.VMEM)


def link_sums(row, site, direction, ids, pop, rb, q, table):
    return pl.pallas_call(
        links_kernel,
        in_specs=[pl.BlockSpec(memory_space=pl.ANY)] + [VM] * 8,
        out_specs=(VM, VM, VM),
        out_shape=(
            jax.ShapeDtypeStruct((LINKS // 128, 128), jnp.int32),
            jax.ShapeDtypeStruct((6, LINKS // 128, 128), jnp.float32),
            jax.ShapeDtypeStruct((8, SLOTS_PAD), jnp.float32),
        ),
        scratch_shapes=[
            pltpu.VMEM((SLOTS, CHUNK), jnp.bfloat16), pltpu.VMEM((64, 128), jnp.float32), pltpu.VMEM((64, 128), jnp.float32),
            [pltpu.SMEM((CHUNK,), jnp.int32)] * RING, pltpu.SemaphoreType.DMA((RING,)),
        ],
        name="link_sums",
        compiler_params=pltpu.CompilerParams(vmem_limit_bytes=40 * 2**20),
    )(row, site, direction, ids, pop, rb, q, table, lattice_table())


def update_kernel(
    sums_ref, motion_ref, slot_ref, pop_ref, gain_ref, report_ref, out_ref,
    part_ref, got_ref, new_ref, back_ref, table_ref, onehot_ref, at_ref, send_sem, recv_sem,
):
    greeted = greet()
    mail = Mail(send_sem, recv_sem)
    lane = lax.broadcasted_iota(jnp.int32, (8, 128), 1)
    row = lax.broadcasted_iota(jnp.int32, (8, 128), 0)
    for t in range(9):
        value = sums_ref[:, 128 * (t // 4):128 * (t // 4) + 128]
        if t % 4:
            value = pltpu.roll(value, 128 - NC_DEV * (t % 4), 1)
        part_ref[t] = jnp.where(lane < NC_DEV, value, 0.0)
    greeted()
    for t, _ in beside():
        mail.send(t, part_ref.at[t], got_ref.at[8 - t])

    def prepare(b, _):
        for pair in range(4):
            onehot_ref[b, :, 256 * pair:256 * pair + 256] = onehot_of(slot_ref, pl.multiple_of(b * 8, 8), pair)
        return 0

    lax.fori_loop(0, CHUNKS // 2, prepare, 0)
    total = part_ref[4]
    mail.wait()
    for t in range(9):
        if t != 4:
            total = total + got_ref[t]
    mass = 4.0 / 3.0 * math.pi * RADIUS**3
    inertia = 0.4 * mass * RADIUS**2
    report_ref[...] = jnp.where(row < 3, total, total / RADIUS)
    new_ref[...] = motion_ref[...] + jnp.where(row < 3, total / mass, total / inertia)
    for t, _ in beside():
        mail.send(t, new_ref, back_ref.at[8 - t])
    lax.fori_loop(CHUNKS // 2, CHUNKS, prepare, 0)
    mail.wait()
    write_table(table_ref, lambda t: new_ref[...] if t == 4 else back_ref[t])
    table = split(table_ref[...])[:, 0:SLOTS]

    def group(b, _):
        rows = pl.ds(pl.multiple_of(b * 8, 8), 8)
        for pair in range(4):
            found_at(table, onehot_ref[b, :, 256 * pair:256 * pair + 256], pair, at_ref)
        value = pop_ref[rows, :]
        for i in range(6):
            value = value - gain_ref[i, rows, :] * at_ref[pl.ds(i, 8, stride=8), :]
        out_ref[rows, :] = value
        return 0

    lax.fori_loop(0, CHUNKS, group, 0)


def update(sums, motion, slot, pop, gain):
    return pl.pallas_call(
        update_kernel,
        out_shape=(jax.ShapeDtypeStruct((8, 128), jnp.float32), jax.ShapeDtypeStruct((LINKS // 128, 128), jnp.float32)),
        in_specs=[VM] * 5,
        out_specs=(VM, VM),
        scratch_shapes=[
            pltpu.VMEM((9, 8, 128), jnp.float32), pltpu.VMEM((9, 8, 128), jnp.float32),
            pltpu.VMEM((8, 128), jnp.float32), pltpu.VMEM((9, 8, 128), jnp.float32),
            pltpu.VMEM((8, SLOTS_PAD), jnp.float32), pltpu.VMEM((CHUNKS, SLOTS, CHUNK), jnp.bfloat16),
            pltpu.VMEM((64, 128), jnp.float32),
            pltpu.SemaphoreType.DMA((16,)), pltpu.SemaphoreType.DMA((16,)),
        ],
        name="update",
        compiler_params=pltpu.CompilerParams(vmem_limit_bytes=40 * 2**20, collective_id=1, has_side_effects=True),
    )(sums, motion, slot, pop, gain)


def shards(
    eps_field, charge, potential_start, colloid_vel, colloid_spin, link_dir, link_colloid, link_site, link_depth,
    link_pop, link_rb,
):
    flat = lambda a: a.reshape(LINKS // 128, 128)
    motion = jnp.pad(jnp.concatenate([colloid_vel, colloid_spin], axis=0), ((0, 2), (0, 128 - NC_DEV)))
    potential, q, table = relax(eps_field, charge, potential_start, motion)
    row = link_depth.reshape(-1) * TX + (link_site.reshape(-1) >> 7)
    rb = link_rb.reshape(3, LINKS // 128, 128)
    slot, gain, sums = link_sums(
        row, flat(link_site), flat(link_dir), flat(link_colloid), flat(link_pop), rb, q.reshape(NZ * TX, TY), table
    )
    report, link_out = update(sums, motion, slot, flat(link_pop), gain)
    link_out = link_out.reshape(link_pop.shape)
    return potential, report[0:6, 0:NC_DEV], link_out


def solution(mesh):
    tile = P(None, "gx", "gy")
    owned = P(None, ("gx", "gy"))
    link = P("gx", "gy", None)
    return jax.shard_map(
        shards,
        mesh=mesh,
        in_specs=(tile, tile, tile, owned, owned, link, link, link, link, link, P(None, "gx", "gy", None)),
        out_specs=(tile, owned, link),
        check_vma=False,
    )
```

```python
import math

import jax
import jax.numpy as jnp
import numpy as np
from jax import lax
from jax.experimental import pallas as pl
from jax.experimental.pallas import tpu as pltpu
from jax.sharding import PartitionSpec as P

TILES_X, TILES_Y = 8, 16
NC_DEV = 32
LINKS = 32768
RADIUS = 8
SWEEPS = 6
OVER_RELAX = 1.6
NZ, TX, TY = 48, 64, 128
HALF = NZ // 2
GROUPS = HALF // 8
ROWS = 96
TOP = 16
UNROLL = 8
WU = 4


def beside():
    x, y = lax.axis_index("gx"), lax.axis_index("gy")
    for t in range(9):
        if t != 4:
            yield t, (lax.rem(x + t // 3 - 1 + TILES_X, TILES_X), lax.rem(y + t % 3 - 1 + TILES_Y, TILES_Y))


def greet():
    barrier = pltpu.get_barrier_semaphore()
    for _, device in beside():
        pl.semaphore_signal(barrier, inc=1, device_id=device, device_id_type=pl.DeviceIdType.MESH)
    return lambda: pl.semaphore_wait(barrier, 8)


class Mail:
    def __init__(self, send_sem, recv_sem):
        self.sems, self.count, self.copies, self.device = (send_sem, recv_sem), 0, [], dict(beside())

    def send(self, t, source, target):
        copy = pltpu.make_async_remote_copy(
            src_ref=source, dst_ref=target, send_sem=self.sems[0].at[self.count], recv_sem=self.sems[1].at[self.count],
            device_id=self.device[t], device_id_type=pl.DeviceIdType.MESH,
        )
        copy.start()
        self.count += 1
        self.copies.append(copy)

    def wait(self):
        for copy in self.copies:
            copy.wait()
        self.copies = []


def write_table(table_ref, block):
    for tile in range(3):
        total = jnp.zeros((8, 128), jnp.float32)
        for i in range(4):
            if 4 * tile + i < 9:
                value = block(4 * tile + i)
                total = total + (pltpu.roll(value, NC_DEV * i, 1) if i else value)
        table_ref[:, 128 * tile:128 * tile + 128] = total


def relax_kernel(
    eps_ref, charge_ref, phi_ref, motion_ref, pot_ref, q_ref, table_ref,
    p_refs, e_refs, ps_refs, es_refs, gs_refs, seam_refs, c_refs, coef_refs, cs_refs, coefs_refs,
    to_low, to_high, from_low, from_high, x_eps, x_charge, x_phi, to2_low, to2_high, from2_low, from2_high, x2_refs,
    got_ref, send_sem, recv_sem,
):
    sub = lax.broadcasted_iota(jnp.int32, (8, 128), 0)
    lane = lax.broadcasted_iota(jnp.int32, (8, 128), 1)
    even = (sub + lane) % 2 == 0
    odd = ~even
    first = lane % 16 < 8
    slot = lane // 16
    zero = jnp.zeros((8, 128), jnp.float32)
    blocks = range(8, ROWS - 8, 8)
    greeted = greet()
    mail = Mail(send_sem, recv_sem)

    def pack(plane, low_ref, high_ref, at):
        def group(g, _):
            for r in range(0, TX, 16):
                low, high = [zero, zero], [zero, zero]
                for k in range(16):
                    rows = plane(g, k, r)
                    for h in (0, 1):
                        value = rows[h]
                        here = lane // 8 == k
                        low[h] = jnp.where(here, pltpu.roll(value, 8 * k, 1) if k else value, low[h])
                        high[h] = jnp.where(here, pltpu.roll(value, 8 * (k + 1), 1) if k < 15 else value, high[h])
                for h in (0, 1):
                    low_ref[at + g, r + 8 * h:r + 8 * h + 8, :] = low[h]
                    high_ref[at + g, r + 8 * h:r + 8 * h + 8, :] = high[h]
            return 0
        lax.fori_loop(0, GROUPS, group, 0)

    def send_sides(low_ref, high_ref, dst_low, dst_high, at):
        span = pl.ds(at, GROUPS)
        for t, rows, target in ((3, (0, TX), 8), (0, (0, 8), 72), (6, (TX - 8, 8), 0)):
            mail.send(t, low_ref.at[span, pl.ds(*rows), :], dst_high.at[span, pl.ds(target, rows[1]), :])
            mail.send(t + 2, high_ref.at[span, pl.ds(*rows), :], dst_low.at[span, pl.ds(target, rows[1]), :])

    def natural(ref):
        def plane(g, k, r):
            value = ref[16 * g + k, r:r + 16, :].astype(jnp.float32)
            return value[0:8], value[8:16]
        return plane

    def send_rows(ref, target, rows):
        mail.send(1, ref.at[:, pl.ds(0, rows), :], target.at[1])
        mail.send(7, ref.at[:, pl.ds(TX - rows, rows), :], target.at[0])

    pack(natural(eps_ref), to_low, to_high, GROUPS)
    greeted()
    send_sides(to_low, to_high, from_low, from_high, GROUPS)
    send_rows(eps_ref, x_eps, 16)
    send_rows(charge_ref, x_charge, 8)
    pack(natural(charge_ref), to_low, to_high, 2 * GROUPS)
    send_sides(to_low, to_high, from_low, from_high, 2 * GROUPS)
    early, mail.copies = mail.copies, []
    send_rows(phi_ref, x_phi, 8)
    pack(natural(phi_ref), to_low, to_high, 0)
    send_sides(to_low, to_high, from_low, from_high, 0)
    for t, _ in beside():
        mail.send(t, motion_ref, got_ref.at[8 - t])

    def clear(m, _):
        for ref in (*p_refs, *e_refs):
            for g in (0, ROWS - 8):
                ref[m, g:g + 8, :] = zero
        return 0
    lax.fori_loop(0, HALF + 2, clear, 0)
    for ref in p_refs:
        for g in blocks:
            ref[0, g:g + 8, :] = zero
            ref[HALF + 1, g:g + 8, :] = zero
    for ref in (*ps_refs, *es_refs):
        for g in (0, ROWS - 8):
            for m in range(GROUPS + 2):
                ref[m, g:g + 8, :] = zero
    for ref in ps_refs:
        for g in blocks:
            ref[0, g:g + 8, :] = zero
            ref[GROUPS + 1, g:g + 8, :] = zero

    def two(refs, m, rows, a, b):
        refs[0][m, rows, :] = jnp.where(even, a, b)
        refs[1][m, rows, :] = jnp.where(even, b, a)

    def compact(m, _):
        for r in range(0, TX, 16):
            a = eps_ref[2 * m, r:r + 16, :].astype(jnp.float32)
            b = eps_ref[2 * m + 1, r:r + 16, :].astype(jnp.float32)
            for h in (0, 8):
                two(e_refs, m + 1, slice(TOP + r + h, TOP + r + h + 8), a[h:h + 8], b[h:h + 8])
        for r in range(0, TX, 8):
            two(p_refs, m + 1, slice(TOP + r, TOP + r + 8), phi_ref[2 * m, r:r + 8, :], phi_ref[2 * m + 1, r:r + 8, :])
        return 0
    lax.fori_loop(0, HALF, compact, 0)

    for copy in early:
        copy.wait()

    def edges(m, _):
        for side, g in ((0, 8), (1, TOP + TX)):
            rows = slice(8, 16) if side == 0 else slice(0, 8)
            a = x_eps[side, 2 * m].astype(jnp.float32)[rows]
            b = x_eps[side, 2 * m + 1].astype(jnp.float32)[rows]
            two(e_refs, m + 1, slice(g, g + 8), a, b)
        return 0
    lax.fori_loop(0, HALF, edges, 0)

    def unpacked(low_ref, high_ref, at, r):
        low, high = low_ref[at, r:r + 8, :], high_ref[at, r:r + 8, :]
        return jnp.where(first, low, pltpu.roll(high, 8, 1)), jnp.where(first, pltpu.roll(low, 120, 1), high)

    def strips(g, _):
        for r in range(0, TX + 16, 8):
            rows = slice(8 + r, 16 + r)
            two(es_refs, g + 1, rows, *unpacked(from_low, from_high, GROUPS + g, r))
            two(gs_refs, g, slice(r, r + 8), *unpacked(from_low, from_high, 2 * GROUPS + g, r))
        return 0
    lax.fori_loop(0, GROUPS, strips, 0)
    for g in blocks:
        rows = slice(g, g + 8)
        for c in (0, 1):
            e_refs[1 - c][0, rows, :] = e_refs[c][1, rows, :]
            e_refs[1 - c][HALF + 1, rows, :] = e_refs[c][HALF, rows, :]
            es_refs[1 - c][0, rows, :] = pltpu.roll(es_refs[c][1, rows, :], 112, 1)
            es_refs[1 - c][GROUPS + 1, rows, :] = pltpu.roll(es_refs[c][GROUPS, rows, :], 16, 1)

    def turn(seam_ref, n, g, value):
        for k in range(8):
            seam_ref[8 * n + k, g - 8:g, :] = pltpu.roll(value, 120 - 16 * k, 1)

    def turn_all(strip_refs):
        def one(n, _):
            for g in blocks:
                for c in (0, 1):
                    turn(seam_refs[c], n, g, strip_refs[c][n + 1, g:g + 8, :])
            return 0
        lax.fori_loop(0, GROUPS, one, 0)

    def main_sides(ref, seam_ref, m, g, low):
        rows = slice(g, g + 8)
        here = ref[m + 1, rows, :]
        seam = seam_ref[m, g - 8:g, :]
        return (
            here,
            jnp.where(low, ref[m, rows, :], ref[m + 2, rows, :]),
            ref[m + 1, g - 1:g + 7, :],
            ref[m + 1, g + 1:g + 9, :],
            pltpu.roll(jnp.where(lane == 127, seam, here), 1, 1),
            pltpu.roll(jnp.where(lane == 0, seam, here), 127, 1),
        )

    def strip_sides(ref, strip_ref, n, g, low):
        rows = slice(g, g + 8)
        here = strip_ref[n + 1, rows, :]
        seam = zero
        for k in range(8):
            seam = jnp.where(slot == k, pltpu.roll(ref[8 * n + k + 1, rows, :], 16 * k + 8, 1), seam)
        below = pltpu.roll(jnp.where(slot == 7, strip_ref[n, rows, :], here), 16, 1)
        above = pltpu.roll(jnp.where(slot == 0, strip_ref[n + 2, rows, :], here), 112, 1)
        return (
            here,
            jnp.where(low, below, above),
            strip_ref[n + 1, g - 1:g + 7, :],
            strip_ref[n + 1, g + 1:g + 9, :],
            pltpu.roll(jnp.where(lane % 16 == 7, seam, here), 1, 1),
            pltpu.roll(jnp.where(lane % 16 == 8, seam, here), 127, 1),
        )

    turn_all(es_refs)

    def weights(centre, sides, charge, c_ref, coef_ref, m, g):
        faces = [0.5 * (centre + side) for side in sides]
        total = faces[0]
        for face in faces[1:]:
            total = total + face
        scale = OVER_RELAX / total
        c_ref[m, g - 8:g, :] = scale * charge
        for i in range(6):
            coef_ref[i, m, g - 8:g, :] = scale * faces[i]

    for c in (0, 1):
        low = odd if c else even

        def main_weights(n, _):
            for k in range(WU):
                m = WU * n + k
                for g in blocks:
                    if g == 8:
                        a, b = x_charge[0, 2 * m], x_charge[0, 2 * m + 1]
                    elif g == TOP + TX:
                        a, b = x_charge[1, 2 * m], x_charge[1, 2 * m + 1]
                    else:
                        a, b = charge_ref[2 * m, g - TOP:g - TOP + 8, :], charge_ref[2 * m + 1, g - TOP:g - TOP + 8, :]
                    sides = main_sides(e_refs[1 - c], seam_refs[1 - c], m, g, low)
                    weights(e_refs[c][m + 1, g:g + 8, :], sides, jnp.where(low, a, b), c_refs[c], coef_refs[c], m, g)
            return 0
        lax.fori_loop(0, HALF // WU, main_weights, 0)

        def strip_weights(n, _):
            for g in blocks:
                sides = strip_sides(e_refs[1 - c], es_refs[1 - c], n, g, low)
                weights(es_refs[c][n + 1, g:g + 8, :], sides, gs_refs[c][n, g - 8:g, :], cs_refs[c], coefs_refs[c], n, g)
            return 0
        lax.fori_loop(0, GROUPS, strip_weights, 0)

    def updated(own, sides, c_ref, coef_ref, m, g):
        parts = [coef_ref[i, m, g - 8:g, :] * side for i, side in enumerate(sides)]
        first_part = c_ref[m, g - 8:g, :] - (OVER_RELAX - 1.0) * own
        return ((first_part + parts[0]) + (parts[1] + parts[2])) + (parts[3] + (parts[4] + parts[5]))

    def step(c, inner):
        low = odd if c else even

        def main_step(n, _):
            for k in range(UNROLL):
                m = UNROLL * n + k
                chosen = blocks[1:-1] if inner else blocks
                values = []
                for g in chosen:
                    sides = main_sides(p_refs[1 - c], seam_refs[1 - c], m, g, low)
                    values.append(updated(p_refs[c][m + 1, g:g + 8, :], sides, c_refs[c], coef_refs[c], m, g))
                for g, value in zip(chosen, values):
                    p_refs[c][m + 1, g:g + 8, :] = value
            return 0
        lax.fori_loop(0, HALF // UNROLL, main_step, 0)
        if inner:
            return

        def strip_step(n, _):
            for g in blocks:
                sides = strip_sides(p_refs[1 - c], ps_refs[1 - c], n, g, low)
                value = updated(ps_refs[c][n + 1, g:g + 8, :], sides, cs_refs[c], coefs_refs[c], n, g)
                ps_refs[c][n + 1, g:g + 8, :] = value
                turn(seam_refs[c], n, g, value)
            return 0
        lax.fori_loop(0, GROUPS, strip_step, 0)

    mail.wait()
    write_table(table_ref, lambda t: motion_ref[...] if t == 4 else got_ref[t])

    def edges1(m, _):
        for side, g in ((0, 8), (1, TOP + TX)):
            two(p_refs, m + 1, slice(g, g + 8), x_phi[side, 2 * m], x_phi[side, 2 * m + 1])
        return 0
    lax.fori_loop(0, HALF, edges1, 0)

    def strips1(g, _):
        for r in range(0, TX + 16, 8):
            two(ps_refs, g + 1, slice(8 + r, 16 + r), *unpacked(from_low, from_high, g, r))
        return 0
    lax.fori_loop(0, GROUPS, strips1, 0)
    turn_all(ps_refs)

    def three(i, _):
        step(0, False)
        step(1, False)
        return 0
    lax.fori_loop(0, 3, three, 0)
    step(0, False)

    def send_rows2(c):
        mail.send(1, p_refs[c].at[pl.ds(1, HALF), pl.ds(TOP, 8), :], x2_refs[c].at[1])
        mail.send(7, p_refs[c].at[pl.ds(1, HALF), pl.ds(TOP + TX - 8, 8), :], x2_refs[c].at[0])

    send_rows2(0)
    step(1, True)

    def coloured(g, k, r):
        value = p_refs[k % 2][8 * g + k // 2 + 1, TOP + r:TOP + r + 16, :]
        return value[0:8], value[8:16]

    send_rows2(1)
    pack(coloured, to2_low, to2_high, 0)
    send_sides(to2_low, to2_high, from2_low, from2_high, 0)
    mail.wait()

    def edges2(m, _):
        for c in (0, 1):
            p_refs[c][m + 1, 8:16, :] = x2_refs[c][0, m]
            p_refs[c][m + 1, TOP + TX:TOP + TX + 8, :] = x2_refs[c][1, m]
        return 0
    lax.fori_loop(0, HALF, edges2, 0)

    def strips2(g, _):
        for r in range(0, TX + 16, 8):
            a, b = unpacked(from2_low, from2_high, g, r)
            ps_refs[0][g + 1, 8 + r:16 + r, :] = a
            ps_refs[1][g + 1, 8 + r:16 + r, :] = b
        return 0
    lax.fori_loop(0, GROUPS, strips2, 0)
    turn_all(ps_refs)
    step(0, False)
    step(1, False)
    step(0, False)
    step(1, True)

    def out(m, _):
        for g in range(0, TX, 8):
            a, b = [ref[m + 1, TOP + g:TOP + g + 8, :] for ref in p_refs]
            ea, eb = [ref[m + 1, TOP + g:TOP + g + 8, :] for ref in e_refs]
            lo, hi = jnp.where(even, a, b), jnp.where(even, b, a)
            elo, ehi = jnp.where(even, ea, eb), jnp.where(even, eb, ea)
            pot_ref[2 * m, g:g + 8, :] = lo
            pot_ref[2 * m + 1, g:g + 8, :] = hi
            q_ref[2 * m, g:g + 8, :] = 0.5 * elo * lo * lo
            q_ref[2 * m + 1, g:g + 8, :] = 0.5 * ehi * hi * hi
        return 0
    lax.fori_loop(0, HALF, out, 0)


def relax(eps, charge, phi, motion):
    vm = lambda *s: pltpu.VMEM(s, jnp.float32)
    spec = pl.BlockSpec(memory_space=pltpu.VMEM)
    return pl.pallas_call(
        relax_kernel,
        out_shape=(
            jax.ShapeDtypeStruct((NZ, TX, TY), jnp.float32),
            jax.ShapeDtypeStruct((NZ, TX, TY), jnp.float32),
            jax.ShapeDtypeStruct((8, SLOTS_PAD), jnp.float32),
        ),
        in_specs=[spec] * 4,
        out_specs=(spec,) * 3,
        scratch_shapes=[
            [vm(HALF + 2, ROWS, 128)] * 2,
            [vm(HALF + 2, ROWS, 128)] * 2,
            [vm(GROUPS + 2, ROWS, 128)] * 2,
            [vm(GROUPS + 2, ROWS, 128)] * 2,
            [vm(GROUPS, ROWS - 16, 128)] * 2,
            [vm(HALF, ROWS - 16, 128)] * 2,
            [vm(HALF, ROWS - 16, 128)] * 2,
            [vm(6, HALF, ROWS - 16, 128)] * 2,
            [vm(GROUPS, ROWS - 16, 128)] * 2,
            [vm(6, GROUPS, ROWS - 16, 128)] * 2,
            vm(3 * GROUPS, TX, 128), vm(3 * GROUPS, TX, 128),
            vm(3 * GROUPS, TX + 16, 128), vm(3 * GROUPS, TX + 16, 128),
            pltpu.VMEM((2, NZ, 16, 128), jnp.bfloat16), vm(2, NZ, 8, 128), vm(2, NZ, 8, 128),
            vm(GROUPS, TX, 128), vm(GROUPS, TX, 128),
            vm(GROUPS, TX + 16, 128), vm(GROUPS, TX + 16, 128),
            [vm(2, HALF, 8, 128)] * 2,
            vm(9, 8, 128),
            pltpu.SemaphoreType.DMA((42,)), pltpu.SemaphoreType.DMA((42,)),
        ],
        name="relax",
        compiler_params=pltpu.CompilerParams(vmem_limit_bytes=58 * 2**20, collective_id=0, has_side_effects=True),
    )(eps, charge, phi, motion)


CHUNK = 1024
CHUNKS = LINKS // CHUNK
SLOTS = 9 * NC_DEV
SLOTS_PAD = 384
VELOCITY = np.array(
    [[1, 0, 0], [-1, 0, 0], [0, 1, 0], [0, -1, 0], [0, 0, 1], [0, 0, -1], [1, 1, 0], [1, -1, 0], [-1, 1, 0],
     [-1, -1, 0], [1, 0, 1], [1, 0, -1], [-1, 0, 1], [-1, 0, -1], [0, 1, 1], [0, 1, -1], [0, -1, 1], [0, -1, -1]],
    dtype=np.float32,
).T
WEIGHT = np.array([1.0 / 18.0] * 6 + [1.0 / 36.0] * 12, dtype=np.float32)


def lattice_table():
    rows = np.zeros((4, 8, 128), np.float32)
    rows[0:3, :, 0:18] = VELOCITY[:, None, :]
    rows[3, :, 0:18] = WEIGHT[None, :]
    return jnp.asarray(rows.reshape(32, 128))


def split(values):
    high = values.astype(jnp.bfloat16).astype(jnp.float32)
    return jnp.concatenate([high, values - high], axis=0).astype(jnp.bfloat16)


def cross(first, second):
    return (
        first[1] * second[2] - first[2] * second[1],
        first[2] * second[0] - first[0] * second[2],
        first[0] * second[1] - first[1] * second[0],
    )


def decode(lat_ref, direction):
    return [jnp.take_along_axis(lat_ref[8 * i:8 * i + 8, :], direction, axis=1) for i in range(4)]


def onehot_of(slot_ref, pair):
    ids = lax.broadcasted_iota(jnp.int32, (SLOTS, 128), 0)
    halves = [ids == slot_ref[2 * pair + h:2 * pair + h + 1, :] for h in (0, 1)]
    return jnp.concatenate([half.astype(jnp.float32) for half in halves], axis=1).astype(jnp.bfloat16)


def found_at(table, onehot, pair, at_ref):
    found = jnp.dot(table, onehot, preferred_element_type=jnp.float32)
    found = found[0:8] + found[8:16]
    at_ref[16 * pair:16 * pair + 8, :] = found[:, 0:128]
    at_ref[16 * pair + 8:16 * pair + 16, :] = found[:, 128:256]


def links_kernel(
    row_ref, site_ref, dir_ref, ids_ref, pop_ref, rb_ref, q_ref, table_ref, lat_ref, motion_ref, report_ref, out_ref,
    slot_ref, gain_ref, sums_ref, onehot_ref, at_ref, term_ref, press_refs, index_refs,
    part_ref, got_ref, new_ref, back_ref, moved_ref, index_sem, send_sem, recv_sem,
):
    greeted = greet()
    mail = Mail(send_sem, recv_sem)
    home_x = lax.axis_index("gx")
    home_y = lax.axis_index("gy")
    lane = lax.broadcasted_iota(jnp.int32, (8, 128), 1)
    sub = lax.broadcasted_iota(jnp.int32, (8, 128), 0)

    def fetch(b, k):
        rows = row_ref.at[pl.ds(pl.multiple_of(b * CHUNK, CHUNK), CHUNK)]
        return pltpu.make_async_copy(rows, index_refs[k], index_sem.at[k])

    def gather(b, k):
        column = site_ref[pl.ds(pl.multiple_of(b * 8, 8), 8), :] & 127
        pressure = jnp.zeros((8, 128), jnp.float32)
        for j in range(128):
            at = lambda s: jnp.broadcast_to(q_ref[pl.ds(index_refs[k][s * 128 + j], 1), :], (8, 128))
            picked = at(0)
            for s in range(1, 8):
                picked = jnp.where(sub == s, at(s), picked)
            pressure = jnp.where(lane == j, jnp.take_along_axis(picked, column, axis=1), pressure)
        press_refs[k][...] = pressure

    sums_ref[...] = jnp.zeros_like(sums_ref)
    term_ref[...] = jnp.zeros_like(term_ref)
    table = split(table_ref[...])[:, 0:SLOTS]

    def add(b, k):
        rows = pl.ds(pl.multiple_of(b * 8, 8), 8)
        ids = ids_ref[rows, :]
        owner = ids >> 5
        near_x = ((owner >> 4) - home_x + 1) & (TILES_X - 1)
        near_y = ((owner & (TILES_Y - 1)) - home_y + 1) & (TILES_Y - 1)
        slot_ref[...] = jnp.where(ids >= 0, (near_x * 3 + near_y) * NC_DEV + (ids & (NC_DEV - 1)), -1)
        *velocity, weight = decode(lat_ref, dir_ref[rows, :])
        offsets = [rb_ref[i, rows, :] for i in range(3)]
        arms = (*velocity, *cross(offsets, velocity))
        onehots = [onehot_of(slot_ref, pair) for pair in range(4)]
        for pair in range(4):
            onehot_ref[b, :, 256 * pair:256 * pair + 256] = onehots[pair]
            found_at(table, onehots[pair], pair, at_ref)
        live = ids >= 0
        scale = jnp.where(live, 6.0 * weight, 0.0)
        source = jnp.where(live, 2.0 * pop_ref[rows, :] + weight * press_refs[k][...], 0.0)
        for i, arm in enumerate(arms):
            gain = scale * arm
            gain_ref[i, rows, :] = gain
            source = source - gain * at_ref[pl.ds(i, 8, stride=8), :]
        for i, arm in enumerate(arms):
            term_ref[pl.ds(i, 8, stride=8), :] = arm * source
        total = jnp.zeros((16, SLOTS), jnp.float32)
        for pair in range(4):
            terms = jnp.concatenate([term_ref[16 * pair:16 * pair + 8, :], term_ref[16 * pair + 8:16 * pair + 16, :]], axis=1)
            total = total + lax.dot_general(
                split(terms), onehot_ref[b, :, 256 * pair:256 * pair + 256], (((1,), (1,)), ((), ())),
                preferred_element_type=jnp.float32,
            )
        sums_ref[:, 0:SLOTS] += total[0:8] + total[8:16]

    fetch(0, 0).start()
    fetch(1, 1).start()
    fetch(0, 0).wait()
    gather(0, 0)

    def ring(i, _):
        @pl.when(i < CHUNKS // 2 - 1)
        def _():
            fetch(2 * i + 2, 0).start()
        fetch(2 * i + 1, 1).wait()
        gather(2 * i + 1, 1)
        add(2 * i, 0)

        @pl.when(i < CHUNKS // 2 - 1)
        def _():
            fetch(2 * i + 3, 1).start()
            fetch(2 * i + 2, 0).wait()
        gather(lax.rem(2 * i + 2, CHUNKS), 0)
        add(2 * i + 1, 1)
        return 0

    lax.fori_loop(0, CHUNKS // 2, ring, 0)

    row = lax.broadcasted_iota(jnp.int32, (8, 128), 0)
    for t in range(9):
        value = sums_ref[:, 128 * (t // 4):128 * (t // 4) + 128]
        if t % 4:
            value = pltpu.roll(value, 128 - NC_DEV * (t % 4), 1)
        part_ref[t] = jnp.where(lane < NC_DEV, value, 0.0)
    greeted()
    for t, _ in beside():
        mail.send(t, part_ref.at[t], got_ref.at[8 - t])
    total = part_ref[4]
    mail.wait()
    for t in range(9):
        if t != 4:
            total = total + got_ref[t]
    mass = 4.0 / 3.0 * math.pi * RADIUS**3
    inertia = 0.4 * mass * RADIUS**2
    new_ref[...] = motion_ref[...] + jnp.where(row < 3, total / mass, total / inertia)
    for t, _ in beside():
        mail.send(t, new_ref, back_ref.at[8 - t])
    report_ref[...] = jnp.where(row < 3, total, total / RADIUS)
    mail.wait()
    write_table(moved_ref, lambda t: new_ref[...] if t == 4 else back_ref[t])
    moved = split(moved_ref[...])[:, 0:SLOTS]

    def group(b, _):
        rows = pl.ds(pl.multiple_of(b * 8, 8), 8)
        for pair in range(4):
            found_at(moved, onehot_ref[b, :, 256 * pair:256 * pair + 256], pair, at_ref)
        value = pop_ref[rows, :]
        for i in range(6):
            value = value - gain_ref[i, rows, :] * at_ref[pl.ds(i, 8, stride=8), :]
        out_ref[rows, :] = value
        return 0

    lax.fori_loop(0, CHUNKS, group, 0)


VM = pl.BlockSpec(memory_space=pltpu.VMEM)


def links(row, site, direction, ids, pop, rb, q, table, motion):
    small = pltpu.VMEM((9, 8, 128), jnp.float32)
    wide = pltpu.VMEM((8, SLOTS_PAD), jnp.float32)
    column = pltpu.VMEM((64, 128), jnp.float32)
    return pl.pallas_call(
        links_kernel,
        in_specs=[pl.BlockSpec(memory_space=pl.ANY)] + [VM] * 9,
        out_specs=(VM, VM),
        out_shape=(jax.ShapeDtypeStruct((8, 128), jnp.float32), jax.ShapeDtypeStruct((LINKS // 128, 128), jnp.float32)),
        scratch_shapes=[
            pltpu.VMEM((8, 128), jnp.int32), pltpu.VMEM((6, LINKS // 128, 128), jnp.float32), wide,
            pltpu.VMEM((CHUNKS, SLOTS, CHUNK), jnp.bfloat16), column, column,
            [pltpu.VMEM((8, 128), jnp.float32)] * 2, [pltpu.SMEM((CHUNK,), jnp.int32)] * 2,
            small, small, pltpu.VMEM((8, 128), jnp.float32), small, wide,
            pltpu.SemaphoreType.DMA((2,)), pltpu.SemaphoreType.DMA((16,)), pltpu.SemaphoreType.DMA((16,)),
        ],
        name="links",
        compiler_params=pltpu.CompilerParams(vmem_limit_bytes=40 * 2**20, collective_id=1, has_side_effects=True),
    )(row, site, direction, ids, pop, rb, q, table, lattice_table(), motion)


def shards(
    eps_field, charge, potential_start, colloid_vel, colloid_spin, link_dir, link_colloid, link_site, link_depth,
    link_pop, link_rb,
):
    flat = lambda a: a.reshape(LINKS // 128, 128)
    motion = jnp.pad(jnp.concatenate([colloid_vel, colloid_spin], axis=0), ((0, 2), (0, 128 - NC_DEV)))
    potential, q, table = relax(eps_field, charge, potential_start, motion)
    row = link_depth.reshape(-1) * TX + (link_site.reshape(-1) >> 7)
    rb = link_rb.reshape(3, LINKS // 128, 128)
    report, link_out = links(
        row, flat(link_site), flat(link_dir), flat(link_colloid), flat(link_pop), rb, q.reshape(NZ * TX, TY), table, motion
    )
    link_out = link_out.reshape(link_pop.shape)
    return potential, report[0:6, 0:NC_DEV], link_out


def solution(mesh):
    tile = P(None, "gx", "gy")
    owned = P(None, ("gx", "gy"))
    link = P("gx", "gy", None)
    return jax.shard_map(
        shards,
        mesh=mesh,
        in_specs=(tile, tile, tile, owned, owned, link, link, link, link, link, P(None, "gx", "gy", None)),
        out_specs=(tile, owned, link),
        check_vma=False,
    )
```

```python
import math

import jax
import jax.numpy as jnp
import numpy as np
from jax import lax
from jax.experimental import pallas as pl
from jax.experimental.pallas import tpu as pltpu
from jax.sharding import PartitionSpec as P

TILES_X, TILES_Y = 8, 16
NC_DEV = 32
LINKS = 32768
RADIUS = 8
SWEEPS = 6
OVER_RELAX = 1.6
NZ, TX, TY = 48, 64, 128
HALF = NZ // 2
GROUPS = HALF // 8
ROWS = 96
TOP = 16
UNROLL = 8
WU = 4


def beside():
    x, y = lax.axis_index("gx"), lax.axis_index("gy")
    for t in range(9):
        if t != 4:
            yield t, (lax.rem(x + t // 3 - 1 + TILES_X, TILES_X), lax.rem(y + t % 3 - 1 + TILES_Y, TILES_Y))


def greet():
    barrier = pltpu.get_barrier_semaphore()
    for _, device in beside():
        pl.semaphore_signal(barrier, inc=1, device_id=device, device_id_type=pl.DeviceIdType.MESH)
    return lambda: pl.semaphore_wait(barrier, 8)


class Mail:
    def __init__(self, send_sem, recv_sem):
        self.sems, self.count, self.copies, self.device = (send_sem, recv_sem), 0, [], dict(beside())

    def send(self, t, source, target):
        copy = pltpu.make_async_remote_copy(
            src_ref=source, dst_ref=target, send_sem=self.sems[0].at[self.count], recv_sem=self.sems[1].at[self.count],
            device_id=self.device[t], device_id_type=pl.DeviceIdType.MESH,
        )
        copy.start()
        self.count += 1
        self.copies.append(copy)

    def wait(self):
        for copy in self.copies:
            copy.wait()
        self.copies = []


def write_blocks(blocks_ref, block):
    for t in range(9):
        blocks_ref[8 * t:8 * t + 8, :] = block(t)


def relax_kernel(
    eps_ref, charge_ref, phi_ref, motion_ref, pot_ref, q_ref, table_ref,
    p_refs, e_refs, ps_refs, es_refs, gs_refs, seam_refs, c_refs, coef_refs, cs_refs, coefs_refs,
    to_low, to_high, from_low, from_high, x_eps, x_charge, x_phi, to2_low, to2_high, from2_low, from2_high, x2_refs,
    got_ref, send_sem, recv_sem,
):
    sub = lax.broadcasted_iota(jnp.int32, (8, 128), 0)
    lane = lax.broadcasted_iota(jnp.int32, (8, 128), 1)
    even = (sub + lane) % 2 == 0
    odd = ~even
    first = lane % 16 < 8
    slot = lane // 16
    zero = jnp.zeros((8, 128), jnp.float32)
    blocks = range(8, ROWS - 8, 8)
    greeted = greet()
    mail = Mail(send_sem, recv_sem)

    def pack(plane, low_ref, high_ref, at):
        def group(g, _):
            for r in range(0, TX, 16):
                low, high = [zero, zero], [zero, zero]
                for k in range(16):
                    rows = plane(g, k, r)
                    for h in (0, 1):
                        value = rows[h]
                        here = lane // 8 == k
                        low[h] = jnp.where(here, pltpu.roll(value, 8 * k, 1) if k else value, low[h])
                        high[h] = jnp.where(here, pltpu.roll(value, 8 * (k + 1), 1) if k < 15 else value, high[h])
                for h in (0, 1):
                    low_ref[at + g, r + 8 * h:r + 8 * h + 8, :] = low[h]
                    high_ref[at + g, r + 8 * h:r + 8 * h + 8, :] = high[h]
            return 0
        lax.fori_loop(0, GROUPS, group, 0)

    def send_sides(low_ref, high_ref, dst_low, dst_high, at):
        span = pl.ds(at, GROUPS)
        for t, rows, target in ((3, (0, TX), 8), (0, (0, 8), 72), (6, (TX - 8, 8), 0)):
            mail.send(t, low_ref.at[span, pl.ds(*rows), :], dst_high.at[span, pl.ds(target, rows[1]), :])
            mail.send(t + 2, high_ref.at[span, pl.ds(*rows), :], dst_low.at[span, pl.ds(target, rows[1]), :])

    def natural(ref):
        def plane(g, k, r):
            value = ref[16 * g + k, r:r + 16, :].astype(jnp.float32)
            return value[0:8], value[8:16]
        return plane

    def send_rows(ref, target, rows):
        mail.send(1, ref.at[:, pl.ds(0, rows), :], target.at[1])
        mail.send(7, ref.at[:, pl.ds(TX - rows, rows), :], target.at[0])

    pack(natural(eps_ref), to_low, to_high, GROUPS)
    greeted()
    send_sides(to_low, to_high, from_low, from_high, GROUPS)
    send_rows(eps_ref, x_eps, 16)
    send_rows(charge_ref, x_charge, 8)
    pack(natural(charge_ref), to_low, to_high, 2 * GROUPS)
    send_sides(to_low, to_high, from_low, from_high, 2 * GROUPS)
    early, mail.copies = mail.copies, []
    send_rows(phi_ref, x_phi, 8)
    pack(natural(phi_ref), to_low, to_high, 0)
    send_sides(to_low, to_high, from_low, from_high, 0)
    for t, _ in beside():
        mail.send(t, motion_ref, got_ref.at[8 - t])

    def clear(m, _):
        for ref in (*p_refs, *e_refs):
            for g in (0, ROWS - 8):
                ref[m, g:g + 8, :] = zero
        return 0
    lax.fori_loop(0, HALF + 2, clear, 0)
    for ref in p_refs:
        for g in blocks:
            ref[0, g:g + 8, :] = zero
            ref[HALF + 1, g:g + 8, :] = zero
    for ref in (*ps_refs, *es_refs):
        for g in (0, ROWS - 8):
            for m in range(GROUPS + 2):
                ref[m, g:g + 8, :] = zero
    for ref in ps_refs:
        for g in blocks:
            ref[0, g:g + 8, :] = zero
            ref[GROUPS + 1, g:g + 8, :] = zero

    def two(refs, m, rows, a, b):
        refs[0][m, rows, :] = jnp.where(even, a, b)
        refs[1][m, rows, :] = jnp.where(even, b, a)

    def compact(m, _):
        for r in range(0, TX, 16):
            a = eps_ref[2 * m, r:r + 16, :].astype(jnp.float32)
            b = eps_ref[2 * m + 1, r:r + 16, :].astype(jnp.float32)
            for h in (0, 8):
                two(e_refs, m + 1, slice(TOP + r + h, TOP + r + h + 8), a[h:h + 8], b[h:h + 8])
        for r in range(0, TX, 8):
            two(p_refs, m + 1, slice(TOP + r, TOP + r + 8), phi_ref[2 * m, r:r + 8, :], phi_ref[2 * m + 1, r:r + 8, :])
        return 0
    lax.fori_loop(0, HALF, compact, 0)

    for copy in early:
        copy.wait()

    def edges(m, _):
        for side, g in ((0, 8), (1, TOP + TX)):
            rows = slice(8, 16) if side == 0 else slice(0, 8)
            a = x_eps[side, 2 * m].astype(jnp.float32)[rows]
            b = x_eps[side, 2 * m + 1].astype(jnp.float32)[rows]
            two(e_refs, m + 1, slice(g, g + 8), a, b)
        return 0
    lax.fori_loop(0, HALF, edges, 0)

    def unpacked(low_ref, high_ref, at, r):
        low, high = low_ref[at, r:r + 8, :], high_ref[at, r:r + 8, :]
        return jnp.where(first, low, pltpu.roll(high, 8, 1)), jnp.where(first, pltpu.roll(low, 120, 1), high)

    def strips(g, _):
        for r in range(0, TX + 16, 8):
            rows = slice(8 + r, 16 + r)
            two(es_refs, g + 1, rows, *unpacked(from_low, from_high, GROUPS + g, r))
            two(gs_refs, g, slice(r, r + 8), *unpacked(from_low, from_high, 2 * GROUPS + g, r))
        return 0
    lax.fori_loop(0, GROUPS, strips, 0)
    for g in blocks:
        rows = slice(g, g + 8)
        for c in (0, 1):
            e_refs[1 - c][0, rows, :] = e_refs[c][1, rows, :]
            e_refs[1 - c][HALF + 1, rows, :] = e_refs[c][HALF, rows, :]
            es_refs[1 - c][0, rows, :] = pltpu.roll(es_refs[c][1, rows, :], 112, 1)
            es_refs[1 - c][GROUPS + 1, rows, :] = pltpu.roll(es_refs[c][GROUPS, rows, :], 16, 1)

    def turn(seam_ref, n, g, value):
        for k in range(8):
            seam_ref[8 * n + k, g - 8:g, :] = pltpu.roll(value, 120 - 16 * k, 1)

    def turn_all(strip_refs):
        def one(n, _):
            for g in blocks:
                for c in (0, 1):
                    turn(seam_refs[c], n, g, strip_refs[c][n + 1, g:g + 8, :])
            return 0
        lax.fori_loop(0, GROUPS, one, 0)

    def main_sides(ref, seam_ref, m, g, low):
        rows = slice(g, g + 8)
        here = ref[m + 1, rows, :]
        seam = seam_ref[m, g - 8:g, :]
        return (
            here,
            jnp.where(low, ref[m, rows, :], ref[m + 2, rows, :]),
            ref[m + 1, g - 1:g + 7, :],
            ref[m + 1, g + 1:g + 9, :],
            pltpu.roll(jnp.where(lane == 127, seam, here), 1, 1),
            pltpu.roll(jnp.where(lane == 0, seam, here), 127, 1),
        )

    def strip_sides(ref, strip_ref, n, g, low):
        rows = slice(g, g + 8)
        here = strip_ref[n + 1, rows, :]
        seam = zero
        for k in range(8):
            seam = jnp.where(slot == k, pltpu.roll(ref[8 * n + k + 1, rows, :], 16 * k + 8, 1), seam)
        below = pltpu.roll(jnp.where(slot == 7, strip_ref[n, rows, :], here), 16, 1)
        above = pltpu.roll(jnp.where(slot == 0, strip_ref[n + 2, rows, :], here), 112, 1)
        return (
            here,
            jnp.where(low, below, above),
            strip_ref[n + 1, g - 1:g + 7, :],
            strip_ref[n + 1, g + 1:g + 9, :],
            pltpu.roll(jnp.where(lane % 16 == 7, seam, here), 1, 1),
            pltpu.roll(jnp.where(lane % 16 == 8, seam, here), 127, 1),
        )

    turn_all(es_refs)

    def weights(centre, sides, charge, c_ref, coef_ref, m, g):
        faces = [0.5 * (centre + side) for side in sides]
        total = faces[0]
        for face in faces[1:]:
            total = total + face
        scale = OVER_RELAX / total
        c_ref[m, g - 8:g, :] = scale * charge
        for i in range(6):
            coef_ref[i, m, g - 8:g, :] = scale * faces[i]

    for c in (0, 1):
        low = odd if c else even

        def main_weights(n, _):
            for k in range(WU):
                m = WU * n + k
                for g in blocks:
                    if g == 8:
                        a, b = x_charge[0, 2 * m], x_charge[0, 2 * m + 1]
                    elif g == TOP + TX:
                        a, b = x_charge[1, 2 * m], x_charge[1, 2 * m + 1]
                    else:
                        a, b = charge_ref[2 * m, g - TOP:g - TOP + 8, :], charge_ref[2 * m + 1, g - TOP:g - TOP + 8, :]
                    sides = main_sides(e_refs[1 - c], seam_refs[1 - c], m, g, low)
                    weights(e_refs[c][m + 1, g:g + 8, :], sides, jnp.where(low, a, b), c_refs[c], coef_refs[c], m, g)
            return 0
        lax.fori_loop(0, HALF // WU, main_weights, 0)

        def strip_weights(n, _):
            for g in blocks:
                sides = strip_sides(e_refs[1 - c], es_refs[1 - c], n, g, low)
                weights(es_refs[c][n + 1, g:g + 8, :], sides, gs_refs[c][n, g - 8:g, :], cs_refs[c], coefs_refs[c], n, g)
            return 0
        lax.fori_loop(0, GROUPS, strip_weights, 0)

    def updated(own, sides, c_ref, coef_ref, m, g):
        parts = [coef_ref[i, m, g - 8:g, :] * side for i, side in enumerate(sides)]
        first_part = c_ref[m, g - 8:g, :] - (OVER_RELAX - 1.0) * own
        return ((first_part + parts[0]) + (parts[1] + parts[2])) + (parts[3] + (parts[4] + parts[5]))

    def step(c, inner):
        low = odd if c else even

        def main_step(n, _):
            for k in range(UNROLL):
                m = UNROLL * n + k
                chosen = blocks[1:-1] if inner else blocks
                values = []
                for g in chosen:
                    sides = main_sides(p_refs[1 - c], seam_refs[1 - c], m, g, low)
                    values.append(updated(p_refs[c][m + 1, g:g + 8, :], sides, c_refs[c], coef_refs[c], m, g))
                for g, value in zip(chosen, values):
                    p_refs[c][m + 1, g:g + 8, :] = value
            return 0
        lax.fori_loop(0, HALF // UNROLL, main_step, 0)
        if inner:
            return

        def strip_step(n, _):
            for g in blocks:
                sides = strip_sides(p_refs[1 - c], ps_refs[1 - c], n, g, low)
                value = updated(ps_refs[c][n + 1, g:g + 8, :], sides, cs_refs[c], coefs_refs[c], n, g)
                ps_refs[c][n + 1, g:g + 8, :] = value
                turn(seam_refs[c], n, g, value)
            return 0
        lax.fori_loop(0, GROUPS, strip_step, 0)

    mail.wait()
    write_blocks(table_ref, lambda t: motion_ref[...] if t == 4 else got_ref[t])

    def edges1(m, _):
        for side, g in ((0, 8), (1, TOP + TX)):
            two(p_refs, m + 1, slice(g, g + 8), x_phi[side, 2 * m], x_phi[side, 2 * m + 1])
        return 0
    lax.fori_loop(0, HALF, edges1, 0)

    def strips1(g, _):
        for r in range(0, TX + 16, 8):
            two(ps_refs, g + 1, slice(8 + r, 16 + r), *unpacked(from_low, from_high, g, r))
        return 0
    lax.fori_loop(0, GROUPS, strips1, 0)
    turn_all(ps_refs)

    def three(i, _):
        step(0, False)
        step(1, False)
        return 0
    lax.fori_loop(0, 3, three, 0)
    step(0, False)

    def send_rows2(c):
        mail.send(1, p_refs[c].at[pl.ds(1, HALF), pl.ds(TOP, 8), :], x2_refs[c].at[1])
        mail.send(7, p_refs[c].at[pl.ds(1, HALF), pl.ds(TOP + TX - 8, 8), :], x2_refs[c].at[0])

    send_rows2(0)
    step(1, True)

    def coloured(g, k, r):
        value = p_refs[k % 2][8 * g + k // 2 + 1, TOP + r:TOP + r + 16, :]
        return value[0:8], value[8:16]

    send_rows2(1)
    pack(coloured, to2_low, to2_high, 0)
    send_sides(to2_low, to2_high, from2_low, from2_high, 0)
    mail.wait()

    def edges2(m, _):
        for c in (0, 1):
            p_refs[c][m + 1, 8:16, :] = x2_refs[c][0, m]
            p_refs[c][m + 1, TOP + TX:TOP + TX + 8, :] = x2_refs[c][1, m]
        return 0
    lax.fori_loop(0, HALF, edges2, 0)

    def strips2(g, _):
        for r in range(0, TX + 16, 8):
            a, b = unpacked(from2_low, from2_high, g, r)
            ps_refs[0][g + 1, 8 + r:16 + r, :] = a
            ps_refs[1][g + 1, 8 + r:16 + r, :] = b
        return 0
    lax.fori_loop(0, GROUPS, strips2, 0)
    turn_all(ps_refs)
    step(0, False)
    step(1, False)
    step(0, False)
    step(1, True)

    def out(m, _):
        for g in range(0, TX, 8):
            a, b = [ref[m + 1, TOP + g:TOP + g + 8, :] for ref in p_refs]
            ea, eb = [ref[m + 1, TOP + g:TOP + g + 8, :] for ref in e_refs]
            lo, hi = jnp.where(even, a, b), jnp.where(even, b, a)
            elo, ehi = jnp.where(even, ea, eb), jnp.where(even, eb, ea)
            pot_ref[2 * m, g:g + 8, :] = lo
            pot_ref[2 * m + 1, g:g + 8, :] = hi
            q_ref[2 * m, g:g + 8, :] = 0.5 * elo * lo * lo
            q_ref[2 * m + 1, g:g + 8, :] = 0.5 * ehi * hi * hi
        return 0
    lax.fori_loop(0, HALF, out, 0)


def relax(eps, charge, phi, motion):
    vm = lambda *s: pltpu.VMEM(s, jnp.float32)
    spec = pl.BlockSpec(memory_space=pltpu.VMEM)
    return pl.pallas_call(
        relax_kernel,
        out_shape=(
            jax.ShapeDtypeStruct((NZ, TX, TY), jnp.float32),
            jax.ShapeDtypeStruct((NZ, TX, TY), jnp.float32),
            jax.ShapeDtypeStruct((72, 128), jnp.float32),
        ),
        in_specs=[spec] * 4,
        out_specs=(spec,) * 3,
        scratch_shapes=[
            [vm(HALF + 2, ROWS, 128)] * 2,
            [vm(HALF + 2, ROWS, 128)] * 2,
            [vm(GROUPS + 2, ROWS, 128)] * 2,
            [vm(GROUPS + 2, ROWS, 128)] * 2,
            [vm(GROUPS, ROWS - 16, 128)] * 2,
            [vm(HALF, ROWS - 16, 128)] * 2,
            [vm(HALF, ROWS - 16, 128)] * 2,
            [vm(6, HALF, ROWS - 16, 128)] * 2,
            [vm(GROUPS, ROWS - 16, 128)] * 2,
            [vm(6, GROUPS, ROWS - 16, 128)] * 2,
            vm(3 * GROUPS, TX, 128), vm(3 * GROUPS, TX, 128),
            vm(3 * GROUPS, TX + 16, 128), vm(3 * GROUPS, TX + 16, 128),
            pltpu.VMEM((2, NZ, 16, 128), jnp.bfloat16), vm(2, NZ, 8, 128), vm(2, NZ, 8, 128),
            vm(GROUPS, TX, 128), vm(GROUPS, TX, 128),
            vm(GROUPS, TX + 16, 128), vm(GROUPS, TX + 16, 128),
            [vm(2, HALF, 8, 128)] * 2,
            vm(9, 8, 128),
            pltpu.SemaphoreType.DMA((42,)), pltpu.SemaphoreType.DMA((42,)),
        ],
        name="relax",
        compiler_params=pltpu.CompilerParams(vmem_limit_bytes=58 * 2**20, collective_id=0, has_side_effects=True),
    )(eps, charge, phi, motion)


CHUNK = 1024
CHUNKS = LINKS // CHUNK
RING = 4
FINAL = 8
VELOCITY = np.array(
    [[1, 0, 0], [-1, 0, 0], [0, 1, 0], [0, -1, 0], [0, 0, 1], [0, 0, -1], [1, 1, 0], [1, -1, 0], [-1, 1, 0],
     [-1, -1, 0], [1, 0, 1], [1, 0, -1], [-1, 0, 1], [-1, 0, -1], [0, 1, 1], [0, 1, -1], [0, -1, 1], [0, -1, -1]],
    dtype=np.float32,
).T
WEIGHT = np.array([1.0 / 18.0] * 6 + [1.0 / 36.0] * 12, dtype=np.float32)


def lattice_table():
    rows = np.zeros((4, 8, 128), np.float32)
    rows[0:3, :, 0:18] = VELOCITY[:, None, :]
    rows[3, :, 0:18] = WEIGHT[None, :]
    return jnp.asarray(rows.reshape(32, 128))


def cross(first, second):
    return (
        first[1] * second[2] - first[2] * second[1],
        first[2] * second[0] - first[0] * second[2],
        first[0] * second[1] - first[1] * second[0],
    )


def decode(lat_ref, direction):
    return [jnp.take_along_axis(lat_ref[8 * i:8 * i + 8, :], direction, axis=1) for i in range(4)]


def pair_of(slot_ref, base, pair):
    slots = jnp.concatenate([slot_ref[pl.ds(base + 2 * pair + h, 1), :] for h in (0, 1)], axis=1)
    colloid = lax.broadcasted_iota(jnp.int32, (NC_DEV, 256), 0) == (slots & (NC_DEV - 1))
    return slots >> 5, colloid.astype(jnp.float32)


def block_table(block):
    rows = []
    for t in range(9):
        value = block(t)
        high = value.astype(jnp.bfloat16).astype(jnp.float32)
        rows.append(high + pltpu.roll(value - high, NC_DEV, 1))
    rows.append(jnp.zeros((8, 128), jnp.float32))
    return jnp.concatenate(rows, axis=0).astype(jnp.bfloat16)[:, 0:2 * NC_DEV]


def found_at(table, slot_ref, base, at_ref):
    for pair in range(4):
        near, colloid = pair_of(slot_ref, base, pair)
        onehot = jnp.concatenate([colloid, colloid], axis=0).astype(jnp.bfloat16)
        every = jnp.dot(table, onehot, preferred_element_type=jnp.float32)
        found = jnp.zeros((8, 256), jnp.float32)
        for t in range(9):
            found = jnp.where(near == t, every[8 * t:8 * t + 8], found)
        at_ref[16 * pair:16 * pair + 8, :] = found[:, 0:128]
        at_ref[16 * pair + 8:16 * pair + 16, :] = found[:, 128:256]


def links_kernel(
    row_ref, site_ref, dir_ref, ids_ref, pop_ref, rb_ref, q_ref, table_ref, lat_ref, motion_ref, report_ref, out_ref,
    slot_ref, slots_refs, gain_ref, sums_ref, at_refs, term_refs, press_refs, index_refs,
    part_ref, got_ref, new_ref, back_ref, index_sem, send_sem, recv_sem,
):
    greeted = greet()
    mail = Mail(send_sem, recv_sem)
    home_x = lax.axis_index("gx")
    home_y = lax.axis_index("gy")
    lane = lax.broadcasted_iota(jnp.int32, (8, 128), 1)
    sub = lax.broadcasted_iota(jnp.int32, (8, 128), 0)

    def fetch(b, k):
        rows = row_ref.at[pl.ds(pl.multiple_of(b * CHUNK, CHUNK), CHUNK)]
        return pltpu.make_async_copy(rows, index_refs[k], index_sem.at[k])

    def gather(b, k):
        column = site_ref[pl.ds(pl.multiple_of(b * 8, 8), 8), :] & 127
        pressure = jnp.zeros((8, 128), jnp.float32)
        for j in range(128):
            at = lambda s: jnp.broadcast_to(q_ref[pl.ds(index_refs[k][s * 128 + j], 1), :], (8, 128))
            picked = at(0)
            for s in range(1, 8):
                picked = jnp.where(sub == s, at(s), picked)
            pressure = jnp.where(lane == j, jnp.take_along_axis(picked, column, axis=1), pressure)
        press_refs[k][...] = pressure

    sums_ref[...] = jnp.zeros_like(sums_ref)
    for term_ref in term_refs:
        term_ref[...] = jnp.zeros_like(term_ref)
    table = block_table(lambda t: table_ref[8 * t:8 * t + 8, :])

    def place(b, k):
        rows = pl.ds(pl.multiple_of(b * 8, 8), 8)
        ids = ids_ref[rows, :]
        owner = ids >> 5
        near_x = ((owner >> 4) - home_x + 1) & (TILES_X - 1)
        near_y = ((owner & (TILES_Y - 1)) - home_y + 1) & (TILES_Y - 1)
        slots = jnp.where(ids >= 0, (near_x * 3 + near_y) * NC_DEV + (ids & (NC_DEV - 1)), -1)
        slot_ref[rows, :] = slots
        slots_refs[k][...] = slots

    def terms_of(b, k):
        rows = pl.ds(pl.multiple_of(b * 8, 8), 8)
        *velocity, weight = decode(lat_ref, dir_ref[rows, :])
        offsets = [rb_ref[i, rows, :] for i in range(3)]
        arms = (*velocity, *cross(offsets, velocity))
        live = slots_refs[k][...] >= 0
        scale = jnp.where(live, 6.0 * weight, 0.0)
        source = jnp.where(live, 2.0 * pop_ref[rows, :] + weight * press_refs[k][...], 0.0)
        for i, arm in enumerate(arms):
            gain = scale * arm
            gain_ref[i, rows, :] = gain
            source = source - gain * at_refs[k][pl.ds(i, 8, stride=8), :]
        for i, arm in enumerate(arms):
            term_refs[k][pl.ds(i, 8, stride=8), :] = arm * source

    def summed(k, total):
        for pair in range(4):
            near, colloid = pair_of(slots_refs[k], 0, pair)
            terms = [term_refs[k][16 * pair + 8 * h:16 * pair + 8 * h + 8, :] for h in (0, 1)]
            terms = jnp.concatenate(terms, axis=1)
            high = terms.astype(jnp.bfloat16).astype(jnp.float32)
            both = jnp.concatenate([high, terms - high], axis=0)
            spread = jnp.concatenate([jnp.where(near == t, both, 0.0) for t in range(9)], axis=0).astype(jnp.bfloat16)
            total = total + lax.dot_general(
                spread, colloid.astype(jnp.bfloat16), (((1,), (1,)), ((), ())), preferred_element_type=jnp.float32
            )
        return total

    for k in range(RING):
        fetch(k, k).start()

    def ring(i, _):
        first = i * RING
        for k in range(RING):
            fetch(first + k, k).wait()
        for k in range(RING):
            gather(first + k, k)

        @pl.when(i < CHUNKS // RING - 1)
        def _():
            for k in range(RING):
                fetch(first + RING + k, k).start()
        for k in range(RING):
            place(first + k, k)
        for k in range(RING):
            found_at(table, slots_refs[k], 0, at_refs[k])
        for k in range(RING):
            terms_of(first + k, k)
        total = jnp.zeros((144, NC_DEV), jnp.float32)
        for k in range(RING):
            total = summed(k, total)
        sums_ref[:, 0:NC_DEV] += total
        return 0

    lax.fori_loop(0, CHUNKS // RING, ring, 0)

    row = lax.broadcasted_iota(jnp.int32, (8, 128), 0)
    for t in range(9):
        part_ref[t] = sums_ref[16 * t:16 * t + 8, :] + sums_ref[16 * t + 8:16 * t + 16, :]
    greeted()
    for t, _ in beside():
        mail.send(t, part_ref.at[t], got_ref.at[8 - t])
    total = part_ref[4]
    mail.wait()
    for t in range(9):
        if t != 4:
            total = total + got_ref[t]
    mass = 4.0 / 3.0 * math.pi * RADIUS**3
    inertia = 0.4 * mass * RADIUS**2
    new_ref[...] = motion_ref[...] + jnp.where(row < 3, total / mass, total / inertia)
    for t, _ in beside():
        mail.send(t, new_ref, back_ref.at[8 - t])
    report_ref[...] = jnp.where(row < 3, total, total / RADIUS)
    mail.wait()
    moved = block_table(lambda t: new_ref[...] if t == 4 else back_ref[t])

    def group(i, _):
        for k in range(FINAL):
            found_at(moved, slot_ref, pl.multiple_of((i * FINAL + k) * 8, 8), at_refs[k])
        for k in range(FINAL):
            rows = pl.ds(pl.multiple_of((i * FINAL + k) * 8, 8), 8)
            value = pop_ref[rows, :]
            for j in range(6):
                value = value - gain_ref[j, rows, :] * at_refs[k][pl.ds(j, 8, stride=8), :]
            out_ref[rows, :] = value
        return 0

    lax.fori_loop(0, CHUNKS // FINAL, group, 0)


VM = pl.BlockSpec(memory_space=pltpu.VMEM)


def links(row, site, direction, ids, pop, rb, q, table, motion):
    small = pltpu.VMEM((9, 8, 128), jnp.float32)
    column = pltpu.VMEM((64, 128), jnp.float32)
    return pl.pallas_call(
        links_kernel,
        in_specs=[pl.BlockSpec(memory_space=pl.ANY)] + [VM] * 9,
        out_specs=(VM, VM),
        out_shape=(jax.ShapeDtypeStruct((8, 128), jnp.float32), jax.ShapeDtypeStruct((LINKS // 128, 128), jnp.float32)),
        scratch_shapes=[
            pltpu.VMEM((LINKS // 128, 128), jnp.int32), [pltpu.VMEM((8, 128), jnp.int32)] * RING, pltpu.VMEM((6, LINKS // 128, 128), jnp.float32),
            pltpu.VMEM((144, 128), jnp.float32), [column] * max(RING, FINAL), [column] * RING,
            [pltpu.VMEM((8, 128), jnp.float32)] * RING, [pltpu.SMEM((CHUNK,), jnp.int32)] * RING,
            small, small, pltpu.VMEM((8, 128), jnp.float32), small,
            pltpu.SemaphoreType.DMA((RING,)), pltpu.SemaphoreType.DMA((16,)), pltpu.SemaphoreType.DMA((16,)),
        ],
        name="links",
        compiler_params=pltpu.CompilerParams(vmem_limit_bytes=40 * 2**20, collective_id=1, has_side_effects=True),
    )(row, site, direction, ids, pop, rb, q, table, lattice_table(), motion)


def shards(
    eps_field, charge, potential_start, colloid_vel, colloid_spin, link_dir, link_colloid, link_site, link_depth,
    link_pop, link_rb,
):
    flat = lambda a: a.reshape(LINKS // 128, 128)
    motion = jnp.pad(jnp.concatenate([colloid_vel, colloid_spin], axis=0), ((0, 2), (0, 128 - NC_DEV)))
    potential, q, table = relax(eps_field, charge, potential_start, motion)
    row = link_depth.reshape(-1) * TX + (link_site.reshape(-1) >> 7)
    rb = link_rb.reshape(3, LINKS // 128, 128)
    report, link_out = links(
        row, flat(link_site), flat(link_dir), flat(link_colloid), flat(link_pop), rb, q.reshape(NZ * TX, TY), table, motion
    )
    link_out = link_out.reshape(link_pop.shape)
    return potential, report[0:6, 0:NC_DEV], link_out


def solution(mesh):
    tile = P(None, "gx", "gy")
    owned = P(None, ("gx", "gy"))
    link = P("gx", "gy", None)
    return jax.shard_map(
        shards,
        mesh=mesh,
        in_specs=(tile, tile, tile, owned, owned, link, link, link, link, link, P(None, "gx", "gy", None)),
        out_specs=(tile, owned, link),
        check_vma=False,
    )
```

```python
import math

import jax
import jax.numpy as jnp
import numpy as np
from jax import lax
from jax.experimental import pallas as pl
from jax.experimental.pallas import tpu as pltpu
from jax.sharding import PartitionSpec as P

TILES_X, TILES_Y = 8, 16
NC_DEV = 32
LINKS = 32768
RADIUS = 8
SWEEPS = 6
OVER_RELAX = 1.6
NZ, TX, TY = 48, 64, 128
HALF = NZ // 2
GROUPS = HALF // 8
ROWS = 96
TOP = 16
UNROLL = 8
WU = 4


def beside():
    x, y = lax.axis_index("gx"), lax.axis_index("gy")
    for t in range(9):
        if t != 4:
            yield t, (lax.rem(x + t // 3 - 1 + TILES_X, TILES_X), lax.rem(y + t % 3 - 1 + TILES_Y, TILES_Y))


def greet():
    barrier = pltpu.get_barrier_semaphore()
    for _, device in beside():
        pl.semaphore_signal(barrier, inc=1, device_id=device, device_id_type=pl.DeviceIdType.MESH)
    return lambda: pl.semaphore_wait(barrier, 8)


class Mail:
    def __init__(self, send_sem, recv_sem):
        self.sems, self.count, self.copies, self.device = (send_sem, recv_sem), 0, [], dict(beside())

    def send(self, t, source, target):
        copy = pltpu.make_async_remote_copy(
            src_ref=source, dst_ref=target, send_sem=self.sems[0].at[self.count], recv_sem=self.sems[1].at[self.count],
            device_id=self.device[t], device_id_type=pl.DeviceIdType.MESH,
        )
        copy.start()
        self.count += 1
        self.copies.append(copy)

    def wait(self):
        for copy in self.copies:
            copy.wait()
        self.copies = []


def write_blocks(blocks_ref, block):
    for t in range(9):
        blocks_ref[8 * t:8 * t + 8, :] = block(t)


def relax_kernel(
    eps_ref, charge_ref, phi_ref, vel_ref, spin_ref, pot_ref, q_ref, table_ref,
    p_refs, e_refs, ps_refs, es_refs, gs_refs, seam_refs, c_refs, coef_refs, cs_refs, coefs_refs,
    to_low, to_high, from_low, from_high, x_eps, x_charge, x_phi, to2_low, to2_high, from2_low, from2_high, x2_refs,
    motion_ref, got_ref, send_sem, recv_sem,
):
    sub = lax.broadcasted_iota(jnp.int32, (8, 128), 0)
    lane = lax.broadcasted_iota(jnp.int32, (8, 128), 1)
    even = (sub + lane) % 2 == 0
    odd = ~even
    first = lane % 16 < 8
    slot = lane // 16
    zero = jnp.zeros((8, 128), jnp.float32)
    blocks = range(8, ROWS - 8, 8)
    greeted = greet()
    mail = Mail(send_sem, recv_sem)

    def pack(plane, low_ref, high_ref, at):
        def group(g, _):
            for r in range(0, TX, 16):
                low, high = [zero, zero], [zero, zero]
                for k in range(16):
                    rows = plane(g, k, r)
                    for h in (0, 1):
                        value = rows[h]
                        here = lane // 8 == k
                        low[h] = jnp.where(here, pltpu.roll(value, 8 * k, 1) if k else value, low[h])
                        high[h] = jnp.where(here, pltpu.roll(value, 8 * (k + 1), 1) if k < 15 else value, high[h])
                for h in (0, 1):
                    low_ref[at + g, r + 8 * h:r + 8 * h + 8, :] = low[h]
                    high_ref[at + g, r + 8 * h:r + 8 * h + 8, :] = high[h]
            return 0
        lax.fori_loop(0, GROUPS, group, 0)

    def send_sides(low_ref, high_ref, dst_low, dst_high, at):
        span = pl.ds(at, GROUPS)
        for t, rows, target in ((3, (0, TX), 8), (0, (0, 8), 72), (6, (TX - 8, 8), 0)):
            mail.send(t, low_ref.at[span, pl.ds(*rows), :], dst_high.at[span, pl.ds(target, rows[1]), :])
            mail.send(t + 2, high_ref.at[span, pl.ds(*rows), :], dst_low.at[span, pl.ds(target, rows[1]), :])

    def natural(ref):
        def plane(g, k, r):
            value = ref[16 * g + k, r:r + 16, :].astype(jnp.float32)
            return value[0:8], value[8:16]
        return plane

    def send_rows(ref, target, rows):
        mail.send(1, ref.at[:, pl.ds(0, rows), :], target.at[1])
        mail.send(7, ref.at[:, pl.ds(TX - rows, rows), :], target.at[0])

    motion_ref[...] = zero
    motion_ref[0:3, 0:NC_DEV] = vel_ref[...]
    motion_ref[3:6, 0:NC_DEV] = spin_ref[...]
    pack(natural(eps_ref), to_low, to_high, GROUPS)
    greeted()
    send_sides(to_low, to_high, from_low, from_high, GROUPS)
    send_rows(eps_ref, x_eps, 16)
    send_rows(charge_ref, x_charge, 8)
    pack(natural(charge_ref), to_low, to_high, 2 * GROUPS)
    send_sides(to_low, to_high, from_low, from_high, 2 * GROUPS)
    early, mail.copies = mail.copies, []
    send_rows(phi_ref, x_phi, 8)
    pack(natural(phi_ref), to_low, to_high, 0)
    send_sides(to_low, to_high, from_low, from_high, 0)
    for t, _ in beside():
        mail.send(t, motion_ref, got_ref.at[8 - t])

    def clear(m, _):
        for ref in (*p_refs, *e_refs):
            for g in (0, ROWS - 8):
                ref[m, g:g + 8, :] = zero
        return 0
    lax.fori_loop(0, HALF + 2, clear, 0)
    for ref in p_refs:
        for g in blocks:
            ref[0, g:g + 8, :] = zero
            ref[HALF + 1, g:g + 8, :] = zero
    for ref in (*ps_refs, *es_refs):
        for g in (0, ROWS - 8):
            for m in range(GROUPS + 2):
                ref[m, g:g + 8, :] = zero
    for ref in ps_refs:
        for g in blocks:
            ref[0, g:g + 8, :] = zero
            ref[GROUPS + 1, g:g + 8, :] = zero

    def two(refs, m, rows, a, b):
        refs[0][m, rows, :] = jnp.where(even, a, b)
        refs[1][m, rows, :] = jnp.where(even, b, a)

    def compact(m, _):
        for r in range(0, TX, 16):
            a = eps_ref[2 * m, r:r + 16, :].astype(jnp.float32)
            b = eps_ref[2 * m + 1, r:r + 16, :].astype(jnp.float32)
            for h in (0, 8):
                two(e_refs, m + 1, slice(TOP + r + h, TOP + r + h + 8), a[h:h + 8], b[h:h + 8])
        for r in range(0, TX, 8):
            two(p_refs, m + 1, slice(TOP + r, TOP + r + 8), phi_ref[2 * m, r:r + 8, :], phi_ref[2 * m + 1, r:r + 8, :])
        return 0
    lax.fori_loop(0, HALF, compact, 0)

    for copy in early:
        copy.wait()

    def edges(m, _):
        for side, g in ((0, 8), (1, TOP + TX)):
            rows = slice(8, 16) if side == 0 else slice(0, 8)
            a = x_eps[side, 2 * m].astype(jnp.float32)[rows]
            b = x_eps[side, 2 * m + 1].astype(jnp.float32)[rows]
            two(e_refs, m + 1, slice(g, g + 8), a, b)
        return 0
    lax.fori_loop(0, HALF, edges, 0)

    def unpacked(low_ref, high_ref, at, r):
        low, high = low_ref[at, r:r + 8, :], high_ref[at, r:r + 8, :]
        return jnp.where(first, low, pltpu.roll(high, 8, 1)), jnp.where(first, pltpu.roll(low, 120, 1), high)

    def strips(g, _):
        for r in range(0, TX + 16, 8):
            rows = slice(8 + r, 16 + r)
            two(es_refs, g + 1, rows, *unpacked(from_low, from_high, GROUPS + g, r))
            two(gs_refs, g, slice(r, r + 8), *unpacked(from_low, from_high, 2 * GROUPS + g, r))
        return 0
    lax.fori_loop(0, GROUPS, strips, 0)
    for g in blocks:
        rows = slice(g, g + 8)
        for c in (0, 1):
            e_refs[1 - c][0, rows, :] = e_refs[c][1, rows, :]
            e_refs[1 - c][HALF + 1, rows, :] = e_refs[c][HALF, rows, :]
            es_refs[1 - c][0, rows, :] = pltpu.roll(es_refs[c][1, rows, :], 112, 1)
            es_refs[1 - c][GROUPS + 1, rows, :] = pltpu.roll(es_refs[c][GROUPS, rows, :], 16, 1)

    def turn(seam_ref, n, g, value):
        for k in range(8):
            seam_ref[8 * n + k, g - 8:g, :] = pltpu.roll(value, 120 - 16 * k, 1)

    def turn_all(strip_refs):
        def one(n, _):
            for g in blocks:
                for c in (0, 1):
                    turn(seam_refs[c], n, g, strip_refs[c][n + 1, g:g + 8, :])
            return 0
        lax.fori_loop(0, GROUPS, one, 0)

    def main_sides(ref, seam_ref, m, g, low):
        rows = slice(g, g + 8)
        here = ref[m + 1, rows, :]
        seam = seam_ref[m, g - 8:g, :]
        return (
            here,
            jnp.where(low, ref[m, rows, :], ref[m + 2, rows, :]),
            ref[m + 1, g - 1:g + 7, :],
            ref[m + 1, g + 1:g + 9, :],
            pltpu.roll(jnp.where(lane == 127, seam, here), 1, 1),
            pltpu.roll(jnp.where(lane == 0, seam, here), 127, 1),
        )

    def strip_sides(ref, strip_ref, n, g, low):
        rows = slice(g, g + 8)
        here = strip_ref[n + 1, rows, :]
        seam = zero
        for k in range(8):
            seam = jnp.where(slot == k, pltpu.roll(ref[8 * n + k + 1, rows, :], 16 * k + 8, 1), seam)
        below = pltpu.roll(jnp.where(slot == 7, strip_ref[n, rows, :], here), 16, 1)
        above = pltpu.roll(jnp.where(slot == 0, strip_ref[n + 2, rows, :], here), 112, 1)
        return (
            here,
            jnp.where(low, below, above),
            strip_ref[n + 1, g - 1:g + 7, :],
            strip_ref[n + 1, g + 1:g + 9, :],
            pltpu.roll(jnp.where(lane % 16 == 7, seam, here), 1, 1),
            pltpu.roll(jnp.where(lane % 16 == 8, seam, here), 127, 1),
        )

    turn_all(es_refs)

    def weights(centre, sides, charge, c_ref, coef_ref, m, g):
        faces = [0.5 * (centre + side) for side in sides]
        total = faces[0]
        for face in faces[1:]:
            total = total + face
        scale = OVER_RELAX / total
        c_ref[m, g - 8:g, :] = scale * charge
        for i in range(6):
            coef_ref[i, m, g - 8:g, :] = scale * faces[i]

    for c in (0, 1):
        low = odd if c else even

        def main_weights(n, _):
            for k in range(WU):
                m = WU * n + k
                for g in blocks:
                    if g == 8:
                        a, b = x_charge[0, 2 * m], x_charge[0, 2 * m + 1]
                    elif g == TOP + TX:
                        a, b = x_charge[1, 2 * m], x_charge[1, 2 * m + 1]
                    else:
                        a, b = charge_ref[2 * m, g - TOP:g - TOP + 8, :], charge_ref[2 * m + 1, g - TOP:g - TOP + 8, :]
                    sides = main_sides(e_refs[1 - c], seam_refs[1 - c], m, g, low)
                    weights(e_refs[c][m + 1, g:g + 8, :], sides, jnp.where(low, a, b), c_refs[c], coef_refs[c], m, g)
            return 0
        lax.fori_loop(0, HALF // WU, main_weights, 0)

        def strip_weights(n, _):
            for g in blocks:
                sides = strip_sides(e_refs[1 - c], es_refs[1 - c], n, g, low)
                weights(es_refs[c][n + 1, g:g + 8, :], sides, gs_refs[c][n, g - 8:g, :], cs_refs[c], coefs_refs[c], n, g)
            return 0
        lax.fori_loop(0, GROUPS, strip_weights, 0)

    def updated(own, sides, c_ref, coef_ref, m, g):
        parts = [coef_ref[i, m, g - 8:g, :] * side for i, side in enumerate(sides)]
        first_part = c_ref[m, g - 8:g, :] - (OVER_RELAX - 1.0) * own
        return ((first_part + parts[0]) + (parts[1] + parts[2])) + (parts[3] + (parts[4] + parts[5]))

    def step(c, inner):
        low = odd if c else even

        def main_step(n, _):
            for k in range(UNROLL):
                m = UNROLL * n + k
                chosen = blocks[1:-1] if inner else blocks
                values = []
                for g in chosen:
                    sides = main_sides(p_refs[1 - c], seam_refs[1 - c], m, g, low)
                    values.append(updated(p_refs[c][m + 1, g:g + 8, :], sides, c_refs[c], coef_refs[c], m, g))
                for g, value in zip(chosen, values):
                    p_refs[c][m + 1, g:g + 8, :] = value
            return 0
        lax.fori_loop(0, HALF // UNROLL, main_step, 0)
        if inner:
            return

        def strip_step(n, _):
            for g in blocks:
                sides = strip_sides(p_refs[1 - c], ps_refs[1 - c], n, g, low)
                value = updated(ps_refs[c][n + 1, g:g + 8, :], sides, cs_refs[c], coefs_refs[c], n, g)
                ps_refs[c][n + 1, g:g + 8, :] = value
                turn(seam_refs[c], n, g, value)
            return 0
        lax.fori_loop(0, GROUPS, strip_step, 0)

    mail.wait()
    write_blocks(table_ref, lambda t: motion_ref[...] if t == 4 else got_ref[t])

    def edges1(m, _):
        for side, g in ((0, 8), (1, TOP + TX)):
            two(p_refs, m + 1, slice(g, g + 8), x_phi[side, 2 * m], x_phi[side, 2 * m + 1])
        return 0
    lax.fori_loop(0, HALF, edges1, 0)

    def strips1(g, _):
        for r in range(0, TX + 16, 8):
            two(ps_refs, g + 1, slice(8 + r, 16 + r), *unpacked(from_low, from_high, g, r))
        return 0
    lax.fori_loop(0, GROUPS, strips1, 0)
    turn_all(ps_refs)

    def three(i, _):
        step(0, False)
        step(1, False)
        return 0
    lax.fori_loop(0, 3, three, 0)
    step(0, False)

    def send_rows2(c):
        mail.send(1, p_refs[c].at[pl.ds(1, HALF), pl.ds(TOP, 8), :], x2_refs[c].at[1])
        mail.send(7, p_refs[c].at[pl.ds(1, HALF), pl.ds(TOP + TX - 8, 8), :], x2_refs[c].at[0])

    send_rows2(0)
    step(1, True)

    def coloured(g, k, r):
        value = p_refs[k % 2][8 * g + k // 2 + 1, TOP + r:TOP + r + 16, :]
        return value[0:8], value[8:16]

    send_rows2(1)
    pack(coloured, to2_low, to2_high, 0)
    send_sides(to2_low, to2_high, from2_low, from2_high, 0)
    mail.wait()

    def edges2(m, _):
        for c in (0, 1):
            p_refs[c][m + 1, 8:16, :] = x2_refs[c][0, m]
            p_refs[c][m + 1, TOP + TX:TOP + TX + 8, :] = x2_refs[c][1, m]
        return 0
    lax.fori_loop(0, HALF, edges2, 0)

    def strips2(g, _):
        for r in range(0, TX + 16, 8):
            a, b = unpacked(from2_low, from2_high, g, r)
            ps_refs[0][g + 1, 8 + r:16 + r, :] = a
            ps_refs[1][g + 1, 8 + r:16 + r, :] = b
        return 0
    lax.fori_loop(0, GROUPS, strips2, 0)
    turn_all(ps_refs)
    step(0, False)
    step(1, False)
    step(0, False)
    step(1, True)

    def out(m, _):
        for g in range(0, TX, 8):
            a, b = [ref[m + 1, TOP + g:TOP + g + 8, :] for ref in p_refs]
            ea, eb = [ref[m + 1, TOP + g:TOP + g + 8, :] for ref in e_refs]
            lo, hi = jnp.where(even, a, b), jnp.where(even, b, a)
            elo, ehi = jnp.where(even, ea, eb), jnp.where(even, eb, ea)
            pot_ref[2 * m, g:g + 8, :] = lo
            pot_ref[2 * m + 1, g:g + 8, :] = hi
            q_ref[2 * m, g:g + 8, :] = 0.5 * elo * lo * lo
            q_ref[2 * m + 1, g:g + 8, :] = 0.5 * ehi * hi * hi
        return 0
    lax.fori_loop(0, HALF, out, 0)


def relax(eps, charge, phi, vel, spin):
    vm = lambda *s: pltpu.VMEM(s, jnp.float32)
    spec = pl.BlockSpec(memory_space=pltpu.VMEM)
    return pl.pallas_call(
        relax_kernel,
        out_shape=(
            jax.ShapeDtypeStruct((NZ, TX, TY), jnp.float32),
            jax.ShapeDtypeStruct((NZ, TX, TY), jnp.float32),
            jax.ShapeDtypeStruct((72, 128), jnp.float32),
        ),
        in_specs=[spec] * 5,
        out_specs=(spec,) * 3,
        scratch_shapes=[
            [vm(HALF + 2, ROWS, 128)] * 2,
            [vm(HALF + 2, ROWS, 128)] * 2,
            [vm(GROUPS + 2, ROWS, 128)] * 2,
            [vm(GROUPS + 2, ROWS, 128)] * 2,
            [vm(GROUPS, ROWS - 16, 128)] * 2,
            [vm(HALF, ROWS - 16, 128)] * 2,
            [vm(HALF, ROWS - 16, 128)] * 2,
            [vm(6, HALF, ROWS - 16, 128)] * 2,
            [vm(GROUPS, ROWS - 16, 128)] * 2,
            [vm(6, GROUPS, ROWS - 16, 128)] * 2,
            vm(3 * GROUPS, TX, 128), vm(3 * GROUPS, TX, 128),
            vm(3 * GROUPS, TX + 16, 128), vm(3 * GROUPS, TX + 16, 128),
            pltpu.VMEM((2, NZ, 16, 128), jnp.bfloat16), vm(2, NZ, 8, 128), vm(2, NZ, 8, 128),
            vm(GROUPS, TX, 128), vm(GROUPS, TX, 128),
            vm(GROUPS, TX + 16, 128), vm(GROUPS, TX + 16, 128),
            [vm(2, HALF, 8, 128)] * 2,
            vm(8, 128), vm(9, 8, 128),
            pltpu.SemaphoreType.DMA((42,)), pltpu.SemaphoreType.DMA((42,)),
        ],
        name="relax",
        compiler_params=pltpu.CompilerParams(vmem_limit_bytes=58 * 2**20, collective_id=0, has_side_effects=True),
    )(eps, charge, phi, vel, spin)


CHUNK = 1024
CHUNKS = LINKS // CHUNK
RING = 8
FINAL = 8
VELOCITY = np.array(
    [[1, 0, 0], [-1, 0, 0], [0, 1, 0], [0, -1, 0], [0, 0, 1], [0, 0, -1], [1, 1, 0], [1, -1, 0], [-1, 1, 0],
     [-1, -1, 0], [1, 0, 1], [1, 0, -1], [-1, 0, 1], [-1, 0, -1], [0, 1, 1], [0, 1, -1], [0, -1, 1], [0, -1, -1]],
    dtype=np.float32,
).T
WEIGHT = np.array([1.0 / 18.0] * 6 + [1.0 / 36.0] * 12, dtype=np.float32)


def lattice_table():
    rows = np.zeros((4, 8, 128), np.float32)
    rows[0:3, :, 0:18] = VELOCITY[:, None, :]
    rows[3, :, 0:18] = WEIGHT[None, :]
    return jnp.asarray(rows.reshape(32, 128))


def cross(first, second):
    return (
        first[1] * second[2] - first[2] * second[1],
        first[2] * second[0] - first[0] * second[2],
        first[0] * second[1] - first[1] * second[0],
    )


def decode(lat_ref, direction):
    return [jnp.take_along_axis(lat_ref[8 * i:8 * i + 8, :], direction, axis=1) for i in range(4)]


def pair_of(slot_ref, base, pair):
    slots = jnp.concatenate([slot_ref[pl.ds(base + 2 * pair + h, 1), :] for h in (0, 1)], axis=1)
    colloid = lax.broadcasted_iota(jnp.int32, (NC_DEV, 256), 0) == (slots & (NC_DEV - 1))
    return slots >> 5, colloid.astype(jnp.float32)


def block_table(block):
    rows = []
    for t in range(9):
        value = block(t)
        high = value.astype(jnp.bfloat16).astype(jnp.float32)
        rows.append(high + pltpu.roll(value - high, NC_DEV, 1))
    rows.append(jnp.zeros((8, 128), jnp.float32))
    return jnp.concatenate(rows, axis=0).astype(jnp.bfloat16)[:, 0:2 * NC_DEV]


def found_at(table, slot_ref, base, at_ref):
    for pair in range(4):
        near, colloid = pair_of(slot_ref, base, pair)
        onehot = jnp.concatenate([colloid, colloid], axis=0).astype(jnp.bfloat16)
        every = jnp.dot(table, onehot, preferred_element_type=jnp.float32)
        found = jnp.zeros((8, 256), jnp.float32)
        for t in range(9):
            found = jnp.where(near == t, every[8 * t:8 * t + 8], found)
        at_ref[16 * pair:16 * pair + 8, :] = found[:, 0:128]
        at_ref[16 * pair + 8:16 * pair + 16, :] = found[:, 128:256]


def links_kernel(
    row_ref, site_ref, dir_ref, ids_ref, pop_ref, rb_ref, q_ref, table_ref, lat_ref, report_ref, out_ref,
    slot_ref, slots_refs, gain_ref, sums_ref, at_refs, term_refs, press_refs, index_refs,
    part_ref, got_ref, new_ref, back_ref, index_sem, send_sem, recv_sem,
):
    greeted = greet()
    mail = Mail(send_sem, recv_sem)
    home_x = lax.axis_index("gx")
    home_y = lax.axis_index("gy")
    lane = lax.broadcasted_iota(jnp.int32, (8, 128), 1)
    sub = lax.broadcasted_iota(jnp.int32, (8, 128), 0)

    def fetch(b, k):
        rows = row_ref.at[pl.ds(pl.multiple_of(b * CHUNK, CHUNK), CHUNK)]
        return pltpu.make_async_copy(rows, index_refs[k], index_sem.at[k])

    def gather(b, k):
        column = site_ref[pl.ds(pl.multiple_of(b * 8, 8), 8), :] & 127
        pressure = jnp.zeros((8, 128), jnp.float32)
        for j in range(128):
            at = lambda s: jnp.broadcast_to(q_ref[pl.ds(index_refs[k][s * 128 + j], 1), :], (8, 128))
            picked = at(0)
            for s in range(1, 8):
                picked = jnp.where(sub == s, at(s), picked)
            pressure = jnp.where(lane == j, jnp.take_along_axis(picked, column, axis=1), pressure)
        press_refs[k][...] = pressure

    sums_ref[...] = jnp.zeros_like(sums_ref)
    for term_ref in term_refs:
        term_ref[...] = jnp.zeros_like(term_ref)
    table = block_table(lambda t: table_ref[8 * t:8 * t + 8, :])

    def place(b, k):
        rows = pl.ds(pl.multiple_of(b * 8, 8), 8)
        ids = ids_ref[rows, :]
        owner = ids >> 5
        near_x = ((owner >> 4) - home_x + 1) & (TILES_X - 1)
        near_y = ((owner & (TILES_Y - 1)) - home_y + 1) & (TILES_Y - 1)
        slots = jnp.where(ids >= 0, (near_x * 3 + near_y) * NC_DEV + (ids & (NC_DEV - 1)), -1)
        slot_ref[rows, :] = slots
        slots_refs[k][...] = slots

    def terms_of(b, k):
        rows = pl.ds(pl.multiple_of(b * 8, 8), 8)
        *velocity, weight = decode(lat_ref, dir_ref[rows, :])
        offsets = [rb_ref[i, rows, :] for i in range(3)]
        arms = (*velocity, *cross(offsets, velocity))
        live = slots_refs[k][...] >= 0
        scale = jnp.where(live, 6.0 * weight, 0.0)
        source = jnp.where(live, 2.0 * pop_ref[rows, :] + weight * press_refs[k][...], 0.0)
        for i, arm in enumerate(arms):
            gain = scale * arm
            gain_ref[i, rows, :] = gain
            source = source - gain * at_refs[k][pl.ds(i, 8, stride=8), :]
        for i, arm in enumerate(arms):
            term_refs[k][pl.ds(i, 8, stride=8), :] = arm * source

    def summed(k, total):
        for pair in range(4):
            near, colloid = pair_of(slots_refs[k], 0, pair)
            terms = [term_refs[k][16 * pair + 8 * h:16 * pair + 8 * h + 8, :] for h in (0, 1)]
            terms = jnp.concatenate(terms, axis=1)
            high = terms.astype(jnp.bfloat16).astype(jnp.float32)
            both = jnp.concatenate([high, terms - high], axis=0)
            spread = jnp.concatenate([jnp.where(near == t, both, 0.0) for t in range(9)], axis=0).astype(jnp.bfloat16)
            total = total + lax.dot_general(
                spread, colloid.astype(jnp.bfloat16), (((1,), (1,)), ((), ())), preferred_element_type=jnp.float32
            )
        return total

    for k in range(RING):
        fetch(k, k).start()

    def ring(i, _):
        first = i * RING
        for k in range(RING):
            fetch(first + k, k).wait()
        for k in range(RING):
            gather(first + k, k)

        @pl.when(i < CHUNKS // RING - 1)
        def _():
            for k in range(RING):
                fetch(first + RING + k, k).start()
        for k in range(RING):
            place(first + k, k)
        for k in range(RING):
            found_at(table, slots_refs[k], 0, at_refs[k])
        for k in range(RING):
            terms_of(first + k, k)
        total = jnp.zeros((144, NC_DEV), jnp.float32)
        for k in range(RING):
            total = summed(k, total)
        sums_ref[:, 0:NC_DEV] += total
        return 0

    lax.fori_loop(0, CHUNKS // RING, ring, 0)

    row = lax.broadcasted_iota(jnp.int32, (8, 128), 0)
    for t in range(9):
        part_ref[t] = sums_ref[16 * t:16 * t + 8, :] + sums_ref[16 * t + 8:16 * t + 16, :]
    greeted()
    for t, _ in beside():
        mail.send(t, part_ref.at[t], got_ref.at[8 - t])
    total = part_ref[4]
    mail.wait()
    for t in range(9):
        if t != 4:
            total = total + got_ref[t]
    mass = 4.0 / 3.0 * math.pi * RADIUS**3
    inertia = 0.4 * mass * RADIUS**2
    new_ref[...] = table_ref[32:40, :] + jnp.where(row < 3, total / mass, total / inertia)
    for t, _ in beside():
        mail.send(t, new_ref, back_ref.at[8 - t])
    report_ref[...] = jnp.where(row < 3, total, total / RADIUS)
    mail.wait()
    moved = block_table(lambda t: new_ref[...] if t == 4 else back_ref[t])

    def group(i, _):
        for k in range(FINAL):
            found_at(moved, slot_ref, pl.multiple_of((i * FINAL + k) * 8, 8), at_refs[k])
        for k in range(FINAL):
            rows = pl.ds(pl.multiple_of((i * FINAL + k) * 8, 8), 8)
            value = pop_ref[rows, :]
            for j in range(6):
                value = value - gain_ref[j, rows, :] * at_refs[k][pl.ds(j, 8, stride=8), :]
            out_ref[rows, :] = value
        return 0

    lax.fori_loop(0, CHUNKS // FINAL, group, 0)


VM = pl.BlockSpec(memory_space=pltpu.VMEM)


def links(row, site, direction, ids, pop, rb, q, table):
    small = pltpu.VMEM((9, 8, 128), jnp.float32)
    column = pltpu.VMEM((64, 128), jnp.float32)
    return pl.pallas_call(
        links_kernel,
        in_specs=[pl.BlockSpec(memory_space=pl.ANY)] + [VM] * 8,
        out_specs=(VM, VM),
        out_shape=(jax.ShapeDtypeStruct((8, 128), jnp.float32), jax.ShapeDtypeStruct((LINKS // 128, 128), jnp.float32)),
        scratch_shapes=[
            pltpu.VMEM((LINKS // 128, 128), jnp.int32), [pltpu.VMEM((8, 128), jnp.int32)] * RING, pltpu.VMEM((6, LINKS // 128, 128), jnp.float32),
            pltpu.VMEM((144, 128), jnp.float32), [column] * max(RING, FINAL), [column] * RING,
            [pltpu.VMEM((8, 128), jnp.float32)] * RING, [pltpu.SMEM((CHUNK,), jnp.int32)] * RING,
            small, small, pltpu.VMEM((8, 128), jnp.float32), small,
            pltpu.SemaphoreType.DMA((RING,)), pltpu.SemaphoreType.DMA((16,)), pltpu.SemaphoreType.DMA((16,)),
        ],
        name="links",
        compiler_params=pltpu.CompilerParams(vmem_limit_bytes=40 * 2**20, collective_id=1, has_side_effects=True),
    )(row, site, direction, ids, pop, rb, q, table, lattice_table())


def shards(
    eps_field, charge, potential_start, colloid_vel, colloid_spin, link_dir, link_colloid, link_site, link_depth,
    link_pop, link_rb,
):
    flat = lambda a: a.reshape(LINKS // 128, 128)
    potential, q, table = relax(eps_field, charge, potential_start, colloid_vel, colloid_spin)
    row = link_depth.reshape(-1) * TX + (link_site.reshape(-1) >> 7)
    rb = link_rb.reshape(3, LINKS // 128, 128)
    report, link_out = links(
        row, flat(link_site), flat(link_dir), flat(link_colloid), flat(link_pop), rb, q.reshape(NZ * TX, TY), table
    )
    link_out = link_out.reshape(link_pop.shape)
    return potential, report[0:6, 0:NC_DEV], link_out


def solution(mesh):
    tile = P(None, "gx", "gy")
    owned = P(None, ("gx", "gy"))
    link = P("gx", "gy", None)
    return jax.shard_map(
        shards,
        mesh=mesh,
        in_specs=(tile, tile, tile, owned, owned, link, link, link, link, link, P(None, "gx", "gy", None)),
        out_specs=(tile, owned, link),
        check_vma=False,
    )
```
